256 devices in a mesh: cache: 16 (over x, y), heads: 16 (over z, core).
Axes of the slice: x: 4, y: 4, z: 8, core: 2. Of those that a mesh axis runs over, the one named last changes fastest.
Arguments:
- hidden: bfloat16 [3072, 8192], P('cache'), may hold values from -6 to 6
- norm_gain: bfloat16 [8192], replicated, may hold values from 0.099609375 to 1.8984375
- q_weight: bfloat16 [8192, 8192], P('cache', 'heads'), may hold values from -0.0625 to 0.0625
- q_bias: bfloat16 [8192], P('heads'), may hold values from -4 to 4
- kv_weight: bfloat16 [8192, 2048], P('cache'), may hold values from -0.0625 to 0.0625
- kv_bias: bfloat16 [2048], replicated, may hold values from -4 to 4
- out_weight: bfloat16 [8192, 8192], P('heads', 'cache'), may hold values from -0.0625 to 0.0625
- kv_store: bfloat16 [128, 16, 512, 256], P('cache', 'heads'), as said below
- stretch_place: int32 [128], replicated, may hold values from 0 to 127, as said below
- req_stretches: int32 [16, 8], replicated, may hold values from 0 to 127, as said below
- rec_rows: int32 [16, 8, 24], replicated, may hold values from 0 to 511, as said below
Outputs:
- attn_out: bfloat16 [3072, 8192], P('cache', 'heads')
- new_store: bfloat16 [128, 16, 512, 256], P('cache', 'heads')
The draws below stay inside these ranges and needn't reach their ends.
Inputs may be any that keep to these rules, and one draw needn't show every extreme that they name: `req_stretches`: each stretch stands in exactly one request; among the stretches of one request at most 2 have the same owner, and in every request some owner has exactly 2. `stretch_place`: A permutation of the slots; each owner holds 8 stretches. `rec_rows`: distinct and increasing within each stretch. `kv_store`: entries g and g2 of the second dimension are equal when g // 2 == g2 // 2.
All inputs are finite; a program needn't handle non-finite values.
Results may differ from the reference program's by a relative error of at most 0.023.
The reference program's roundings to bfloat16 on the way count: a program that leaves them out, or rounds other values in their place, can miss the bound.
Values may be sent and summed in bfloat16 or wider, within the bound.
A program may use at most 128 MiB of HBM per device.

```python
import math
import jax
import jax.numpy as jnp
from jax import lax

D = 8192
HD = 128
QHEADS = 64
KVHEADS = 8
CLEN = 512
R = 8
SEL = 24
QH_DEV = 4
ROWS = 3072
MOST = 2
N_CACHE = 16
N_HEADS = 16


def stretch_layout(key):
    owner_perm = jax.random.permutation(jax.random.fold_in(key, 11), N_CACHE)
    inverse = jnp.zeros((N_CACHE,), jnp.int32).at[owner_perm].set(jnp.arange(N_CACHE, dtype=jnp.int32))
    special = jnp.array([N_CACHE // 2, 1, N_CACHE - 1], jnp.int32)
    special_order = special[jax.random.permutation(jax.random.fold_in(key, 15), 3)]
    values = jnp.arange(N_CACHE, dtype=jnp.int32)
    ranking = 3 + inverse
    ranking = jnp.where(values == special_order[2], 2, ranking)
    ranking = jnp.where(values == special_order[1], 1, ranking)
    ranking = jnp.where(values == special_order[0], 0, ranking)
    shift_list = jnp.argsort(ranking).astype(jnp.int32)
    order = jax.random.permutation(jax.random.fold_in(key, 12), R)
    shifts = shift_list[order // MOST]
    owners = (jnp.arange(N_CACHE)[:, None] + shifts[None, :]) % N_CACHE
    slot_perm = jax.random.permutation(jax.random.fold_in(key, 13), R)
    places = owners * R + slot_perm[None, :]
    stretch_ids = jax.random.permutation(jax.random.fold_in(key, 14), N_CACHE * R).reshape(N_CACHE, R)
    return (stretch_ids.astype(jnp.int32), places.astype(jnp.int32))


def draw_req_stretches(key, part):
    stretch_ids, places = stretch_layout(key)
    return stretch_ids


def draw_stretch_place(key, part):
    stretch_ids, places = stretch_layout(key)
    table = jnp.zeros((N_CACHE * R,), jnp.int32)
    return table.at[stretch_ids.reshape(-1)].set(places.reshape(-1))


def draw_rec_rows(key, part):
    key = jax.random.fold_in(key, 21)
    keys_all = jax.random.split(key, N_CACHE * R)
    picks = jax.vmap(lambda single: jnp.sort(jax.random.permutation(single, CLEN)[:SEL]))(keys_all)
    return picks.reshape(N_CACHE, R, SEL).astype(jnp.int32)


def draw_kv_store(key, part):
    key = jax.random.fold_in(key, 31)
    shape = (N_CACHE * R, KVHEADS, CLEN, 2 * HD)
    base = jax.random.normal(key, shape, jnp.float32)
    base = jnp.repeat(base, N_HEADS // KVHEADS, axis=1)
    return base.astype(jnp.bfloat16)


def levels(own_key, extent, shards, least, largest):
    def one(dim, parts):
        heights = jax.random.uniform(jax.random.fold_in(jax.random.fold_in(own_key, 6), dim), (parts,), jnp.float32, least / len(shards), largest / len(shards))
        return jnp.repeat(jnp.exp(heights), extent[dim] // parts).reshape((-1,) + (1,) * (len(extent) - dim - 1))

    factor_of = one(*shards[0])
    for cut in shards[1:]:
        factor_of = factor_of * one(*cut)
    return factor_of


def centred(rng, extent, deviation, limit, cuts=(), held_as=jnp.bfloat16):
    level = levels(rng, extent, cuts, -0.22, 0.18) if cuts else 1.0
    entries = jax.random.normal(rng, extent, jnp.float32) * deviation * level
    return jnp.minimum(jnp.maximum(entries, -limit), limit).astype(held_as)


def setup_inputs(seed: int = 0) -> dict:
    arg_keys = jax.random.split(jax.random.key(seed), 12)
    return {
        "hidden": centred(arg_keys[0], (ROWS, D), 1.0, 6.0, ((0, 16),)),
        "norm_gain": jnp.clip(1.0 + 0.18 * jax.random.normal(arg_keys[1], (D,), jnp.float32), 0.099609375, 1.8984375).astype(jnp.bfloat16),
        "q_weight": centred(arg_keys[2], (D, QHEADS * HD), D ** -0.5, 0.0625, ((0, 16), (1, 16))),
        "q_bias": centred(arg_keys[3], (QHEADS * HD,), 1.0, 4.0, ((0, 16),)),
        "kv_weight": centred(arg_keys[4], (D, KVHEADS * 2 * HD), D ** -0.5, 0.0625, ((0, 16),)),
        "kv_bias": centred(arg_keys[5], (KVHEADS * 2 * HD,), 1.0, 4.0),
        "out_weight": centred(arg_keys[6], (QHEADS * HD, D), (QHEADS * HD) ** -0.5, 0.0625, ((0, 16), (1, 16))),
        "kv_store": draw_kv_store(jax.random.fold_in(arg_keys[11], 71), 0),
        "stretch_place": draw_stretch_place(jax.random.fold_in(arg_keys[11], 71), 0),
        "req_stretches": draw_req_stretches(jax.random.fold_in(arg_keys[11], 71), 0),
        "rec_rows": draw_rec_rows(jax.random.fold_in(arg_keys[11], 71), 0),
    }


def rms_norm(hidden, norm_gain):
    values = hidden.astype(jnp.float32)
    factor = lax.rsqrt(lax.optimization_barrier(jnp.mean(values * values, axis=-1, keepdims=True)) + 1e-06)
    return (values * factor * norm_gain.astype(jnp.float32)).astype(jnp.bfloat16)

def reference(hidden, norm_gain, q_weight, q_bias, kv_weight, kv_bias, out_weight, kv_store, stretch_place, req_stretches, rec_rows):
    query_width = QH_DEV * HD
    copies = N_HEADS // KVHEADS
    normed = rms_norm(hidden, norm_gain)
    q_mixed = jnp.dot(normed, q_weight, preferred_element_type=jnp.float32) + q_bias.astype(jnp.float32)
    kv_mixed = jnp.dot(normed, kv_weight, preferred_element_type=jnp.float32) + kv_bias.astype(jnp.float32)
    queries = q_mixed.astype(jnp.bfloat16).reshape(N_CACHE, R, SEL, N_HEADS * query_width)
    fresh = kv_mixed.astype(jnp.bfloat16).reshape(N_CACHE, R, SEL, KVHEADS, 2 * HD)
    fresh = jnp.repeat(fresh, copies, axis=3)
    places = stretch_place[req_stretches].astype(jnp.int32)
    out_heads = out_weight.reshape(N_HEADS, query_width, D).astype(jnp.float32)

    def one_request(inputs):
        query_rows, fresh_rows, place_list, row_list = inputs
        blocks = kv_store[place_list]
        blocks = blocks.at[jnp.arange(R)[:, None], :, row_list, :].set(fresh_rows)
        keyvals = jnp.transpose(blocks, (1, 0, 2, 3)).reshape(N_HEADS, R * CLEN, 2 * HD).astype(jnp.float32)
        query_f = query_rows.reshape(R * SEL, N_HEADS, QH_DEV, HD).astype(jnp.float32)
        scores = jnp.einsum('qgjd,gkd->gjqk', query_f, keyvals[..., :HD]) / math.sqrt(HD)
        query_pos = (jnp.arange(R)[:, None] * CLEN + row_list).reshape(R * SEL)
        key_pos = jnp.arange(R * CLEN)
        allowed = key_pos[None, :] <= query_pos[:, None]
        scores = jnp.where(allowed, scores, -jnp.inf)
        highest = lax.optimization_barrier(jnp.max(scores, axis=-1, keepdims=True))
        expon = jnp.exp(scores - highest)
        weights = (expon / lax.optimization_barrier(jnp.sum(expon, axis=-1, keepdims=True))).astype(jnp.bfloat16)
        context = jnp.einsum('gjqk,gkd->qgjd', weights.astype(jnp.float32), keyvals[..., HD:]).astype(jnp.bfloat16)
        context = context.reshape(R * SEL, N_HEADS, query_width).astype(jnp.float32)
        partial_terms = jnp.einsum('qgd,gde->qge', context, out_heads)
        partial_terms = lax.optimization_barrier(partial_terms.astype(jnp.bfloat16)).astype(jnp.float32)
        return lax.optimization_barrier(jnp.sum(partial_terms, axis=1)).astype(jnp.bfloat16)
    outputs = lax.map(one_request, (queries, fresh, places, rec_rows))
    attn_out = outputs.reshape(N_CACHE * R * SEL, D)
    new_store = kv_store.at[places[:, :, None], :, rec_rows, :].set(fresh)
    return (attn_out, new_store)
```

```python
import functools
import math

import jax
import jax.numpy as jnp
from jax import lax
from jax.experimental import pallas as pl
from jax.experimental.pallas import tpu as pltpu
from jax.sharding import PartitionSpec as P

MESH = pl.DeviceIdType.MESH
SIDE = 4
BF16 = jnp.bfloat16
F32 = jnp.float32
PAD = 32


def remote(src, dst, send_sem, recv_sem, device):
    return pltpu.make_async_remote_copy(
        src_ref=src, dst_ref=dst, send_sem=send_sem, recv_sem=recv_sem, device_id=device, device_id_type=MESH
    )


def gather_project(
    place_ref, hid_hbm, gain_ref, qw_hbm, kvw_hbm, qb_ref, kvb_ref, store_hbm,
    q_ref, fresh_ref, blocks_hbm,
    hid, nrm, w, acc, hop_in, hop_out, qs, fpad,
    loc, w_send, w_recv, h1_send, h1_recv, h2_send, h2_recv, x_send, x_recv,
):
    me = lax.axis_index("cache")
    head = lax.axis_index("heads")
    core = lax.rem(head, 2)
    partner = (me, head + 1 - 2 * core)
    x, y = me // SIDE, lax.rem(me, SIDE)
    owners = SIDE * SIDE
    rows = hid.shape[0]
    depth, width = w.shape[1], w.shape[2]
    unit, half = depth // 4, depth // 2
    q_cols = qw_hbm.shape[1]
    hd = width - q_cols

    def at(dx, dy):
        return lax.rem(x + dx, SIDE) * SIDE + lax.rem(y + dy, SIDE)

    own_q = pltpu.make_async_copy(qw_hbm, w.at[me, :, 0:q_cols], loc.at[0])
    own_kv = pltpu.make_async_copy(
        kvw_hbm.at[:, pl.ds(pl.multiple_of(head * hd, hd), hd)], w.at[me, :, q_cols:width], loc.at[1]
    )
    own_hid = pltpu.make_async_copy(hid_hbm, hid, loc.at[2])
    own_hop = pltpu.make_async_copy(store_hbm.at[:, me, core], hop_in.at[pl.ds(me * 8, 8)], loc.at[3])
    own_q.start()
    own_kv.start()
    own_hop.start()
    own_hid.start()

    barrier = pltpu.get_barrier_semaphore()

    @pl.loop(1, owners)
    def _(o):
        pl.semaphore_signal(barrier, inc=1, device_id=(lax.rem(me + o, owners), head), device_id_type=MESH)

    pl.semaphore_signal(barrier, inc=1, device_id=partner, device_id_type=MESH)
    pl.semaphore_wait(barrier, owners)

    def hop1(o):
        to = lax.rem(me + o, owners)
        return remote(
            store_hbm.at[:, to, core], hop_in.at[pl.ds(me * 8, 8)], h1_send.at[o], h1_recv.at[me], (to, head)
        )

    def hop1_from(o):
        src = lax.rem(me + owners - o, owners)
        return remote(
            store_hbm.at[:, src, core], hop_in.at[pl.ds(src * 8, 8)], h1_send.at[o], h1_recv.at[src], (src, head)
        )

    def hop2(o):
        to = lax.rem(me + o, owners)
        return remote(hop_out.at[to], blocks_hbm.at[:, me, core], h2_send.at[o], h2_recv.at[me], (to, head))

    def hop2_from(o):
        src = lax.rem(me + owners - o, owners)
        return remote(hop_out.at[src], blocks_hbm.at[:, src, core], h2_send.at[o], h2_recv.at[src], (src, head))

    @pl.loop(1, owners)
    def _(o):
        hop1(o).start()

    own_q.wait()
    own_kv.wait()

    sends = []

    def piece(c, u):
        return w.at[c, pl.ds(u * unit, unit)]

    def send(c, u, dx, dy):
        copy = remote(piece(c, u), piece(c, u), w_send.at[len(sends)], w_recv.at[c, u], (at(dx, dy), head))
        copy.start()
        sends.append(copy)

    def arrived(c, u):
        remote(piece(c, u), piece(c, u), w_send.at[0], w_recv.at[c, u], (at(1, 0), head)).wait_recv()

    L, O, R = SIDE - 1, 2, 1

    def first(axis, d):
        return at(d, 0) if axis == 0 else at(0, d)

    def go(c, u, axis, d):
        send(c, u, d if axis == 0 else 0, d if axis == 1 else 0)

    for u in (0, 1):
        for axis in (0, 1):
            for d in (R, L):
                go(me, 2 * axis + u, axis, d)

    own_hid.wait()
    tall = 16

    @pl.loop(0, rows // tall)
    def _(i):
        lines = pl.ds(pl.multiple_of(i * tall, tall), tall)
        total = jnp.zeros((tall, 1), F32)
        for c in range(owners):
            v = hid[lines, c * depth : (c + 1) * depth].astype(F32)
            total += jnp.sum(v * v, axis=-1, keepdims=True)
        factor = lax.rsqrt(total / (owners * depth) + 1e-06)
        for c in range(owners):
            v = hid[lines, c * depth : (c + 1) * depth].astype(F32)
            g = gain_ref[:, c * depth : (c + 1) * depth].astype(F32)
            nrm[c, lines, :] = (v * factor * g).astype(BF16)

    acc[...] = jnp.zeros_like(acc)

    def multiply(c, axis):
        lo = axis * half
        acc[...] += jnp.dot(nrm[c, :, lo : lo + half], w[c, lo : lo + half, :], preferred_element_type=F32)

    for axis in (0, 1):
        arrived(first(axis, L), 2 * axis)
        go(first(axis, L), 2 * axis, axis, R)
        arrived(first(axis, R), 2 * axis + 1)
        go(first(axis, R), 2 * axis + 1, axis, L)
    for axis in (0, 1):
        for u in (0, 1):
            for d in (R, L):
                go(me, 2 * axis + u, 1 - axis, d)

    own_hop.wait()

    @pl.loop(1, owners)
    def _(o):
        hop1_from(o).wait_recv()

    @pl.loop(0, owners)
    def _(i):
        for r in range(8):
            hop_out[i, r] = hop_in[place_ref[i * 8 + r]]

    @pl.loop(1, owners)
    def _(o):
        hop2(o).start()

    own_out = pltpu.make_async_copy(hop_out.at[me], blocks_hbm.at[:, me, core], loc.at[4])
    own_out.start()

    for axis in (0, 1):
        arrived(first(axis, L), 2 * axis + 1)
        arrived(first(axis, R), 2 * axis)
        for s in (L, R):
            for u in (0, 1):
                for d in (R, L):
                    go(first(axis, s), 2 * axis + u, 1 - axis, d)
    for axis in (0, 1):
        arrived(first(axis, O), 2 * axis)
        arrived(first(axis, O), 2 * axis + 1)
        for u in (0, 1):
            for d in (R, L):
                go(first(axis, O), 2 * axis + u, 1 - axis, d)

    @pl.loop(0, SIDE)
    def _(i):
        multiply(at(i, 0), 0)
        multiply(at(0, i), 1)

    def second(axis, s, d):
        return at(s, d) if axis == 0 else at(d, s)

    def core_swap(which):
        return remote(
            blocks_hbm.at[:, :, which], blocks_hbm.at[:, :, which], x_send.at[0], x_recv.at[0], partner
        )

    for n, s in enumerate((0, L, R, O)):
        for axis in (0, 1):
            arrived(second(axis, s, L), 2 * axis)
            go(second(axis, s, L), 2 * axis, 1 - axis, R)
            arrived(second(axis, s, R), 2 * axis + 1)
            go(second(axis, s, R), 2 * axis + 1, 1 - axis, L)
        for axis in (0, 1):
            arrived(second(axis, s, L), 2 * axis + 1)
            arrived(second(axis, s, R), 2 * axis)
            arrived(second(axis, s, O), 2 * axis)
            arrived(second(axis, s, O), 2 * axis + 1)

        @pl.loop(1, SIDE)
        def _(i):
            multiply(second(0, s, i), 0)
            multiply(second(1, s, i), 1)

        if n == 2:
            own_out.wait()

            @pl.loop(1, owners)
            def _(o):
                hop2_from(o).wait_recv()

            core_swap(core).start()

    per = rows // 8
    heads = q_cols // hd
    bias = qb_ref[...].astype(F32)
    kv_bias = kvb_ref[:, pl.ds(pl.multiple_of(head * hd, hd), hd)].astype(F32)
    for r in range(8):
        lines = slice(per * r, per * (r + 1))
        for j in range(heads):
            at_row = (r * heads + j) * per
            qs[at_row : at_row + per, :] = acc[lines, j * hd : (j + 1) * hd] + bias[:, j * hd : (j + 1) * hd]
        fpad[r * PAD : r * PAD + per, :] = acc[lines, q_cols:width] + kv_bias
        fpad[r * PAD + per : (r + 1) * PAD, :] = jnp.zeros((PAD - per, hd), F32)
    fresh_ref[core] = fpad[...].astype(BF16)
    swap = remote(fresh_ref.at[core], fresh_ref.at[core], x_send.at[1], x_recv.at[1], partner)
    swap.start()
    q_ref[...] = qs[...].astype(BF16)

    core_swap(1 - core).wait_recv()
    remote(fresh_ref.at[1 - core], fresh_ref.at[1 - core], x_send.at[1], x_recv.at[1], partner).wait_recv()
    swap.wait_send()
    core_swap(core).wait_send()
    for copy in sends:
        copy.wait_send()

    @pl.loop(1, owners)
    def _(o):
        hop1(o).wait_send()
        hop2(o).wait_send()


def attend(q_ref, fresh_ref, blocks_ref, row_ref, pos_ref, ctx_ref, ks, vs, sc, top, low, out, flat):
    stretches, length = blocks_ref.shape[0], blocks_ref.shape[1]
    hd = q_ref.shape[1]
    total = q_ref.shape[0]
    group = total // stretches
    heads = ctx_ref.shape[1] // hd
    per = group // heads
    scale = math.log2(math.e) / math.sqrt(hd)
    ones = jnp.ones((PAD, hd), BF16)
    for r in range(stretches):
        hit = lax.broadcasted_iota(jnp.int32, (length, PAD), 0) == row_ref[r : r + 1, :]
        lines = slice(r * PAD, (r + 1) * PAD)
        table = jnp.concatenate([fresh_ref[0, lines, :], fresh_ref[1, lines, :], ones], axis=1)
        new = jnp.dot(hit.astype(F32).astype(BF16), table, preferred_element_type=F32)
        there = new[:, 2 * hd :] > 0.5
        ks[r] = jnp.where(there, new[:, :hd], blocks_ref[r, :, :hd].astype(F32)).astype(BF16)
        vs[r] = jnp.where(there, new[:, hd : 2 * hd], blocks_ref[r, :, hd:].astype(F32)).astype(BF16)
    top[...] = jnp.full_like(top, -jnp.inf)
    low[...] = jnp.zeros_like(low)
    out[...] = jnp.zeros_like(out)

    def fold(a, op):
        parts = [a[:, i * hd : (i + 1) * hd] for i in range(length // hd)]
        while len(parts) > 1:
            parts = [op(parts[i], parts[i + 1]) for i in range(0, len(parts), 2)]
        return parts[0]

    for s in range(stretches):
        scores = lax.dot_general(
            q_ref[s * group :, :], ks[s], (((1,), (1,)), ((), ())), preferred_element_type=F32
        )
        key = lax.broadcasted_iota(jnp.int32, (group, length), 1)
        first = jnp.where(key <= pos_ref[s * group : (s + 1) * group, :], scores[:group], -jnp.inf)
        sc[s, s * group : (s + 1) * group, :] = first
        top[s * group : (s + 1) * group, :] = jnp.maximum(
            top[s * group : (s + 1) * group, :], fold(first, jnp.maximum)
        )
        if s + 1 < stretches:
            sc[s, (s + 1) * group :, :] = scores[group:]
            top[(s + 1) * group :, :] = jnp.maximum(top[(s + 1) * group :, :], fold(scores[group:], jnp.maximum))
    top[...] = jnp.broadcast_to(jnp.max(top[...], axis=1, keepdims=True), top.shape)
    for s in range(stretches):
        here = slice(s * group, total)
        peak = top[here, :]
        expon = jnp.concatenate(
            [jnp.exp2((sc[s, here, i * hd : (i + 1) * hd] - peak) * scale) for i in range(length // hd)], axis=1
        )
        low[here, :] += fold(expon, jnp.add)
        out[here, :] += jnp.dot(expon.astype(BF16), vs[s], preferred_element_type=F32)
    out[...] = out[...] / jnp.sum(low[...], axis=1, keepdims=True)
    for r in range(stretches):
        for j in range(heads):
            at_row = (r * heads + j) * per
            flat[r * per : (r + 1) * per, j * hd : (j + 1) * hd] = out[at_row : at_row + per, :]
    ctx_ref[...] = flat[...].astype(BF16)


def project_out(
    slot_ref, pick_ref, ctx_ref, w_hbm, fresh_ref,
    out_ref, back_ref,
    w, pair_out, pair_in, own, r_out, l_out, r_in, l_in, f_out, f_in,
    w_sem, p_send, p_recv, r_send, r_recv, l_send, l_recv, f_send, f_recv, b_send, b_recv,
):
    me = lax.axis_index("cache")
    head = lax.axis_index("heads")
    owners = lax.axis_size("cache")
    ring = lax.axis_size("heads") // 2
    core = lax.rem(head, 2)
    z = head // 2
    partner = (me, head + 1 - 2 * core)
    right = (me, lax.rem(z + 1, ring) * 2 + core)
    left = (me, lax.rem(z + ring - 1, ring) * 2 + core)
    rows = ctx_ref.shape[0]
    hrow = rows // 2
    order = (4, 3, -3, 2, -2, 1, -1, 0)

    def column(n, parity):
        return lax.rem(z + order[n] + ring, ring) * 2 + parity

    def fetch(n, which):
        block = column(n, 1 - core if which == 0 else core)
        return pltpu.make_async_copy(w_hbm.at[block], w.at[2 * n + which], w_sem.at[2 * n + which])

    for n in range(len(order)):
        for which in (0, 1):
            fetch(n, which).start()

    barrier = pltpu.get_barrier_semaphore()

    @pl.loop(1, owners)
    def _(o):
        pl.semaphore_signal(barrier, inc=1, device_id=(lax.rem(me + o, owners), head), device_id_type=MESH)

    for peer in (partner, left, right):
        pl.semaphore_signal(barrier, inc=1, device_id=peer, device_id_type=MESH)
    pl.semaphore_wait(barrier, owners + 2)

    @pl.loop(0, owners)
    def _(o):
        for m in range(2):
            f_out[2 * o + m] = fresh_ref[core, slot_ref[2 * o + m]]

    def give(o):
        to = lax.rem(me + o, owners)
        return remote(
            f_out.at[pl.ds(2 * to, 2)], f_in.at[pl.ds(2 * me, 2)], f_send.at[o], f_recv.at[me], (to, head)
        )

    def take(o):
        src = lax.rem(me + owners - o, owners)
        return remote(
            f_out.at[pl.ds(2 * src, 2)], f_in.at[pl.ds(2 * src, 2)], f_send.at[o], f_recv.at[src], (src, head)
        )

    @pl.loop(1, owners)
    def _(o):
        give(o).start()

    for m in range(2):
        f_in[2 * me + m] = f_out[2 * me + m]

    def pair(n):
        return remote(pair_out.at[n], pair_in.at[n], p_send.at[n], p_recv.at[n], partner)

    for n in range(len(order)):
        fetch(n, 0).wait()
        pair_out[n] = jnp.dot(ctx_ref[...], w[2 * n], preferred_element_type=F32).astype(BF16)
        pair(n).start()
        fetch(n, 1).wait()
        own[n] = jnp.dot(ctx_ref[...], w[2 * n + 1], preferred_element_type=F32).astype(BF16)

    def lines(part):
        return slice(part * hrow, (part + 1) * hrow)

    def total(n, part):
        return own[n, lines(part), :].astype(F32) + pair_in[n, lines(part), :].astype(F32)

    def ring_copy(step, part, out, into, send_sem, recv_sem, to):
        return remote(
            out.at[step, pl.ds(part * hrow, hrow)],
            into.at[step, pl.ds(part * hrow, hrow)],
            send_sem.at[step, part],
            recv_sem.at[step, part],
            to,
        )

    def rightward(step, part):
        return ring_copy(step, part, r_out, r_in, r_send, r_recv, right)

    def leftward(step, part):
        return ring_copy(step, part, l_out, l_in, l_send, l_recv, left)

    pair(0).wait_recv()
    r_out[0, lines(0), :] = total(0, 0).astype(BF16)
    rightward(0, 0).start()
    l_out[0, lines(1), :] = total(0, 1).astype(BF16)
    leftward(0, 1).start()
    for step in (1, 2, 3):
        n_right, n_left = 2 * step - 1, 2 * step
        pair(n_right).wait_recv()
        pair(n_left).wait_recv()
        parts = ((1, 0), (0, 1)) if step == 1 else ((0, 1), (1, 0))
        for right_part, left_part in zip(*parts):
            value = total(n_right, right_part)
            if step > 1 or right_part == 0:
                rightward(step - 1, right_part).wait_recv()
                value += r_in[step - 1, lines(right_part), :].astype(F32)
            r_out[step, lines(right_part), :] = value.astype(BF16)
            rightward(step, right_part).start()
            value = total(n_left, left_part)
            if step > 1 or left_part == 1:
                leftward(step - 1, left_part).wait_recv()
                value += l_in[step - 1, lines(left_part), :].astype(F32)
            l_out[step, lines(left_part), :] = value.astype(BF16)
            leftward(step, left_part).start()

    @pl.loop(1, owners)
    def _(o):
        take(o).wait_recv()

    for s in range(back_ref.shape[1]):
        back_ref[core, s] = f_in[pick_ref[s]]
    swap = remote(back_ref.at[core], back_ref.at[core], b_send.at[0], b_recv.at[0], partner)
    swap.start()

    pair(7).wait_recv()
    for part in (0, 1):
        rightward(3, part).wait_recv()
        leftward(3, part).wait_recv()
        value = total(7, part) + r_in[3, lines(part), :].astype(F32) + l_in[3, lines(part), :].astype(F32)
        out_ref[lines(part), :] = value.astype(BF16)

    remote(back_ref.at[1 - core], back_ref.at[1 - core], b_send.at[0], b_recv.at[0], partner).wait_recv()
    swap.wait_send()
    for n in range(len(order)):
        pair(n).wait_send()
    rightward(0, 0).wait_send()
    leftward(0, 1).wait_send()
    for step in (1, 2, 3):
        for part in (0, 1):
            rightward(step, part).wait_send()
            leftward(step, part).wait_send()

    @pl.loop(1, owners)
    def _(o):
        give(o).wait_send()


def write_back(store_ref, back_ref, row_ref, new_ref):
    length, hd = store_ref.shape[2], back_ref.shape[3]
    hit = lax.broadcasted_iota(jnp.int32, (length, PAD), 0) == row_ref[0]
    table = jnp.concatenate([back_ref[0, 0], back_ref[1, 0], jnp.ones((PAD, hd), BF16)], axis=1)
    new = jnp.dot(hit.astype(F32).astype(BF16), table, preferred_element_type=F32)
    there = new[:, 2 * hd :] > 0.5
    for part in (0, 1):
        lanes = slice(part * hd, (part + 1) * hd)
        new_ref[0, 0, :, lanes] = jnp.where(there, new[:, lanes], store_ref[0, 0, :, lanes].astype(F32)).astype(BF16)


def whole(shape=None):
    return pl.BlockSpec(memory_space=pltpu.VMEM)


def shards(
    hidden, norm_gain, q_weight, q_bias, kv_weight, kv_bias, out_weight, kv_store, stretch_place, req_stretches, rec_rows
):
    owners = lax.axis_size("cache")
    me = lax.axis_index("cache")
    rows, width = hidden.shape
    stretches, _, length, kv_width = kv_store.shape
    hd = kv_width // 2
    per = rec_rows.shape[2]
    depth, q_cols = q_weight.shape
    heads = q_cols // hd
    vmem = pl.BlockSpec(memory_space=pltpu.VMEM)
    smem = pl.BlockSpec(memory_space=pltpu.SMEM)
    hbm = pl.BlockSpec(memory_space=pl.ANY)
    dma = pltpu.SemaphoreType.DMA

    out_blocks = lax.all_gather(out_weight, "cache", axis=0, tiled=False)

    places = stretch_place[req_stretches]
    owner_of = places // stretches
    earlier = jnp.arange(stretches)[None, :] < jnp.arange(stretches)[:, None]
    rank_of = jnp.sum((owner_of[:, :, None] == owner_of[:, None, :]) & earlier[None], axis=2).astype(jnp.int32)
    pair_of = owner_of * 2 + rank_of
    my_pair = lax.dynamic_index_in_dim(pair_of, me, 0, keepdims=False)
    order = jnp.arange(stretches, dtype=jnp.int32)
    slot_r = jnp.sum((my_pair[None, :] == jnp.arange(2 * owners)[:, None]) * order[None, :], axis=1).astype(jnp.int32)
    flat_places = places.reshape(-1)
    mine = flat_places[None, :] == (me * stretches + order)[:, None]
    source = jnp.arange(owners)[:, None] * 2 + rank_of
    pick = jnp.sum(mine * source.reshape(1, -1), axis=1).astype(jnp.int32)
    slot_rows = jnp.sum(mine[:, :, None] * rec_rows.reshape(1, -1, per), axis=1).astype(jnp.int32)
    slot_rows = jnp.pad(slot_rows, ((0, 0), (0, PAD - per)), constant_values=-1)
    my_rows = lax.dynamic_index_in_dim(rec_rows, me, 0, keepdims=False)
    pad_rows = jnp.pad(my_rows, ((0, 0), (0, PAD - per)), constant_values=-1)
    row_pos = jnp.broadcast_to(my_rows[:, None, :], (stretches, heads, per)).reshape(rows * heads, 1)

    store = kv_store.reshape(stretches, owners, 2, length // (2 * owners), kv_width)
    piece = length // (2 * owners)

    queries, fresh, blocks = pl.pallas_call(
        gather_project,
        out_shape=(
            jax.ShapeDtypeStruct((rows * heads, hd), BF16),
            jax.ShapeDtypeStruct((2, stretches * PAD, hd), BF16),
            jax.ShapeDtypeStruct((stretches, owners, 2, piece, kv_width), BF16),
        ),
        in_specs=[smem, hbm, vmem, hbm, hbm, vmem, vmem, hbm],
        out_specs=(vmem, vmem, hbm),
        scratch_shapes=[
            pltpu.VMEM((rows, width), BF16),
            pltpu.VMEM((owners, rows, depth), BF16),
            pltpu.VMEM((owners, depth, q_cols + hd), BF16),
            pltpu.VMEM((rows, q_cols + hd), F32),
            pltpu.VMEM((owners * stretches, piece, kv_width), BF16),
            pltpu.VMEM((owners, stretches, piece, kv_width), BF16),
            pltpu.VMEM((rows * heads, hd), F32),
            pltpu.VMEM((stretches * PAD, hd), F32),
            dma((5,)),
            dma((60,)),
            dma((owners, 4)),
            dma((owners,)),
            dma((owners,)),
            dma((owners,)),
            dma((owners,)),
            dma((2,)),
            dma((2,)),
        ],
        compiler_params=pltpu.CompilerParams(collective_id=0, has_side_effects=True, vmem_limit_bytes=48 << 20),
        name="gather_project",
    )(
        flat_places, hidden, norm_gain.reshape(1, -1), q_weight, kv_weight,
        q_bias.reshape(1, -1), kv_bias.reshape(1, -1), store,
    )
    blocks = blocks.reshape(stretches, length, kv_width)

    context = pl.pallas_call(
        attend,
        out_shape=jax.ShapeDtypeStruct((rows, q_cols), BF16),
        in_specs=[vmem] * 5,
        out_specs=vmem,
        scratch_shapes=[
            pltpu.VMEM((stretches, length, hd), BF16),
            pltpu.VMEM((stretches, length, hd), BF16),
            pltpu.VMEM((stretches, rows * heads, length), F32),
            pltpu.VMEM((rows * heads, hd), F32),
            pltpu.VMEM((rows * heads, hd), F32),
            pltpu.VMEM((rows * heads, hd), F32),
            pltpu.VMEM((rows, q_cols), F32),
        ],
        compiler_params=pltpu.CompilerParams(vmem_limit_bytes=48 << 20),
        name="attend",
    )(queries, fresh, blocks, pad_rows, row_pos)

    ring = 8
    attn_out, back = pl.pallas_call(
        project_out,
        out_shape=(
            jax.ShapeDtypeStruct((rows, q_cols), BF16),
            jax.ShapeDtypeStruct((2, stretches, PAD, hd), BF16),
        ),
        in_specs=[smem, smem, vmem, hbm, vmem],
        out_specs=(vmem, vmem),
        scratch_shapes=[
            pltpu.VMEM((2 * ring, depth, q_cols), BF16),
            pltpu.VMEM((ring, rows, q_cols), BF16),
            pltpu.VMEM((ring, rows, q_cols), BF16),
            pltpu.VMEM((ring, rows, q_cols), BF16),
            pltpu.VMEM((4, rows, q_cols), BF16),
            pltpu.VMEM((4, rows, q_cols), BF16),
            pltpu.VMEM((4, rows, q_cols), BF16),
            pltpu.VMEM((4, rows, q_cols), BF16),
            pltpu.VMEM((2 * owners, PAD, hd), BF16),
            pltpu.VMEM((2 * owners, PAD, hd), BF16),
            dma((2 * ring,)),
            dma((ring,)),
            dma((ring,)),
            dma((4, 2)),
            dma((4, 2)),
            dma((4, 2)),
            dma((4, 2)),
            dma((owners,)),
            dma((owners,)),
            dma((1,)),
            dma((1,)),
        ],
        compiler_params=pltpu.CompilerParams(collective_id=1, has_side_effects=True, vmem_limit_bytes=48 << 20),
        name="project_out",
    )(slot_r, pick, context, out_blocks, fresh.reshape(2, stretches, PAD, hd))

    new_store = pl.pallas_call(
        write_back,
        grid=(stretches,),
        out_shape=jax.ShapeDtypeStruct(kv_store.shape, BF16),
        in_specs=[
            pl.BlockSpec((1, 1, length, kv_width), lambda s: (s, 0, 0, 0)),
            pl.BlockSpec((2, 1, PAD, hd), lambda s: (0, s, 0, 0)),
            pl.BlockSpec((1, 1, PAD), lambda s: (s, 0, 0)),
        ],
        out_specs=pl.BlockSpec((1, 1, length, kv_width), lambda s: (s, 0, 0, 0)),
        name="write_back",
    )(kv_store, back, slot_rows.reshape(stretches, 1, PAD))
    return (attn_out, new_store)


def solution(mesh):
    placed = (
        P("cache", None),
        P(),
        P("cache", "heads"),
        P("heads"),
        P("cache", None),
        P(),
        P("heads", "cache"),
        P("cache", "heads", None, None),
        P(),
        P(),
        P(),
    )
    return jax.shard_map(
        shards,
        mesh=mesh,
        in_specs=placed,
        out_specs=(P("cache", "heads"), P("cache", "heads", None, None)),
        check_vma=False,
    )
```

```python
import functools
import math

import jax
import jax.numpy as jnp
from jax import lax
from jax.experimental import pallas as pl
from jax.experimental.pallas import tpu as pltpu
from jax.sharding import PartitionSpec as P

MESH = pl.DeviceIdType.MESH
SIDE = 4
BF16 = jnp.bfloat16
F32 = jnp.float32
RIGHT, OPPOSITE, LEFT = 1, 2, 3
PAD = 32


def remote(src, dst, send_sem, recv_sem, device):
    return pltpu.make_async_remote_copy(
        src_ref=src, dst_ref=dst, send_sem=send_sem, recv_sem=recv_sem, device_id=device, device_id_type=MESH
    )


class Spread:
    def __init__(self, piece, send_sem, recv_sem, me, head):
        self.piece, self.send_sem, self.recv_sem, self.head = piece, send_sem, recv_sem, head
        self.me, self.x, self.y = me, me // SIDE, lax.rem(me, SIDE)
        self.sends = []

    def at(self, dx, dy):
        return lax.rem(self.x + dx, SIDE) * SIDE + lax.rem(self.y + dy, SIDE)

    def along(self, axis, d, s=0):
        return self.at(d, s) if axis == 0 else self.at(s, d)

    def go(self, c, u, axis, d):
        piece = self.piece(c, u)
        copy = remote(
            piece, piece, self.send_sem.at[len(self.sends)], self.recv_sem.at[c, u], (self.along(axis, d), self.head)
        )
        copy.start()
        self.sends.append(copy)

    def arrived(self, c, u):
        piece = self.piece(c, u)
        remote(piece, piece, self.send_sem.at[0], self.recv_sem.at[c, u], (self.at(1, 0), self.head)).wait_recv()

    def both(self, c, axis, direction):
        for u in (0, 1):
            for d in (RIGHT, LEFT):
                self.go(c, 2 * axis + u, direction, d)

    def start(self):
        for u in (0, 1):
            for axis in (0, 1):
                for d in (RIGHT, LEFT):
                    self.go(self.me, 2 * axis + u, axis, d)

    def first(self):
        for axis in (0, 1):
            self.arrived(self.along(axis, LEFT), 2 * axis)
            self.go(self.along(axis, LEFT), 2 * axis, axis, RIGHT)
            self.arrived(self.along(axis, RIGHT), 2 * axis + 1)
            self.go(self.along(axis, RIGHT), 2 * axis + 1, axis, LEFT)
        for axis in (0, 1):
            self.both(self.me, axis, 1 - axis)

    def turn(self):
        for axis in (0, 1):
            self.arrived(self.along(axis, LEFT), 2 * axis + 1)
            self.arrived(self.along(axis, RIGHT), 2 * axis)
            for s in (LEFT, RIGHT):
                self.both(self.along(axis, s), axis, 1 - axis)
        for axis in (0, 1):
            self.arrived(self.along(axis, OPPOSITE), 2 * axis)
            self.arrived(self.along(axis, OPPOSITE), 2 * axis + 1)
            self.both(self.along(axis, OPPOSITE), axis, 1 - axis)

    def second(self, s):
        for axis in (0, 1):
            self.arrived(self.along(axis, s, LEFT), 2 * axis)
            self.go(self.along(axis, s, LEFT), 2 * axis, 1 - axis, RIGHT)
            self.arrived(self.along(axis, s, RIGHT), 2 * axis + 1)
            self.go(self.along(axis, s, RIGHT), 2 * axis + 1, 1 - axis, LEFT)
        for axis in (0, 1):
            self.arrived(self.along(axis, s, LEFT), 2 * axis + 1)
            self.arrived(self.along(axis, s, RIGHT), 2 * axis)
            self.arrived(self.along(axis, s, OPPOSITE), 2 * axis)
            self.arrived(self.along(axis, s, OPPOSITE), 2 * axis + 1)

    def finish(self):
        for copy in self.sends:
            copy.wait_send()


def gather_project(
    place_ref, hid_hbm, gain_ref, qw_hbm, kvw_hbm, qb_ref, kvb_ref, store_hbm,
    q_ref, fresh_ref, blocks_hbm,
    hid, nrm, w, acc, hop_in, hop_out, qs, fpad,
    loc, w_send, w_recv, h1_send, h1_recv, h2_send, h2_recv, x_send, x_recv,
):
    me = lax.axis_index("cache")
    head = lax.axis_index("heads")
    core = lax.rem(head, 2)
    partner = (me, head + 1 - 2 * core)
    owners = SIDE * SIDE
    rows = hid.shape[0]
    depth, width = w.shape[1], w.shape[2]
    unit, half = depth // 4, depth // 2
    q_cols = qw_hbm.shape[1]
    hd = width - q_cols

    own_q = pltpu.make_async_copy(qw_hbm, w.at[me, :, 0:q_cols], loc.at[0])
    own_kv = pltpu.make_async_copy(
        kvw_hbm.at[:, pl.ds(pl.multiple_of(head * hd, hd), hd)], w.at[me, :, q_cols:width], loc.at[1]
    )
    own_hid = pltpu.make_async_copy(hid_hbm, hid, loc.at[2])
    own_hop = pltpu.make_async_copy(store_hbm.at[:, me, core], hop_in.at[pl.ds(me * 8, 8)], loc.at[3])
    own_q.start()
    own_kv.start()
    own_hop.start()
    own_hid.start()

    barrier = pltpu.get_barrier_semaphore()

    @pl.loop(1, owners)
    def _(o):
        pl.semaphore_signal(barrier, inc=1, device_id=(lax.rem(me + o, owners), head), device_id_type=MESH)

    pl.semaphore_signal(barrier, inc=1, device_id=partner, device_id_type=MESH)
    pl.semaphore_wait(barrier, owners)

    def hop1(o):
        to = lax.rem(me + o, owners)
        return remote(
            store_hbm.at[:, to, core], hop_in.at[pl.ds(me * 8, 8)], h1_send.at[o], h1_recv.at[me], (to, head)
        )

    def hop1_from(o):
        src = lax.rem(me + owners - o, owners)
        return remote(
            store_hbm.at[:, src, core], hop_in.at[pl.ds(src * 8, 8)], h1_send.at[o], h1_recv.at[src], (src, head)
        )

    def hop2(o):
        to = lax.rem(me + o, owners)
        return remote(hop_out.at[to], blocks_hbm.at[:, me, core], h2_send.at[o], h2_recv.at[me], (to, head))

    def hop2_from(o):
        src = lax.rem(me + owners - o, owners)
        return remote(hop_out.at[src], blocks_hbm.at[:, src, core], h2_send.at[o], h2_recv.at[src], (src, head))

    @pl.loop(1, owners)
    def _(o):
        hop1(o).start()

    own_q.wait()
    own_kv.wait()

    spread = Spread(lambda c, u: w.at[c, pl.ds(u * unit, unit)], w_send, w_recv, me, head)
    spread.start()

    own_hid.wait()
    tall = 16

    @pl.loop(0, rows // tall)
    def _(i):
        lines = pl.ds(pl.multiple_of(i * tall, tall), tall)
        total = jnp.zeros((tall, 1), F32)
        for c in range(owners):
            v = hid[lines, c * depth : (c + 1) * depth].astype(F32)
            total += jnp.sum(v * v, axis=-1, keepdims=True)
        factor = lax.rsqrt(total / (owners * depth) + 1e-06)
        for c in range(owners):
            v = hid[lines, c * depth : (c + 1) * depth].astype(F32)
            g = gain_ref[:, c * depth : (c + 1) * depth].astype(F32)
            nrm[c, lines, :] = (v * factor * g).astype(BF16)

    acc[...] = jnp.zeros_like(acc)

    def multiply(c, axis):
        lo = axis * half
        acc[...] += jnp.dot(nrm[c, :, lo : lo + half], w[c, lo : lo + half, :], preferred_element_type=F32)

    spread.first()

    own_hop.wait()

    @pl.loop(1, owners)
    def _(o):
        hop1_from(o).wait_recv()

    @pl.loop(0, owners)
    def _(i):
        for r in range(8):
            hop_out[i, r] = hop_in[place_ref[i * 8 + r]]

    @pl.loop(1, owners)
    def _(o):
        hop2(o).start()

    own_out = pltpu.make_async_copy(hop_out.at[me], blocks_hbm.at[:, me, core], loc.at[4])
    own_out.start()

    spread.turn()

    @pl.loop(0, SIDE)
    def _(i):
        multiply(spread.along(0, i), 0)
        multiply(spread.along(1, i), 1)

    def core_swap(which):
        return remote(
            blocks_hbm.at[:, :, which], blocks_hbm.at[:, :, which], x_send.at[0], x_recv.at[0], partner
        )

    for n, s in enumerate((0, LEFT, RIGHT, OPPOSITE)):
        spread.second(s)

        @pl.loop(1, SIDE)
        def _(i):
            multiply(spread.along(0, s, i), 0)
            multiply(spread.along(1, s, i), 1)

        if n == 2:
            own_out.wait()

            @pl.loop(1, owners)
            def _(o):
                hop2_from(o).wait_recv()

            core_swap(core).start()

    per = rows // 8
    heads = q_cols // hd
    bias = qb_ref[...].astype(F32)
    kv_bias = kvb_ref[:, pl.ds(pl.multiple_of(head * hd, hd), hd)].astype(F32)
    for r in range(8):
        lines = slice(per * r, per * (r + 1))
        for j in range(heads):
            at_row = (r * heads + j) * per
            qs[at_row : at_row + per, :] = acc[lines, j * hd : (j + 1) * hd] + bias[:, j * hd : (j + 1) * hd]
        fpad[r * PAD : r * PAD + per, :] = acc[lines, q_cols:width] + kv_bias
        fpad[r * PAD + per : (r + 1) * PAD, :] = jnp.zeros((PAD - per, hd), F32)
    fresh_ref[core] = fpad[...].astype(BF16)
    swap = remote(fresh_ref.at[core], fresh_ref.at[core], x_send.at[1], x_recv.at[1], partner)
    swap.start()
    q_ref[...] = qs[...].astype(BF16)

    core_swap(1 - core).wait_recv()
    remote(fresh_ref.at[1 - core], fresh_ref.at[1 - core], x_send.at[1], x_recv.at[1], partner).wait_recv()
    swap.wait_send()
    core_swap(core).wait_send()
    spread.finish()

    @pl.loop(1, owners)
    def _(o):
        hop1(o).wait_send()
        hop2(o).wait_send()


def attend(q_ref, fresh_ref, blocks_ref, row_ref, pos_ref, ctx_ref, ks, vs, sc, top, low, out, flat):
    stretches, length = blocks_ref.shape[0], blocks_ref.shape[1]
    hd = q_ref.shape[1]
    total = q_ref.shape[0]
    group = total // stretches
    heads = ctx_ref.shape[1] // hd
    per = group // heads
    scale = math.log2(math.e) / math.sqrt(hd)
    ones = jnp.ones((PAD, hd), BF16)
    for r in range(stretches):
        hit = lax.broadcasted_iota(jnp.int32, (length, PAD), 0) == row_ref[r : r + 1, :]
        lines = slice(r * PAD, (r + 1) * PAD)
        table = jnp.concatenate([fresh_ref[0, lines, :], fresh_ref[1, lines, :], ones], axis=1)
        new = jnp.dot(hit.astype(F32).astype(BF16), table, preferred_element_type=F32)
        there = new[:, 2 * hd :] > 0.5
        ks[r] = jnp.where(there, new[:, :hd], blocks_ref[r, :, :hd].astype(F32)).astype(BF16)
        vs[r] = jnp.where(there, new[:, hd : 2 * hd], blocks_ref[r, :, hd:].astype(F32)).astype(BF16)
    top[...] = jnp.full_like(top, -jnp.inf)
    low[...] = jnp.zeros_like(low)
    out[...] = jnp.zeros_like(out)

    def fold(a, op):
        parts = [a[:, i * hd : (i + 1) * hd] for i in range(length // hd)]
        while len(parts) > 1:
            parts = [op(parts[i], parts[i + 1]) for i in range(0, len(parts), 2)]
        return parts[0]

    for s in range(stretches):
        scores = lax.dot_general(
            q_ref[s * group :, :], ks[s], (((1,), (1,)), ((), ())), preferred_element_type=F32
        )
        key = lax.broadcasted_iota(jnp.int32, (group, length), 1)
        first = jnp.where(key <= pos_ref[s * group : (s + 1) * group, :], scores[:group], -jnp.inf)
        sc[s, s * group : (s + 1) * group, :] = first
        top[s * group : (s + 1) * group, :] = jnp.maximum(
            top[s * group : (s + 1) * group, :], fold(first, jnp.maximum)
        )
        if s + 1 < stretches:
            sc[s, (s + 1) * group :, :] = scores[group:]
            top[(s + 1) * group :, :] = jnp.maximum(top[(s + 1) * group :, :], fold(scores[group:], jnp.maximum))
    top[...] = jnp.broadcast_to(jnp.max(top[...], axis=1, keepdims=True), top.shape)
    for s in range(stretches):
        here = slice(s * group, total)
        peak = top[here, :]
        expon = jnp.concatenate(
            [jnp.exp2((sc[s, here, i * hd : (i + 1) * hd] - peak) * scale) for i in range(length // hd)], axis=1
        )
        low[here, :] += fold(expon, jnp.add)
        out[here, :] += jnp.dot(expon.astype(BF16), vs[s], preferred_element_type=F32)
    out[...] = out[...] / jnp.sum(low[...], axis=1, keepdims=True)
    for r in range(stretches):
        for j in range(heads):
            at_row = (r * heads + j) * per
            flat[r * per : (r + 1) * per, j * hd : (j + 1) * hd] = out[at_row : at_row + per, :]
    ctx_ref[...] = flat[...].astype(BF16)


def project_out(
    slot_ref, pick_ref, ctx_ref, w_ref, fresh_ref,
    out_ref, back_ref,
    ctxs, pair_out, pair_in, own, r_out, l_out, r_in, l_in, f_out, f_in, total_out,
    c_send, c_recv, p_send, p_recv, r_send, r_recv, l_send, l_recv, f_send, f_recv, b_send, b_recv,
):
    me = lax.axis_index("cache")
    head = lax.axis_index("heads")
    owners = lax.axis_size("cache")
    ring = lax.axis_size("heads") // 2
    core = lax.rem(head, 2)
    z = head // 2
    partner = (me, head + 1 - 2 * core)
    right = (me, lax.rem(z + 1, ring) * 2 + core)
    left = (me, lax.rem(z + ring - 1, ring) * 2 + core)
    mirror = (head, me)
    rows = ctx_ref.shape[0]
    hrow = rows // 2
    order = (4, 3, -3, 2, -2, 1, -1, 0)

    def request(n, parity):
        return lax.rem(z + order[n] + ring, ring) * 2 + parity

    barrier = pltpu.get_barrier_semaphore()

    @pl.loop(1, owners)
    def _(o):
        pl.semaphore_signal(barrier, inc=1, device_id=(lax.rem(me + o, owners), head), device_id_type=MESH)

    for peer in (partner, left, right):
        pl.semaphore_signal(barrier, inc=1, device_id=peer, device_id_type=MESH)

    @pl.when(me != head)
    def _():
        pl.semaphore_signal(barrier, inc=1, device_id=mirror, device_id_type=MESH)

    ctxs[me] = ctx_ref[...]

    @pl.when(me != head)
    def _():
        pl.semaphore_wait(barrier, owners + 3)

    @pl.when(me == head)
    def _():
        pl.semaphore_wait(barrier, owners + 2)

    quarter = rows // 4
    spread = Spread(lambda c, u: ctxs.at[c, pl.ds(u * quarter, quarter)], c_send, c_recv, me, head)
    spread.start()

    @pl.loop(0, owners)
    def _(o):
        for m in range(2):
            f_out[2 * o + m] = fresh_ref[core, slot_ref[2 * o + m]]

    def give(o):
        to = lax.rem(me + o, owners)
        return remote(
            f_out.at[pl.ds(2 * to, 2)], f_in.at[pl.ds(2 * me, 2)], f_send.at[o], f_recv.at[me], (to, head)
        )

    def take(o):
        src = lax.rem(me + owners - o, owners)
        return remote(
            f_out.at[pl.ds(2 * src, 2)], f_in.at[pl.ds(2 * src, 2)], f_send.at[o], f_recv.at[src], (src, head)
        )

    for m in range(2):
        f_in[2 * me + m] = f_out[2 * me + m]

    spread.first()
    spread.turn()

    @pl.loop(1, owners)
    def _(o):
        give(o).start()

    for s in (0, LEFT, RIGHT, OPPOSITE):
        spread.second(s)

    def pair(n):
        return remote(pair_out.at[n], pair_in.at[n], p_send.at[n], p_recv.at[n], partner)

    for n in range(len(order)):
        pair_out[n] = jnp.dot(ctxs[request(n, 1 - core)], w_ref[...], preferred_element_type=F32).astype(BF16)
        pair(n).start()
        own[n] = jnp.dot(ctxs[request(n, core)], w_ref[...], preferred_element_type=F32).astype(BF16)

    def lines(part):
        return slice(part * hrow, (part + 1) * hrow)

    def total(n, part):
        return own[n, lines(part), :].astype(F32) + pair_in[n, lines(part), :].astype(F32)

    def ring_copy(step, part, out, into, send_sem, recv_sem, to):
        return remote(
            out.at[step, pl.ds(part * hrow, hrow)],
            into.at[step, pl.ds(part * hrow, hrow)],
            send_sem.at[step, part],
            recv_sem.at[step, part],
            to,
        )

    def rightward(step, part):
        return ring_copy(step, part, r_out, r_in, r_send, r_recv, right)

    def leftward(step, part):
        return ring_copy(step, part, l_out, l_in, l_send, l_recv, left)

    pair(0).wait_recv()
    r_out[0, lines(0), :] = total(0, 0).astype(BF16)
    rightward(0, 0).start()
    l_out[0, lines(1), :] = total(0, 1).astype(BF16)
    leftward(0, 1).start()
    for step in (1, 2, 3):
        n_right, n_left = 2 * step - 1, 2 * step
        pair(n_right).wait_recv()
        pair(n_left).wait_recv()
        parts = ((1, 0), (0, 1)) if step == 1 else ((0, 1), (1, 0))
        for right_part, left_part in zip(*parts):
            value = total(n_right, right_part)
            if step > 1 or right_part == 0:
                rightward(step - 1, right_part).wait_recv()
                value += r_in[step - 1, lines(right_part), :].astype(F32)
            r_out[step, lines(right_part), :] = value.astype(BF16)
            rightward(step, right_part).start()
            value = total(n_left, left_part)
            if step > 1 or left_part == 1:
                leftward(step - 1, left_part).wait_recv()
                value += l_in[step - 1, lines(left_part), :].astype(F32)
            l_out[step, lines(left_part), :] = value.astype(BF16)
            leftward(step, left_part).start()

    @pl.loop(1, owners)
    def _(o):
        take(o).wait_recv()

    for s in range(back_ref.shape[1]):
        back_ref[core, s] = f_in[pick_ref[s]]
    swap = remote(back_ref.at[core], back_ref.at[core], b_send.at[0], b_recv.at[0], partner)
    swap.start()

    pair(7).wait_recv()
    for part in (0, 1):
        rightward(3, part).wait_recv()
        leftward(3, part).wait_recv()
        value = total(7, part) + r_in[3, lines(part), :].astype(F32) + l_in[3, lines(part), :].astype(F32)
        total_out[lines(part), :] = value.astype(BF16)

    flip = remote(total_out, out_ref, b_send.at[1], b_recv.at[1], mirror)

    @pl.when(me != head)
    def _():
        flip.start()

    @pl.when(me == head)
    def _():
        out_ref[...] = total_out[...]

    remote(back_ref.at[1 - core], back_ref.at[1 - core], b_send.at[0], b_recv.at[0], partner).wait_recv()
    swap.wait_send()
    for n in range(len(order)):
        pair(n).wait_send()
    rightward(0, 0).wait_send()
    leftward(0, 1).wait_send()
    for step in (1, 2, 3):
        for part in (0, 1):
            rightward(step, part).wait_send()
            leftward(step, part).wait_send()

    @pl.loop(1, owners)
    def _(o):
        give(o).wait_send()

    spread.finish()

    @pl.when(me != head)
    def _():
        flip.wait()


def write_back(store_ref, back_ref, row_ref, new_ref):
    length, hd = store_ref.shape[2], back_ref.shape[3]
    hit = lax.broadcasted_iota(jnp.int32, (length, PAD), 0) == row_ref[0]
    table = jnp.concatenate([back_ref[0, 0], back_ref[1, 0], jnp.ones((PAD, hd), BF16)], axis=1)
    new = jnp.dot(hit.astype(F32).astype(BF16), table, preferred_element_type=F32)
    there = new[:, 2 * hd :] > 0.5
    for part in (0, 1):
        lanes = slice(part * hd, (part + 1) * hd)
        new_ref[0, 0, :, lanes] = jnp.where(there, new[:, lanes], store_ref[0, 0, :, lanes].astype(F32)).astype(BF16)


def whole(shape=None):
    return pl.BlockSpec(memory_space=pltpu.VMEM)


def shards(
    hidden, norm_gain, q_weight, q_bias, kv_weight, kv_bias, out_weight, kv_store, stretch_place, req_stretches, rec_rows
):
    owners = lax.axis_size("cache")
    me = lax.axis_index("cache")
    rows, width = hidden.shape
    stretches, _, length, kv_width = kv_store.shape
    hd = kv_width // 2
    per = rec_rows.shape[2]
    depth, q_cols = q_weight.shape
    heads = q_cols // hd
    vmem = pl.BlockSpec(memory_space=pltpu.VMEM)
    smem = pl.BlockSpec(memory_space=pltpu.SMEM)
    hbm = pl.BlockSpec(memory_space=pl.ANY)
    dma = pltpu.SemaphoreType.DMA

    places = stretch_place[req_stretches]
    owner_of = places // stretches
    earlier = jnp.arange(stretches)[None, :] < jnp.arange(stretches)[:, None]
    rank_of = jnp.sum((owner_of[:, :, None] == owner_of[:, None, :]) & earlier[None], axis=2).astype(jnp.int32)
    pair_of = owner_of * 2 + rank_of
    my_pair = lax.dynamic_index_in_dim(pair_of, me, 0, keepdims=False)
    order = jnp.arange(stretches, dtype=jnp.int32)
    slot_r = jnp.sum((my_pair[None, :] == jnp.arange(2 * owners)[:, None]) * order[None, :], axis=1).astype(jnp.int32)
    flat_places = places.reshape(-1)
    mine = flat_places[None, :] == (me * stretches + order)[:, None]
    source = jnp.arange(owners)[:, None] * 2 + rank_of
    pick = jnp.sum(mine * source.reshape(1, -1), axis=1).astype(jnp.int32)
    slot_rows = jnp.sum(mine[:, :, None] * rec_rows.reshape(1, -1, per), axis=1).astype(jnp.int32)
    slot_rows = jnp.pad(slot_rows, ((0, 0), (0, PAD - per)), constant_values=-1)
    my_rows = lax.dynamic_index_in_dim(rec_rows, me, 0, keepdims=False)
    pad_rows = jnp.pad(my_rows, ((0, 0), (0, PAD - per)), constant_values=-1)
    row_pos = jnp.broadcast_to(my_rows[:, None, :], (stretches, heads, per)).reshape(rows * heads, 1)

    store = kv_store.reshape(stretches, owners, 2, length // (2 * owners), kv_width)
    piece = length // (2 * owners)

    queries, fresh, blocks = pl.pallas_call(
        gather_project,
        out_shape=(
            jax.ShapeDtypeStruct((rows * heads, hd), BF16),
            jax.ShapeDtypeStruct((2, stretches * PAD, hd), BF16),
            jax.ShapeDtypeStruct((stretches, owners, 2, piece, kv_width), BF16),
        ),
        in_specs=[smem, hbm, vmem, hbm, hbm, vmem, vmem, hbm],
        out_specs=(vmem, vmem, hbm),
        scratch_shapes=[
            pltpu.VMEM((rows, width), BF16),
            pltpu.VMEM((owners, rows, depth), BF16),
            pltpu.VMEM((owners, depth, q_cols + hd), BF16),
            pltpu.VMEM((rows, q_cols + hd), F32),
            pltpu.VMEM((owners * stretches, piece, kv_width), BF16),
            pltpu.VMEM((owners, stretches, piece, kv_width), BF16),
            pltpu.VMEM((rows * heads, hd), F32),
            pltpu.VMEM((stretches * PAD, hd), F32),
            dma((5,)),
            dma((60,)),
            dma((owners, 4)),
            dma((owners,)),
            dma((owners,)),
            dma((owners,)),
            dma((owners,)),
            dma((2,)),
            dma((2,)),
        ],
        compiler_params=pltpu.CompilerParams(collective_id=0, has_side_effects=True, vmem_limit_bytes=48 << 20),
        name="gather_project",
    )(
        flat_places, hidden, norm_gain.reshape(1, -1), q_weight, kv_weight,
        q_bias.reshape(1, -1), kv_bias.reshape(1, -1), store,
    )
    blocks = blocks.reshape(stretches, length, kv_width)

    context = pl.pallas_call(
        attend,
        out_shape=jax.ShapeDtypeStruct((rows, q_cols), BF16),
        in_specs=[vmem] * 5,
        out_specs=vmem,
        scratch_shapes=[
            pltpu.VMEM((stretches, length, hd), BF16),
            pltpu.VMEM((stretches, length, hd), BF16),
            pltpu.VMEM((stretches, rows * heads, length), F32),
            pltpu.VMEM((rows * heads, hd), F32),
            pltpu.VMEM((rows * heads, hd), F32),
            pltpu.VMEM((rows * heads, hd), F32),
            pltpu.VMEM((rows, q_cols), F32),
        ],
        compiler_params=pltpu.CompilerParams(vmem_limit_bytes=48 << 20),
        name="attend",
    )(queries, fresh, blocks, pad_rows, row_pos)

    ring = 8
    attn_out, back = pl.pallas_call(
        project_out,
        out_shape=(
            jax.ShapeDtypeStruct((rows, q_cols), BF16),
            jax.ShapeDtypeStruct((2, stretches, PAD, hd), BF16),
        ),
        in_specs=[smem, smem, vmem, vmem, vmem],
        out_specs=(vmem, vmem),
        scratch_shapes=[
            pltpu.VMEM((owners, rows, q_cols), BF16),
            pltpu.VMEM((ring, rows, q_cols), BF16),
            pltpu.VMEM((ring, rows, q_cols), BF16),
            pltpu.VMEM((ring, rows, q_cols), BF16),
            pltpu.VMEM((4, rows, q_cols), BF16),
            pltpu.VMEM((4, rows, q_cols), BF16),
            pltpu.VMEM((4, rows, q_cols), BF16),
            pltpu.VMEM((4, rows, q_cols), BF16),
            pltpu.VMEM((2 * owners, PAD, hd), BF16),
            pltpu.VMEM((2 * owners, PAD, hd), BF16),
            pltpu.VMEM((rows, q_cols), BF16),
            dma((60,)),
            dma((owners, 4)),
            dma((ring,)),
            dma((ring,)),
            dma((4, 2)),
            dma((4, 2)),
            dma((4, 2)),
            dma((4, 2)),
            dma((owners,)),
            dma((owners,)),
            dma((2,)),
            dma((2,)),
        ],
        compiler_params=pltpu.CompilerParams(collective_id=1, has_side_effects=True, vmem_limit_bytes=48 << 20),
        name="project_out",
    )(slot_r, pick, context, out_weight, fresh.reshape(2, stretches, PAD, hd))

    new_store = pl.pallas_call(
        write_back,
        grid=(stretches,),
        out_shape=jax.ShapeDtypeStruct(kv_store.shape, BF16),
        in_specs=[
            pl.BlockSpec((1, 1, length, kv_width), lambda s: (s, 0, 0, 0)),
            pl.BlockSpec((2, 1, PAD, hd), lambda s: (0, s, 0, 0)),
            pl.BlockSpec((1, 1, PAD), lambda s: (s, 0, 0)),
        ],
        out_specs=pl.BlockSpec((1, 1, length, kv_width), lambda s: (s, 0, 0, 0)),
        name="write_back",
    )(kv_store, back, slot_rows.reshape(stretches, 1, PAD))
    return (attn_out, new_store)


def solution(mesh):
    placed = (
        P("cache", None),
        P(),
        P("cache", "heads"),
        P("heads"),
        P("cache", None),
        P(),
        P("heads", "cache"),
        P("cache", "heads", None, None),
        P(),
        P(),
        P(),
    )
    return jax.shard_map(
        shards,
        mesh=mesh,
        in_specs=placed,
        out_specs=(P("cache", "heads"), P("cache", "heads", None, None)),
        check_vma=False,
    )
```

```python
import functools
import math

import jax
import jax.numpy as jnp
from jax import lax
from jax.experimental import pallas as pl
from jax.experimental.pallas import tpu as pltpu
from jax.sharding import PartitionSpec as P

MESH = pl.DeviceIdType.MESH
SIDE = 4
BF16 = jnp.bfloat16
F32 = jnp.float32
RIGHT, OPPOSITE, LEFT = 1, 2, 3
PAD = 32


def remote(src, dst, send_sem, recv_sem, device):
    return pltpu.make_async_remote_copy(
        src_ref=src, dst_ref=dst, send_sem=send_sem, recv_sem=recv_sem, device_id=device, device_id_type=MESH
    )


class Spread:
    def __init__(self, piece, send_sem, recv_sem, me, head):
        self.piece, self.send_sem, self.recv_sem, self.head = piece, send_sem, recv_sem, head
        self.me, self.x, self.y = me, me // SIDE, lax.rem(me, SIDE)
        self.sends = []

    def at(self, dx, dy):
        return lax.rem(self.x + dx, SIDE) * SIDE + lax.rem(self.y + dy, SIDE)

    def along(self, axis, d, s=0):
        return self.at(d, s) if axis == 0 else self.at(s, d)

    def go(self, c, u, axis, d):
        piece = self.piece(c, u)
        copy = remote(
            piece, piece, self.send_sem.at[len(self.sends)], self.recv_sem.at[c, u], (self.along(axis, d), self.head)
        )
        copy.start()
        self.sends.append(copy)

    def arrived(self, c, u):
        piece = self.piece(c, u)
        remote(piece, piece, self.send_sem.at[0], self.recv_sem.at[c, u], (self.at(1, 0), self.head)).wait_recv()

    def both(self, c, axis, direction):
        for u in (0, 1):
            for d in (RIGHT, LEFT):
                self.go(c, 2 * axis + u, direction, d)

    def start(self):
        for u in (0, 1):
            for axis in (0, 1):
                for d in (RIGHT, LEFT):
                    self.go(self.me, 2 * axis + u, axis, d)

    def first(self):
        for axis in (0, 1):
            self.arrived(self.along(axis, LEFT), 2 * axis)
            self.go(self.along(axis, LEFT), 2 * axis, axis, RIGHT)
            self.arrived(self.along(axis, RIGHT), 2 * axis + 1)
            self.go(self.along(axis, RIGHT), 2 * axis + 1, axis, LEFT)
        for axis in (0, 1):
            self.both(self.me, axis, 1 - axis)

    def turn(self):
        for axis in (0, 1):
            self.arrived(self.along(axis, LEFT), 2 * axis + 1)
            self.arrived(self.along(axis, RIGHT), 2 * axis)
            for s in (LEFT, RIGHT):
                self.both(self.along(axis, s), axis, 1 - axis)
        for axis in (0, 1):
            self.arrived(self.along(axis, OPPOSITE), 2 * axis)
            self.arrived(self.along(axis, OPPOSITE), 2 * axis + 1)
            self.both(self.along(axis, OPPOSITE), axis, 1 - axis)

    def second(self, s):
        for axis in (0, 1):
            self.arrived(self.along(axis, s, LEFT), 2 * axis)
            self.go(self.along(axis, s, LEFT), 2 * axis, 1 - axis, RIGHT)
            self.arrived(self.along(axis, s, RIGHT), 2 * axis + 1)
            self.go(self.along(axis, s, RIGHT), 2 * axis + 1, 1 - axis, LEFT)
        for axis in (0, 1):
            self.arrived(self.along(axis, s, LEFT), 2 * axis + 1)
            self.arrived(self.along(axis, s, RIGHT), 2 * axis)
            self.arrived(self.along(axis, s, OPPOSITE), 2 * axis)
            self.arrived(self.along(axis, s, OPPOSITE), 2 * axis + 1)

    def finish(self):
        for copy in self.sends:
            copy.wait_send()


def gather_project(
    place_ref, hid_hbm, gain_ref, qw_hbm, kvw_hbm, qb_ref, kvb_ref, store_hbm,
    q_ref, fresh_ref, blocks_hbm,
    hid, nrm, acts, w, acc, part, sums, hop_in, hop_out, qs, fpad,
    loc, w_send, w_recv, a_send, a_recv, c_send, c_recv, s_send, s_recv,
    h1_send, h1_recv, h2_send, h2_recv, x_send, x_recv,
):
    me = lax.axis_index("cache")
    head = lax.axis_index("heads")
    core = lax.rem(head, 2)
    partner = (me, head + 1 - 2 * core)
    x, y = me // SIDE, lax.rem(me, SIDE)
    owners = SIDE * SIDE
    rows = hid.shape[0]
    depth, width = w.shape[1], w.shape[2]
    q_cols = qw_hbm.shape[1]
    hd = width - q_cols

    def ring(i, d):
        return lax.rem(i + d, SIDE)

    own_hid = pltpu.make_async_copy(hid_hbm, hid, loc.at[2])
    own_q = pltpu.make_async_copy(qw_hbm, w.at[x, :, 0:q_cols], loc.at[0])
    own_kv = pltpu.make_async_copy(
        kvw_hbm.at[:, pl.ds(pl.multiple_of(head * hd, hd), hd)], w.at[x, :, q_cols:width], loc.at[1]
    )
    own_hop = pltpu.make_async_copy(store_hbm.at[:, me, core], hop_in.at[pl.ds(me * 8, 8)], loc.at[3])
    own_hid.start()
    own_q.start()
    own_kv.start()
    own_hop.start()

    barrier = pltpu.get_barrier_semaphore()

    @pl.loop(1, owners)
    def _(o):
        pl.semaphore_signal(barrier, inc=1, device_id=(lax.rem(me + o, owners), head), device_id_type=MESH)

    pl.semaphore_signal(barrier, inc=1, device_id=partner, device_id_type=MESH)

    own_hid.wait()
    tall = 16

    @pl.loop(0, rows // tall)
    def _(i):
        lines = pl.ds(pl.multiple_of(i * tall, tall), tall)
        total = jnp.zeros((tall, 1), F32)
        for c in range(owners):
            v = hid[lines, c * depth : (c + 1) * depth].astype(F32)
            total += jnp.sum(v * v, axis=-1, keepdims=True)
        factor = lax.rsqrt(total / (owners * depth) + 1e-06)
        for c in range(owners):
            v = hid[lines, c * depth : (c + 1) * depth].astype(F32)
            g = gain_ref[:, c * depth : (c + 1) * depth].astype(F32)
            nrm[c, lines, :] = (v * factor * g).astype(BF16)

    pl.semaphore_wait(barrier, owners)

    def rows_to(d, i):
        to = ring(y, d)
        return remote(
            nrm.at[(2 * core + i) * SIDE + to], acts.at[2 * core + i, y], a_send.at[d, i], a_recv.at[d, i],
            (x * SIDE + to, head),
        )

    def hop1(o):
        to = lax.rem(me + o, owners)
        return remote(
            store_hbm.at[:, to, core], hop_in.at[pl.ds(me * 8, 8)], h1_send.at[o], h1_recv.at[me], (to, head)
        )

    def hop1_from(o):
        src = lax.rem(me + owners - o, owners)
        return remote(
            store_hbm.at[:, src, core], hop_in.at[pl.ds(src * 8, 8)], h1_send.at[o], h1_recv.at[src], (src, head)
        )

    def hop2(o):
        to = lax.rem(me + o, owners)
        return remote(hop_out.at[to], blocks_hbm.at[:, me, core], h2_send.at[o], h2_recv.at[me], (to, head))

    def hop2_from(o):
        src = lax.rem(me + owners - o, owners)
        return remote(hop_out.at[src], blocks_hbm.at[:, src, core], h2_send.at[o], h2_recv.at[src], (src, head))

    def weights_to(d):
        to = ring(x, d)
        return remote(w.at[x], w.at[x], w_send.at[d], w_recv.at[d], (to * SIDE + y, head))

    def weights_from(d):
        src = ring(x, SIDE - d)
        return remote(w.at[src], w.at[src], w_send.at[d], w_recv.at[d], (src * SIDE + y, head))

    steps = (RIGHT, LEFT, OPPOSITE)
    for i in (0, 1):
        for d in steps:
            rows_to(d, i).start()

    @pl.loop(1, owners)
    def _(o):
        hop1(o).start()

    own_q.wait()
    own_kv.wait()
    for d in steps:
        weights_to(d).start()

    for i in range(SIDE):
        pltpu.make_async_copy(nrm.at[i * SIDE + y], acts.at[i, y], loc.at[5 + i]).start()

    def rows_from(d, i, which):
        src = ring(y, SIDE - d)
        place = acts.at[2 * which + i, src]
        return remote(place, place, a_send.at[d, i], a_recv.at[d, i], (x * SIDE + src, head))

    def rows_over(d, i, which):
        place = acts.at[2 * which + i, ring(y, SIDE - d)]
        return remote(place, place, c_send.at[d, i], c_recv.at[d, i], partner)

    for i in (0, 1):
        for d in steps:
            rows_from(d, i, core).wait_recv()
            rows_over(d, i, core).start()

    own_hop.wait()

    @pl.loop(1, owners)
    def _(o):
        hop1_from(o).wait_recv()

    @pl.loop(0, owners)
    def _(i):
        for r in range(8):
            hop_out[i, r] = hop_in[place_ref[i * 8 + r]]

    @pl.loop(1, owners)
    def _(o):
        hop2(o).start()

    own_out = pltpu.make_async_copy(hop_out.at[me], blocks_hbm.at[:, me, core], loc.at[4])
    own_out.start()

    for i in range(SIDE):
        pltpu.make_async_copy(nrm.at[i * SIDE + y], acts.at[i, y], loc.at[5 + i]).wait()
    for d in steps:
        weights_from(d).wait_recv()

    def product(i, j):
        return jnp.dot(acts[i, j], w[i], preferred_element_type=F32)

    @pl.loop(0, SIDE)
    def _(j):
        acc[j] = product(2 * core, j)
        acc[j] += product(2 * core + 1, j)

    for i in (0, 1):
        for d in steps:
            rows_over(d, i, 1 - core).wait_recv()

    def sums_to(d):
        to = ring(y, d)
        return remote(part.at[d], sums.at[d], s_send.at[d], s_recv.at[d], (x * SIDE + to, head))

    for d in (OPPOSITE, RIGHT, LEFT):
        j = ring(y, d)
        acc[j] += product(2 - 2 * core, j)
        part[d] = (acc[j] + product(3 - 2 * core, j)).astype(BF16)
        sums_to(d).start()
    acc[y] += product(2 - 2 * core, y)
    acc[y] += product(3 - 2 * core, y)

    def core_swap(which):
        return remote(
            blocks_hbm.at[:, :, which], blocks_hbm.at[:, :, which], x_send.at[0], x_recv.at[0], partner
        )

    own_out.wait()

    @pl.loop(1, owners)
    def _(o):
        hop2_from(o).wait_recv()

    core_swap(core).start()

    for d in steps:
        sums_to(d).wait_recv()
        acc[y] += sums[d].astype(F32)

    per = rows // 8
    heads = q_cols // hd
    bias = qb_ref[...].astype(F32)
    kv_bias = kvb_ref[:, pl.ds(pl.multiple_of(head * hd, hd), hd)].astype(F32)
    for r in range(8):
        lines = slice(per * r, per * (r + 1))
        for j in range(heads):
            at_row = (r * heads + j) * per
            qs[at_row : at_row + per, :] = acc[y, lines, j * hd : (j + 1) * hd] + bias[:, j * hd : (j + 1) * hd]
        fpad[r * PAD : r * PAD + per, :] = acc[y, lines, q_cols:width] + kv_bias
        fpad[r * PAD + per : (r + 1) * PAD, :] = jnp.zeros((PAD - per, hd), F32)
    fresh_ref[core] = fpad[...].astype(BF16)
    swap = remote(fresh_ref.at[core], fresh_ref.at[core], x_send.at[1], x_recv.at[1], partner)
    swap.start()
    q_ref[...] = qs[...].astype(BF16)

    for i in (0, 1):
        for d in steps:
            rows_to(d, i).wait_send()
            rows_over(d, i, core).wait_send()
    for d in steps:
        weights_to(d).wait_send()
        sums_to(d).wait_send()

    @pl.loop(1, owners)
    def _(o):
        hop1(o).wait_send()
        hop2(o).wait_send()

    core_swap(1 - core).wait_recv()
    remote(fresh_ref.at[1 - core], fresh_ref.at[1 - core], x_send.at[1], x_recv.at[1], partner).wait_recv()
    swap.wait_send()
    core_swap(core).wait_send()


def attend(q_ref, fresh_ref, blocks_ref, row_ref, pos_ref, ctx_ref, ks, vs, sc, top, low, out, flat):
    stretches, length = blocks_ref.shape[0], blocks_ref.shape[1]
    hd = q_ref.shape[1]
    total = q_ref.shape[0]
    group = total // stretches
    heads = ctx_ref.shape[1] // hd
    per = group // heads
    scale = math.log2(math.e) / math.sqrt(hd)
    ones = jnp.ones((PAD, hd), BF16)
    for r in range(stretches):
        hit = lax.broadcasted_iota(jnp.int32, (length, PAD), 0) == row_ref[r : r + 1, :]
        lines = slice(r * PAD, (r + 1) * PAD)
        table = jnp.concatenate([fresh_ref[0, lines, :], fresh_ref[1, lines, :], ones], axis=1)
        new = jnp.dot(hit.astype(F32).astype(BF16), table, preferred_element_type=F32)
        there = new[:, 2 * hd :] > 0.5
        ks[r] = jnp.where(there, new[:, :hd], blocks_ref[r, :, :hd].astype(F32)).astype(BF16)
        vs[r] = jnp.where(there, new[:, hd : 2 * hd], blocks_ref[r, :, hd:].astype(F32)).astype(BF16)
    top[...] = jnp.full_like(top, -jnp.inf)
    low[...] = jnp.zeros_like(low)
    out[...] = jnp.zeros_like(out)

    def fold(a, op):
        parts = [a[:, i * hd : (i + 1) * hd] for i in range(length // hd)]
        while len(parts) > 1:
            parts = [op(parts[i], parts[i + 1]) for i in range(0, len(parts), 2)]
        return parts[0]

    for s in range(stretches):
        scores = lax.dot_general(
            q_ref[s * group :, :], ks[s], (((1,), (1,)), ((), ())), preferred_element_type=F32
        )
        key = lax.broadcasted_iota(jnp.int32, (group, length), 1)
        first = jnp.where(key <= pos_ref[s * group : (s + 1) * group, :], scores[:group], -jnp.inf)
        sc[s, s * group : (s + 1) * group, :] = first
        top[s * group : (s + 1) * group, :] = jnp.maximum(
            top[s * group : (s + 1) * group, :], fold(first, jnp.maximum)
        )
        if s + 1 < stretches:
            sc[s, (s + 1) * group :, :] = scores[group:]
            top[(s + 1) * group :, :] = jnp.maximum(top[(s + 1) * group :, :], fold(scores[group:], jnp.maximum))
    top[...] = jnp.broadcast_to(jnp.max(top[...], axis=1, keepdims=True), top.shape)
    for s in range(stretches):
        here = slice(s * group, total)
        peak = top[here, :]
        expon = jnp.concatenate(
            [jnp.exp2((sc[s, here, i * hd : (i + 1) * hd] - peak) * scale) for i in range(length // hd)], axis=1
        )
        low[here, :] += fold(expon, jnp.add)
        out[here, :] += jnp.dot(expon.astype(BF16), vs[s], preferred_element_type=F32)
    out[...] = out[...] / jnp.sum(low[...], axis=1, keepdims=True)
    for r in range(stretches):
        for j in range(heads):
            at_row = (r * heads + j) * per
            flat[r * per : (r + 1) * per, j * hd : (j + 1) * hd] = out[at_row : at_row + per, :]
    ctx_ref[...] = flat[...].astype(BF16)


def project_out(
    slot_ref, pick_ref, ctx_ref, w_ref, fresh_ref,
    out_ref, back_ref,
    ctxs, pair_out, pair_in, own, r_out, l_out, r_in, l_in, f_out, f_in, total_out,
    c_send, c_recv, p_send, p_recv, r_send, r_recv, l_send, l_recv, f_send, f_recv, b_send, b_recv,
):
    me = lax.axis_index("cache")
    head = lax.axis_index("heads")
    owners = lax.axis_size("cache")
    ring = lax.axis_size("heads") // 2
    core = lax.rem(head, 2)
    z = head // 2
    partner = (me, head + 1 - 2 * core)
    right = (me, lax.rem(z + 1, ring) * 2 + core)
    left = (me, lax.rem(z + ring - 1, ring) * 2 + core)
    mirror = (head, me)
    rows = ctx_ref.shape[0]
    hrow = rows // 2
    order = (4, 3, -3, 2, -2, 1, -1, 0)

    def request(n, parity):
        return lax.rem(z + order[n] + ring, ring) * 2 + parity

    barrier = pltpu.get_barrier_semaphore()

    @pl.loop(1, owners)
    def _(o):
        pl.semaphore_signal(barrier, inc=1, device_id=(lax.rem(me + o, owners), head), device_id_type=MESH)

    for peer in (partner, left, right):
        pl.semaphore_signal(barrier, inc=1, device_id=peer, device_id_type=MESH)

    @pl.when(me != head)
    def _():
        pl.semaphore_signal(barrier, inc=1, device_id=mirror, device_id_type=MESH)

    ctxs[me] = ctx_ref[...]

    @pl.when(me != head)
    def _():
        pl.semaphore_wait(barrier, owners + 3)

    @pl.when(me == head)
    def _():
        pl.semaphore_wait(barrier, owners + 2)

    quarter = rows // 4
    spread = Spread(lambda c, u: ctxs.at[c, pl.ds(u * quarter, quarter)], c_send, c_recv, me, head)
    spread.start()

    @pl.loop(0, owners)
    def _(o):
        for m in range(2):
            f_out[2 * o + m] = fresh_ref[core, slot_ref[2 * o + m]]

    def give(o):
        to = lax.rem(me + o, owners)
        return remote(
            f_out.at[pl.ds(2 * to, 2)], f_in.at[pl.ds(2 * me, 2)], f_send.at[o], f_recv.at[me], (to, head)
        )

    def take(o):
        src = lax.rem(me + owners - o, owners)
        return remote(
            f_out.at[pl.ds(2 * src, 2)], f_in.at[pl.ds(2 * src, 2)], f_send.at[o], f_recv.at[src], (src, head)
        )

    for m in range(2):
        f_in[2 * me + m] = f_out[2 * me + m]

    spread.first()
    spread.turn()

    @pl.loop(1, owners)
    def _(o):
        give(o).start()

    for s in (0, LEFT, RIGHT, OPPOSITE):
        spread.second(s)

    def pair(n):
        return remote(pair_out.at[n], pair_in.at[n], p_send.at[n], p_recv.at[n], partner)

    for n in range(len(order)):
        pair_out[n] = jnp.dot(ctxs[request(n, 1 - core)], w_ref[...], preferred_element_type=F32).astype(BF16)
        pair(n).start()
        own[n] = jnp.dot(ctxs[request(n, core)], w_ref[...], preferred_element_type=F32).astype(BF16)

    def lines(part):
        return slice(part * hrow, (part + 1) * hrow)

    def total(n, part):
        return own[n, lines(part), :].astype(F32) + pair_in[n, lines(part), :].astype(F32)

    def ring_copy(step, part, out, into, send_sem, recv_sem, to):
        return remote(
            out.at[step, pl.ds(part * hrow, hrow)],
            into.at[step, pl.ds(part * hrow, hrow)],
            send_sem.at[step, part],
            recv_sem.at[step, part],
            to,
        )

    def rightward(step, part):
        return ring_copy(step, part, r_out, r_in, r_send, r_recv, right)

    def leftward(step, part):
        return ring_copy(step, part, l_out, l_in, l_send, l_recv, left)

    pair(0).wait_recv()
    r_out[0, lines(0), :] = total(0, 0).astype(BF16)
    rightward(0, 0).start()
    l_out[0, lines(1), :] = total(0, 1).astype(BF16)
    leftward(0, 1).start()
    for step in (1, 2, 3):
        n_right, n_left = 2 * step - 1, 2 * step
        pair(n_right).wait_recv()
        pair(n_left).wait_recv()
        parts = ((1, 0), (0, 1)) if step == 1 else ((0, 1), (1, 0))
        for right_part, left_part in zip(*parts):
            value = total(n_right, right_part)
            if step > 1 or right_part == 0:
                rightward(step - 1, right_part).wait_recv()
                value += r_in[step - 1, lines(right_part), :].astype(F32)
            r_out[step, lines(right_part), :] = value.astype(BF16)
            rightward(step, right_part).start()
            value = total(n_left, left_part)
            if step > 1 or left_part == 1:
                leftward(step - 1, left_part).wait_recv()
                value += l_in[step - 1, lines(left_part), :].astype(F32)
            l_out[step, lines(left_part), :] = value.astype(BF16)
            leftward(step, left_part).start()

    @pl.loop(1, owners)
    def _(o):
        take(o).wait_recv()

    for s in range(back_ref.shape[1]):
        back_ref[core, s] = f_in[pick_ref[s]]
    swap = remote(back_ref.at[core], back_ref.at[core], b_send.at[0], b_recv.at[0], partner)
    swap.start()

    pair(7).wait_recv()
    for part in (0, 1):
        rightward(3, part).wait_recv()
        leftward(3, part).wait_recv()
        value = total(7, part) + r_in[3, lines(part), :].astype(F32) + l_in[3, lines(part), :].astype(F32)
        total_out[lines(part), :] = value.astype(BF16)

    flip = remote(total_out, out_ref, b_send.at[1], b_recv.at[1], mirror)

    @pl.when(me != head)
    def _():
        flip.start()

    @pl.when(me == head)
    def _():
        out_ref[...] = total_out[...]

    remote(back_ref.at[1 - core], back_ref.at[1 - core], b_send.at[0], b_recv.at[0], partner).wait_recv()
    swap.wait_send()
    for n in range(len(order)):
        pair(n).wait_send()
    rightward(0, 0).wait_send()
    leftward(0, 1).wait_send()
    for step in (1, 2, 3):
        for part in (0, 1):
            rightward(step, part).wait_send()
            leftward(step, part).wait_send()

    @pl.loop(1, owners)
    def _(o):
        give(o).wait_send()

    spread.finish()

    @pl.when(me != head)
    def _():
        flip.wait()


def write_back(store_ref, back_ref, row_ref, new_ref):
    length, hd = store_ref.shape[2], back_ref.shape[3]
    hit = lax.broadcasted_iota(jnp.int32, (length, PAD), 0) == row_ref[0]
    table = jnp.concatenate([back_ref[0, 0], back_ref[1, 0], jnp.ones((PAD, hd), BF16)], axis=1)
    new = jnp.dot(hit.astype(F32).astype(BF16), table, preferred_element_type=F32)
    there = new[:, 2 * hd :] > 0.5
    for part in (0, 1):
        lanes = slice(part * hd, (part + 1) * hd)
        new_ref[0, 0, :, lanes] = jnp.where(there, new[:, lanes], store_ref[0, 0, :, lanes].astype(F32)).astype(BF16)


def whole(shape=None):
    return pl.BlockSpec(memory_space=pltpu.VMEM)


def shards(
    hidden, norm_gain, q_weight, q_bias, kv_weight, kv_bias, out_weight, kv_store, stretch_place, req_stretches, rec_rows
):
    owners = lax.axis_size("cache")
    me = lax.axis_index("cache")
    rows, width = hidden.shape
    stretches, _, length, kv_width = kv_store.shape
    hd = kv_width // 2
    per = rec_rows.shape[2]
    depth, q_cols = q_weight.shape
    heads = q_cols // hd
    vmem = pl.BlockSpec(memory_space=pltpu.VMEM)
    smem = pl.BlockSpec(memory_space=pltpu.SMEM)
    hbm = pl.BlockSpec(memory_space=pl.ANY)
    dma = pltpu.SemaphoreType.DMA

    places = stretch_place[req_stretches]
    owner_of = places // stretches
    earlier = jnp.arange(stretches)[None, :] < jnp.arange(stretches)[:, None]
    rank_of = jnp.sum((owner_of[:, :, None] == owner_of[:, None, :]) & earlier[None], axis=2).astype(jnp.int32)
    pair_of = owner_of * 2 + rank_of
    my_pair = lax.dynamic_index_in_dim(pair_of, me, 0, keepdims=False)
    order = jnp.arange(stretches, dtype=jnp.int32)
    slot_r = jnp.sum((my_pair[None, :] == jnp.arange(2 * owners)[:, None]) * order[None, :], axis=1).astype(jnp.int32)
    flat_places = places.reshape(-1)
    mine = flat_places[None, :] == (me * stretches + order)[:, None]
    source = jnp.arange(owners)[:, None] * 2 + rank_of
    pick = jnp.sum(mine * source.reshape(1, -1), axis=1).astype(jnp.int32)
    slot_rows = jnp.sum(mine[:, :, None] * rec_rows.reshape(1, -1, per), axis=1).astype(jnp.int32)
    slot_rows = jnp.pad(slot_rows, ((0, 0), (0, PAD - per)), constant_values=-1)
    my_rows = lax.dynamic_index_in_dim(rec_rows, me, 0, keepdims=False)
    pad_rows = jnp.pad(my_rows, ((0, 0), (0, PAD - per)), constant_values=-1)
    row_pos = jnp.broadcast_to(my_rows[:, None, :], (stretches, heads, per)).reshape(rows * heads, 1)

    store = kv_store.reshape(stretches, owners, 2, length // (2 * owners), kv_width)
    piece = length // (2 * owners)

    queries, fresh, blocks = pl.pallas_call(
        gather_project,
        out_shape=(
            jax.ShapeDtypeStruct((rows * heads, hd), BF16),
            jax.ShapeDtypeStruct((2, stretches * PAD, hd), BF16),
            jax.ShapeDtypeStruct((stretches, owners, 2, piece, kv_width), BF16),
        ),
        in_specs=[smem, hbm, vmem, hbm, hbm, vmem, vmem, hbm],
        out_specs=(vmem, vmem, hbm),
        scratch_shapes=[
            pltpu.VMEM((rows, width), BF16),
            pltpu.VMEM((owners, rows, depth), BF16),
            pltpu.VMEM((SIDE, SIDE, rows, depth), BF16),
            pltpu.VMEM((SIDE, depth, q_cols + hd), BF16),
            pltpu.VMEM((SIDE, rows, q_cols + hd), F32),
            pltpu.VMEM((SIDE, rows, q_cols + hd), BF16),
            pltpu.VMEM((SIDE, rows, q_cols + hd), BF16),
            pltpu.VMEM((owners * stretches, piece, kv_width), BF16),
            pltpu.VMEM((owners, stretches, piece, kv_width), BF16),
            pltpu.VMEM((rows * heads, hd), F32),
            pltpu.VMEM((stretches * PAD, hd), F32),
            dma((5 + SIDE,)),
            dma((SIDE,)),
            dma((SIDE,)),
            dma((SIDE, 2)),
            dma((SIDE, 2)),
            dma((SIDE, 2)),
            dma((SIDE, 2)),
            dma((SIDE,)),
            dma((SIDE,)),
            dma((owners,)),
            dma((owners,)),
            dma((owners,)),
            dma((owners,)),
            dma((2,)),
            dma((2,)),
        ],
        compiler_params=pltpu.CompilerParams(collective_id=0, has_side_effects=True, vmem_limit_bytes=48 << 20),
        name="gather_project",
    )(
        flat_places, hidden, norm_gain.reshape(1, -1), q_weight, kv_weight,
        q_bias.reshape(1, -1), kv_bias.reshape(1, -1), store,
    )
    blocks = blocks.reshape(stretches, length, kv_width)

    context = pl.pallas_call(
        attend,
        out_shape=jax.ShapeDtypeStruct((rows, q_cols), BF16),
        in_specs=[vmem] * 5,
        out_specs=vmem,
        scratch_shapes=[
            pltpu.VMEM((stretches, length, hd), BF16),
            pltpu.VMEM((stretches, length, hd), BF16),
            pltpu.VMEM((stretches, rows * heads, length), F32),
            pltpu.VMEM((rows * heads, hd), F32),
            pltpu.VMEM((rows * heads, hd), F32),
            pltpu.VMEM((rows * heads, hd), F32),
            pltpu.VMEM((rows, q_cols), F32),
        ],
        compiler_params=pltpu.CompilerParams(vmem_limit_bytes=48 << 20),
        name="attend",
    )(queries, fresh, blocks, pad_rows, row_pos)

    ring = 8
    attn_out, back = pl.pallas_call(
        project_out,
        out_shape=(
            jax.ShapeDtypeStruct((rows, q_cols), BF16),
            jax.ShapeDtypeStruct((2, stretches, PAD, hd), BF16),
        ),
        in_specs=[smem, smem, vmem, vmem, vmem],
        out_specs=(vmem, vmem),
        scratch_shapes=[
            pltpu.VMEM((owners, rows, q_cols), BF16),
            pltpu.VMEM((ring, rows, q_cols), BF16),
            pltpu.VMEM((ring, rows, q_cols), BF16),
            pltpu.VMEM((ring, rows, q_cols), BF16),
            pltpu.VMEM((4, rows, q_cols), BF16),
            pltpu.VMEM((4, rows, q_cols), BF16),
            pltpu.VMEM((4, rows, q_cols), BF16),
            pltpu.VMEM((4, rows, q_cols), BF16),
            pltpu.VMEM((2 * owners, PAD, hd), BF16),
            pltpu.VMEM((2 * owners, PAD, hd), BF16),
            pltpu.VMEM((rows, q_cols), BF16),
            dma((60,)),
            dma((owners, 4)),
            dma((ring,)),
            dma((ring,)),
            dma((4, 2)),
            dma((4, 2)),
            dma((4, 2)),
            dma((4, 2)),
            dma((owners,)),
            dma((owners,)),
            dma((2,)),
            dma((2,)),
        ],
        compiler_params=pltpu.CompilerParams(collective_id=1, has_side_effects=True, vmem_limit_bytes=48 << 20),
        name="project_out",
    )(slot_r, pick, context, out_weight, fresh.reshape(2, stretches, PAD, hd))

    new_store = pl.pallas_call(
        write_back,
        grid=(stretches,),
        out_shape=jax.ShapeDtypeStruct(kv_store.shape, BF16),
        in_specs=[
            pl.BlockSpec((1, 1, length, kv_width), lambda s: (s, 0, 0, 0)),
            pl.BlockSpec((2, 1, PAD, hd), lambda s: (0, s, 0, 0)),
            pl.BlockSpec((1, 1, PAD), lambda s: (s, 0, 0)),
        ],
        out_specs=pl.BlockSpec((1, 1, length, kv_width), lambda s: (s, 0, 0, 0)),
        name="write_back",
    )(kv_store, back, slot_rows.reshape(stretches, 1, PAD))
    return (attn_out, new_store)


def solution(mesh):
    placed = (
        P("cache", None),
        P(),
        P("cache", "heads"),
        P("heads"),
        P("cache", None),
        P(),
        P("heads", "cache"),
        P("cache", "heads", None, None),
        P(),
        P(),
        P(),
    )
    return jax.shard_map(
        shards,
        mesh=mesh,
        in_specs=placed,
        out_specs=(P("cache", "heads"), P("cache", "heads", None, None)),
        check_vma=False,
    )
```

```python
import functools
import math

import jax
import jax.numpy as jnp
from jax import lax
from jax.experimental import pallas as pl
from jax.experimental.pallas import tpu as pltpu
from jax.sharding import PartitionSpec as P

MESH = pl.DeviceIdType.MESH
SIDE = 4
BF16 = jnp.bfloat16
F32 = jnp.float32
RIGHT, OPPOSITE, LEFT = 1, 2, 3
PAD = 32


def remote(src, dst, send_sem, recv_sem, device):
    return pltpu.make_async_remote_copy(
        src_ref=src, dst_ref=dst, send_sem=send_sem, recv_sem=recv_sem, device_id=device, device_id_type=MESH
    )


def blend(old, keys, values, rows):
    hd = keys.shape[1]
    hit = lax.broadcasted_iota(jnp.int32, (old.shape[0], PAD), 0) == rows
    table = jnp.concatenate([keys, values, jnp.ones((PAD, hd), BF16)], axis=1)
    new = jnp.dot(hit.astype(F32).astype(BF16), table, preferred_element_type=F32)
    there = new[:, 2 * hd :] > 0.5
    parts = [
        jnp.where(there, new[:, i * hd : (i + 1) * hd], old[:, i * hd : (i + 1) * hd].astype(F32)).astype(BF16)
        for i in (0, 1)
    ]
    return parts[0], parts[1]


def attend(q_ref, fresh_ref, blocks_ref, row_ref, pos_ref, ctx_ref, ks, vs, sc, top, low, out, flat):
    stretches, length = ks.shape[0], ks.shape[1]
    hd = q_ref.shape[1]
    total = q_ref.shape[0]
    group = total // stretches
    heads = ctx_ref.shape[1] // hd
    per = group // heads
    scale = math.log2(math.e) / math.sqrt(hd)
    for r in range(stretches):
        old = blocks_ref[r].reshape(length, 2 * hd)
        ks[r], vs[r] = blend(old, fresh_ref[0, r], fresh_ref[1, r], row_ref[r : r + 1, :])
    top[...] = jnp.full_like(top, -jnp.inf)
    low[...] = jnp.zeros_like(low)
    out[...] = jnp.zeros_like(out)

    def fold(a, op):
        parts = [a[:, i * hd : (i + 1) * hd] for i in range(length // hd)]
        while len(parts) > 1:
            parts = [op(parts[i], parts[i + 1]) for i in range(0, len(parts), 2)]
        return parts[0]

    base = [sum(total - t * group for t in range(s)) for s in range(stretches)]
    for s in range(stretches):
        scores = lax.dot_general(
            q_ref[s * group :, :], ks[s], (((1,), (1,)), ((), ())), preferred_element_type=F32
        )
        key = lax.broadcasted_iota(jnp.int32, (group, length), 1)
        first = jnp.where(key <= pos_ref[s * group : (s + 1) * group, :], scores[:group], -jnp.inf)
        sc[base[s] : base[s] + group, :] = first
        top[s * group : (s + 1) * group, :] = jnp.maximum(
            top[s * group : (s + 1) * group, :], fold(first, jnp.maximum)
        )
        if s + 1 < stretches:
            sc[base[s] + group : base[s] + total - s * group, :] = scores[group:]
            top[(s + 1) * group :, :] = jnp.maximum(top[(s + 1) * group :, :], fold(scores[group:], jnp.maximum))
    top[...] = jnp.broadcast_to(jnp.max(top[...], axis=1, keepdims=True), top.shape)
    for s in range(stretches):
        here = slice(s * group, total)
        held = slice(base[s], base[s] + total - s * group)
        peak = top[here, :]
        expon = jnp.concatenate(
            [jnp.exp2((sc[held, i * hd : (i + 1) * hd] - peak) * scale) for i in range(length // hd)], axis=1
        )
        low[here, :] += fold(expon, jnp.add)
        out[here, :] += jnp.dot(expon.astype(BF16), vs[s], preferred_element_type=F32)
    out[...] = out[...] / jnp.sum(low[...], axis=1, keepdims=True)
    for r in range(stretches):
        for j in range(heads):
            at_row = (r * heads + j) * per
            flat[r * per : (r + 1) * per, j * hd : (j + 1) * hd] = out[at_row : at_row + per, :]
    ctx_ref[...] = flat[...].astype(BF16)


def prefill(
    place_ref, slot_ref, pick_ref, hid_hbm, gain_ref, qw_hbm, kvw_hbm, qb_ref, kvb_ref, ow_hbm, store_hbm,
    row_ref, pos_ref, slot_row_ref,
    out_ref, new_hbm,
    hid, acts, w, acc, part, sums, hop_in, hop_out, qs, fpad,
    queries, own_fresh, fresh, blocks, ks, vs, sc, top, low, res, flat, ctx,
    ow, ctxs, chunk, r_out, l_out, r_in, l_in, done, f_out, f_in, back, old, new,
    loc, w_send, w_recv, a_send, a_recv, c_send, c_recv, s_send, s_recv,
    h1_send, h1_recv, h2_send, h2_recv, x_send, x_recv,
    o_send, o_recv, oo_send, oo_recv, t_send, t_recv,
    r_send, r_recv, l_send, l_recv, f_send, f_recv, n_sem,
):
    me = lax.axis_index("cache")
    head = lax.axis_index("heads")
    core = lax.rem(head, 2)
    partner = (me, head + 1 - 2 * core)
    x, y = me // SIDE, lax.rem(me, SIDE)
    z = head // 2
    owners = SIDE * SIDE
    levels = lax.axis_size("heads") // 2
    right = (me, lax.rem(z + 1, levels) * 2 + core)
    left = (me, lax.rem(z + levels - 1, levels) * 2 + core)
    turn = lax.rem(head, SIDE)
    mirror = (x * SIDE + turn, head - turn + y)
    rows = hid.shape[0]
    depth, width = w.shape[1], w.shape[2]
    q_cols = qw_hbm.shape[1]
    hd = width - q_cols

    def ring(i, d):
        return lax.rem(i + d, SIDE)

    own_hid = pltpu.make_async_copy(hid_hbm, hid, loc.at[2])
    own_q = pltpu.make_async_copy(qw_hbm, w.at[x, :, 0:q_cols], loc.at[0])
    own_kv = pltpu.make_async_copy(
        kvw_hbm.at[:, pl.ds(pl.multiple_of(head * hd, hd), hd)], w.at[x, :, q_cols:width], loc.at[1]
    )
    own_hop = pltpu.make_async_copy(store_hbm.at[:, me, core], hop_in.at[pl.ds(me * 8, 8)], loc.at[3])
    own_hid.start()
    own_q.start()
    own_kv.start()
    own_hop.start()
    own_ow = pltpu.make_async_copy(ow_hbm, ow.at[core, x], loc.at[5 + SIDE])
    own_ow.start()
    old_in = pltpu.make_async_copy(store_hbm, old, loc.at[6 + SIDE])
    old_in.start()

    barrier = pltpu.get_barrier_semaphore()

    @pl.loop(1, owners)
    def _(o):
        pl.semaphore_signal(barrier, inc=1, device_id=(lax.rem(me + o, owners), head), device_id_type=MESH)

    for peer in (partner, left, right):
        pl.semaphore_signal(barrier, inc=1, device_id=peer, device_id_type=MESH)
    for d in (RIGHT, OPPOSITE, LEFT):
        across = (x * SIDE + ring(y, d), head + 1 - 2 * core)
        pl.semaphore_signal(barrier, inc=1, device_id=across, device_id_type=MESH)

    @pl.when(turn != y)
    def _():
        pl.semaphore_signal(barrier, inc=1, device_id=mirror, device_id_type=MESH)

    @pl.when(turn != y)
    def _():
        pl.semaphore_wait(barrier, owners + 6)

    @pl.when(turn == y)
    def _():
        pl.semaphore_wait(barrier, owners + 5)

    def slice_of(c):
        return hid.at[:, pl.ds(pl.multiple_of(c * depth, depth), depth)]

    def rows_to(d, i):
        to = ring(y, d)
        return remote(
            slice_of((2 * core + i) * SIDE + to), acts.at[2 * core + i, y], a_send.at[d, i], a_recv.at[d, i],
            (x * SIDE + to, head),
        )

    def hop1(o):
        to = lax.rem(me + o, owners)
        return remote(
            store_hbm.at[:, to, core], hop_in.at[pl.ds(me * 8, 8)], h1_send.at[o], h1_recv.at[me], (to, head)
        )

    def hop1_from(o):
        src = lax.rem(me + owners - o, owners)
        return remote(
            store_hbm.at[:, src, core], hop_in.at[pl.ds(src * 8, 8)], h1_send.at[o], h1_recv.at[src], (src, head)
        )

    def hop2(o):
        to = lax.rem(me + o, owners)
        return remote(hop_out.at[to], blocks.at[:, me, core], h2_send.at[o], h2_recv.at[me], (to, head))

    def hop2_from(o):
        src = lax.rem(me + owners - o, owners)
        return remote(hop_out.at[src], blocks.at[:, src, core], h2_send.at[o], h2_recv.at[src], (src, head))

    def weights_to(d):
        to = ring(x, d)
        return remote(w.at[x], w.at[x], w_send.at[d], w_recv.at[d], (to * SIDE + y, head))

    def weights_from(d):
        src = ring(x, SIDE - d)
        return remote(w.at[src], w.at[src], w_send.at[d], w_recv.at[d], (src * SIDE + y, head))

    steps = (RIGHT, LEFT, OPPOSITE)
    own_q.wait()
    own_kv.wait()
    for d in steps:
        weights_to(d).start()

    @pl.loop(1, owners)
    def _(o):
        hop1(o).start()

    own_hid.wait()
    tall = 16

    @pl.loop(0, rows // tall)
    def _(i):
        lines = pl.ds(pl.multiple_of(i * tall, tall), tall)
        total = jnp.zeros((tall, 1), F32)
        for c in range(owners):
            v = hid[lines, c * depth : (c + 1) * depth].astype(F32)
            total += jnp.sum(v * v, axis=-1, keepdims=True)
        factor = lax.rsqrt(total / (owners * depth) + 1e-06)
        for c in range(owners):
            v = hid[lines, c * depth : (c + 1) * depth].astype(F32)
            g = gain_ref[:, c * depth : (c + 1) * depth].astype(F32)
            hid[lines, c * depth : (c + 1) * depth] = (v * factor * g).astype(BF16)

    for i in (0, 1):
        for d in steps:
            rows_to(d, i).start()

    for i in range(SIDE):
        pltpu.make_async_copy(slice_of(i * SIDE + y), acts.at[i, y], loc.at[5 + i]).start()

    def rows_from(d, i, which):
        src = ring(y, SIDE - d)
        place = acts.at[2 * which + i, src]
        return remote(place, place, a_send.at[d, i], a_recv.at[d, i], (x * SIDE + src, head))

    def rows_over(d, i, which):
        place = acts.at[2 * which + i, ring(y, SIDE - d)]
        return remote(place, place, c_send.at[d, i], c_recv.at[d, i], partner)

    for i in (0, 1):
        for d in steps:
            rows_from(d, i, core).wait_recv()
            rows_over(d, i, core).start()

    own_hop.wait()

    @pl.loop(1, owners)
    def _(o):
        hop1_from(o).wait_recv()

    @pl.loop(0, owners)
    def _(i):
        for r in range(8):
            hop_out[i, r] = hop_in[place_ref[i * 8 + r]]

    @pl.loop(1, owners)
    def _(o):
        hop2(o).start()

    own_out = pltpu.make_async_copy(hop_out.at[me], blocks.at[:, me, core], loc.at[4])
    own_out.start()

    for i in range(SIDE):
        pltpu.make_async_copy(slice_of(i * SIDE + y), acts.at[i, y], loc.at[5 + i]).wait()
    for d in steps:
        weights_from(d).wait_recv()

    def product(i, j):
        return jnp.dot(acts[i, j], w[i], preferred_element_type=F32)

    @pl.loop(0, SIDE)
    def _(j):
        acc[j] = product(2 * core, j)
        acc[j] += product(2 * core + 1, j)

    for i in (0, 1):
        for d in steps:
            rows_over(d, i, 1 - core).wait_recv()

    def sums_to(d):
        to = ring(y, d)
        return remote(part.at[d], sums.at[d], s_send.at[d], s_recv.at[d], (x * SIDE + to, head))

    for d in (OPPOSITE, RIGHT, LEFT):
        j = ring(y, d)
        acc[j] += product(2 - 2 * core, j)
        part[d] = (acc[j] + product(3 - 2 * core, j)).astype(BF16)
        sums_to(d).start()

    def block_to(d):
        to = ring(x, d)
        return remote(ow_hbm, ow.at[core, x], o_send.at[d], o_recv.at[d], (to * SIDE + y, head))

    def block_from(d, which):
        place = ow.at[which, ring(x, SIDE - d)]
        return remote(place, place, oo_send.at[d], oo_recv.at[d], partner)

    for d in steps:
        block_to(d).start()
    own_ow.wait()
    block_from(0, core).start()
    acc[y] += product(2 - 2 * core, y)
    acc[y] += product(3 - 2 * core, y)

    def core_swap(which):
        return remote(
            blocks.at[:, :, which], blocks.at[:, :, which], x_send.at[0], x_recv.at[0], partner
        )

    own_out.wait()

    @pl.loop(1, owners)
    def _(o):
        hop2_from(o).wait_recv()

    core_swap(core).start()

    for d in steps:
        remote(part.at[d], sums.at[d], s_send.at[d], s_recv.at[d], (x * SIDE + ring(y, SIDE - d), head)).wait_recv()
        acc[y] += sums[d].astype(F32)

    per = rows // 8
    heads = q_cols // hd
    bias = qb_ref[...].astype(F32)
    kv_bias = kvb_ref[:, pl.ds(pl.multiple_of(head * hd, hd), hd)].astype(F32)
    for r in range(8):
        lines = slice(per * r, per * (r + 1))
        for j in range(heads):
            at_row = (r * heads + j) * per
            qs[at_row : at_row + per, :] = acc[y, lines, j * hd : (j + 1) * hd] + bias[:, j * hd : (j + 1) * hd]
        fpad[r * PAD : r * PAD + per, :] = acc[y, lines, q_cols:width] + kv_bias
        fpad[r * PAD + per : (r + 1) * PAD, :] = jnp.zeros((PAD - per, hd), F32)
    own_fresh[...] = fpad[...].astype(BF16).reshape(own_fresh.shape)
    fresh[core] = own_fresh[...]
    swap = remote(own_fresh, fresh.at[core], x_send.at[1], x_recv.at[1], partner)
    swap.start()
    queries[...] = qs[...].astype(BF16)

    @pl.loop(0, owners)
    def _(o):
        for m in range(2):
            f_out[2 * o + m] = own_fresh[slot_ref[2 * o + m]]

    def give(o):
        to = lax.rem(me + o, owners)
        return remote(
            f_out.at[pl.ds(2 * to, 2)], f_in.at[pl.ds(2 * me, 2)], f_send.at[o], f_recv.at[me], (to, head)
        )

    def take(o):
        src = lax.rem(me + owners - o, owners)
        return remote(
            f_out.at[pl.ds(2 * src, 2)], f_in.at[pl.ds(2 * src, 2)], f_send.at[o], f_recv.at[src], (src, head)
        )

    @pl.loop(1, owners)
    def _(o):
        give(o).start()

    for m in range(2):
        f_in[2 * me + m] = f_out[2 * me + m]

    core_swap(1 - core).wait_recv()
    remote(fresh.at[1 - core], fresh.at[1 - core], x_send.at[1], x_recv.at[1], partner).wait_recv()

    attend(queries, fresh, blocks, row_ref, pos_ref, ctx, ks, vs, sc, top, low, res, flat)

    def ctx_to(d):
        to = ring(y, d)
        return remote(
            ctx, ctxs.at[y // 2, core], t_send.at[d], t_recv.at[d, core], (x * SIDE + to, 2 * z + lax.rem(y, 2))
        )

    def ctx_from(d, which):
        src = ring(y, SIDE - d)
        place = ctxs.at[src // 2, which]
        return remote(place, place, t_send.at[d], t_recv.at[d, which], (x * SIDE + src, 2 * z + which))

    for d in (RIGHT, LEFT, OPPOSITE):
        ctx_to(d).start()

    mine = lax.rem(y, 2) == core

    @pl.when(mine)
    def _():
        ctxs[y // 2, core] = ctx[...]

    @pl.when(jnp.logical_not(mine))
    def _():
        ctx_to(0).start()

    for d in steps:
        place = ow.at[core, ring(x, SIDE - d)]
        remote(place, place, o_send.at[d], o_recv.at[d], (ring(x, SIDE - d) * SIDE + y, head)).wait_recv()
        block_from(d, core).start()

    @pl.loop(1, owners)
    def _(o):
        take(o).wait_recv()

    for s in range(8):
        back[core, s] = f_in[pick_ref[s]]
    swap_back = remote(back.at[core], back.at[core], x_send.at[2], x_recv.at[2], partner)
    swap_back.start()

    @pl.when(mine)
    def _():
        ctx_from(0, 1 - core).wait_recv()
        for which in (0, 1):
            ctx_from(OPPOSITE, which).wait_recv()

    @pl.when(jnp.logical_not(mine))
    def _():
        for d in (RIGHT, LEFT):
            for which in (0, 1):
                ctx_from(d, which).wait_recv()

    for d in (0,) + steps:
        block_from(d, 1 - core).wait_recv()

    hrow = rows // 2
    order = (4, 3, -3, 2, -2, 1, -1, 0)

    def compute(n):
        target = lax.rem(z + order[n] + levels, levels)
        column, request = target // 2, lax.rem(target, 2)
        chunk[n] = jnp.dot(ctxs[request, 0], ow[0, column], preferred_element_type=F32)
        chunk[n] += jnp.dot(ctxs[request, 1], ow[1, column], preferred_element_type=F32)

    def lines_of(half):
        return slice(half * hrow, (half + 1) * hrow)

    def ring_copy(step, half, out, into, send_sem, recv_sem, to):
        return remote(
            out.at[step, pl.ds(half * hrow, hrow)],
            into.at[step, pl.ds(half * hrow, hrow)],
            send_sem.at[step, half],
            recv_sem.at[step, half],
            to,
        )

    def rightward(step, half):
        return ring_copy(step, half, r_out, r_in, r_send, r_recv, right)

    def leftward(step, half):
        return ring_copy(step, half, l_out, l_in, l_send, l_recv, left)

    compute(0)
    r_out[0, lines_of(0), :] = chunk[0, lines_of(0), :].astype(BF16)
    rightward(0, 0).start()
    l_out[0, lines_of(1), :] = chunk[0, lines_of(1), :].astype(BF16)
    leftward(0, 1).start()
    compute(1)
    compute(2)
    for step in (1, 2, 3):
        n_right, n_left = 2 * step - 1, 2 * step
        halves = ((1, 0), (0, 1)) if step == 1 else ((0, 1), (1, 0))
        for right_half, left_half in halves:
            value = chunk[n_right, lines_of(right_half), :]
            if step > 1 or right_half == 0:
                rightward(step - 1, right_half).wait_recv()
                value += r_in[step - 1, lines_of(right_half), :].astype(F32)
            r_out[step, lines_of(right_half), :] = value.astype(BF16)
            rightward(step, right_half).start()
            value = chunk[n_left, lines_of(left_half), :]
            if step > 1 or left_half == 1:
                leftward(step - 1, left_half).wait_recv()
                value += l_in[step - 1, lines_of(left_half), :].astype(F32)
            l_out[step, lines_of(left_half), :] = value.astype(BF16)
            leftward(step, left_half).start()
        if step < 3:
            compute(2 * step + 1)
            compute(2 * step + 2)
        else:
            compute(7)

    remote(back.at[1 - core], back.at[1 - core], x_send.at[2], x_recv.at[2], partner).wait_recv()
    old_in.wait()
    for s in range(8):
        keys, values = blend(old[s].reshape(new.shape[1], 2 * hd), back[0, s], back[1, s], slot_row_ref[s : s + 1, :])
        new[s, :, 0:hd] = keys
        new[s, :, hd : 2 * hd] = values
    new_out = pltpu.make_async_copy(new, new_hbm, n_sem.at[0])
    new_out.start()

    def flip(half):
        return remote(
            done.at[pl.ds(half * hrow, hrow)], out_ref.at[pl.ds(half * hrow, hrow)],
            x_send.at[3 + half], x_recv.at[3 + half], mirror,
        )

    for half in (0, 1):
        rightward(3, half).wait_recv()
        leftward(3, half).wait_recv()
        value = chunk[7, lines_of(half), :] + r_in[3, lines_of(half), :].astype(F32)
        value += l_in[3, lines_of(half), :].astype(F32)
        done[lines_of(half), :] = value.astype(BF16)

        @pl.when(turn != y)
        def _():
            flip(half).start()

    @pl.when(turn == y)
    def _():
        out_ref[...] = done[...]

    for i in (0, 1):
        for d in steps:
            rows_to(d, i).wait_send()
            rows_over(d, i, core).wait_send()
    for d in steps:
        weights_to(d).wait_send()
        sums_to(d).wait_send()
        block_to(d).wait_send()
        ctx_to(d).wait_send()
    for d in (0,) + steps:
        block_from(d, core).wait_send()

    @pl.when(jnp.logical_not(mine))
    def _():
        ctx_to(0).wait_send()

    @pl.loop(1, owners)
    def _(o):
        hop1(o).wait_send()
        hop2(o).wait_send()
        give(o).wait_send()

    core_swap(core).wait_send()
    swap.wait_send()
    swap_back.wait_send()
    rightward(0, 0).wait_send()
    leftward(0, 1).wait_send()
    for step in (1, 2, 3):
        for half in (0, 1):
            rightward(step, half).wait_send()
            leftward(step, half).wait_send()
    new_out.wait()

    @pl.when(turn != y)
    def _():
        for half in (0, 1):
            flip(half).wait()


def shards(
    hidden, norm_gain, q_weight, q_bias, kv_weight, kv_bias, out_weight, kv_store, stretch_place, req_stretches, rec_rows
):
    owners = lax.axis_size("cache")
    me = lax.axis_index("cache")
    rows, width = hidden.shape
    stretches, _, length, kv_width = kv_store.shape
    hd = kv_width // 2
    per = rec_rows.shape[2]
    depth, q_cols = q_weight.shape
    levels = lax.axis_size("heads") // 2
    heads = q_cols // hd
    vmem = pl.BlockSpec(memory_space=pltpu.VMEM)
    smem = pl.BlockSpec(memory_space=pltpu.SMEM)
    hbm = pl.BlockSpec(memory_space=pl.ANY)
    dma = pltpu.SemaphoreType.DMA

    places = stretch_place[req_stretches]
    owner_of = places // stretches
    earlier = jnp.arange(stretches)[None, :] < jnp.arange(stretches)[:, None]
    rank_of = jnp.sum((owner_of[:, :, None] == owner_of[:, None, :]) & earlier[None], axis=2).astype(jnp.int32)
    pair_of = owner_of * 2 + rank_of
    my_pair = lax.dynamic_index_in_dim(pair_of, me, 0, keepdims=False)
    order = jnp.arange(stretches, dtype=jnp.int32)
    slot_r = jnp.sum((my_pair[None, :] == jnp.arange(2 * owners)[:, None]) * order[None, :], axis=1).astype(jnp.int32)
    flat_places = places.reshape(-1)
    mine = flat_places[None, :] == (me * stretches + order)[:, None]
    source = jnp.arange(owners)[:, None] * 2 + rank_of
    pick = jnp.sum(mine * source.reshape(1, -1), axis=1).astype(jnp.int32)
    slot_rows = jnp.sum(mine[:, :, None] * rec_rows.reshape(1, -1, per), axis=1).astype(jnp.int32)
    slot_rows = jnp.pad(slot_rows, ((0, 0), (0, PAD - per)), constant_values=-1)
    my_rows = lax.dynamic_index_in_dim(rec_rows, me, 0, keepdims=False)
    pad_rows = jnp.pad(my_rows, ((0, 0), (0, PAD - per)), constant_values=-1)
    row_pos = jnp.broadcast_to(my_rows[:, None, :], (stretches, heads, per)).reshape(rows * heads, 1)

    store = kv_store.reshape(stretches, owners, 2, length // (2 * owners), kv_width)
    piece = length // (2 * owners)

    attn_out, new_store = pl.pallas_call(
        prefill,
        out_shape=(
            jax.ShapeDtypeStruct((rows, q_cols), BF16),
            jax.ShapeDtypeStruct((stretches, length, kv_width), BF16),
        ),
        in_specs=[smem, smem, smem, hbm, vmem, hbm, hbm, vmem, vmem, hbm, hbm, vmem, vmem, vmem],
        out_specs=(vmem, hbm),
        scratch_shapes=[
            pltpu.VMEM((rows, width), BF16),
            pltpu.VMEM((SIDE, SIDE, rows, depth), BF16),
            pltpu.VMEM((SIDE, depth, q_cols + hd), BF16),
            pltpu.VMEM((SIDE, rows, q_cols + hd), F32),
            pltpu.VMEM((SIDE, rows, q_cols + hd), BF16),
            pltpu.VMEM((SIDE, rows, q_cols + hd), BF16),
            pltpu.VMEM((owners * stretches, piece, kv_width), BF16),
            pltpu.VMEM((owners, stretches, piece, kv_width), BF16),
            pltpu.VMEM((rows * heads, hd), F32),
            pltpu.VMEM((stretches * PAD, hd), F32),
            pltpu.VMEM((rows * heads, hd), BF16),
            pltpu.VMEM((stretches, PAD, hd), BF16),
            pltpu.VMEM((2, stretches, PAD, hd), BF16),
            pltpu.VMEM((stretches, owners, 2, piece, kv_width), BF16),
            pltpu.VMEM((stretches, length, hd), BF16),
            pltpu.VMEM((stretches, length, hd), BF16),
            pltpu.VMEM((rows * heads * (stretches + 1) // 2, length), F32),
            pltpu.VMEM((rows * heads, hd), F32),
            pltpu.VMEM((rows * heads, hd), F32),
            pltpu.VMEM((rows * heads, hd), F32),
            pltpu.VMEM((rows, q_cols), F32),
            pltpu.VMEM((rows, q_cols), BF16),
            pltpu.VMEM((2, SIDE, depth, q_cols), BF16),
            pltpu.VMEM((2, 2, rows, q_cols), BF16),
            pltpu.VMEM((levels, rows, q_cols), F32),
            pltpu.VMEM((4, rows, q_cols), BF16),
            pltpu.VMEM((4, rows, q_cols), BF16),
            pltpu.VMEM((4, rows, q_cols), BF16),
            pltpu.VMEM((4, rows, q_cols), BF16),
            pltpu.VMEM((rows, q_cols), BF16),
            pltpu.VMEM((2 * owners, PAD, hd), BF16),
            pltpu.VMEM((2 * owners, PAD, hd), BF16),
            pltpu.VMEM((2, stretches, PAD, hd), BF16),
            pltpu.VMEM((stretches, owners, 2, piece, kv_width), BF16),
            pltpu.VMEM((stretches, length, kv_width), BF16),
            dma((7 + SIDE,)),
            dma((SIDE,)),
            dma((SIDE,)),
            dma((SIDE, 2)),
            dma((SIDE, 2)),
            dma((SIDE, 2)),
            dma((SIDE, 2)),
            dma((SIDE,)),
            dma((SIDE,)),
            dma((owners,)),
            dma((owners,)),
            dma((owners,)),
            dma((owners,)),
            dma((5,)),
            dma((5,)),
            dma((SIDE,)),
            dma((SIDE,)),
            dma((SIDE,)),
            dma((SIDE,)),
            dma((SIDE,)),
            dma((SIDE, 2)),
            dma((4, 2)),
            dma((4, 2)),
            dma((4, 2)),
            dma((4, 2)),
            dma((owners,)),
            dma((owners,)),
            dma((1,)),
        ],
        compiler_params=pltpu.CompilerParams(collective_id=0, has_side_effects=True, vmem_limit_bytes=58 << 20),
        name="prefill",
    )(
        flat_places, slot_r, pick, hidden, norm_gain.reshape(1, -1), q_weight, kv_weight,
        q_bias.reshape(1, -1), kv_bias.reshape(1, -1), out_weight, store, pad_rows, row_pos, slot_rows,
    )
    return (attn_out, new_store.reshape(kv_store.shape))


def solution(mesh):
    placed = (
        P("cache", None),
        P(),
        P("cache", "heads"),
        P("heads"),
        P("cache", None),
        P(),
        P("heads", "cache"),
        P("cache", "heads", None, None),
        P(),
        P(),
        P(),
    )
    return jax.shard_map(
        shards,
        mesh=mesh,
        in_specs=placed,
        out_specs=(P("cache", "heads"), P("cache", "heads", None, None)),
        check_vma=False,
    )
```

```python
import functools
import math

import jax
import jax.numpy as jnp
from jax import lax
from jax.experimental import pallas as pl
from jax.experimental.pallas import tpu as pltpu
from jax.sharding import PartitionSpec as P

MESH = pl.DeviceIdType.MESH
SIDE = 4
BF16 = jnp.bfloat16
F32 = jnp.float32
RIGHT, OPPOSITE, LEFT = 1, 2, 3
PAD = 32


def remote(src, dst, send_sem, recv_sem, device):
    return pltpu.make_async_remote_copy(
        src_ref=src, dst_ref=dst, send_sem=send_sem, recv_sem=recv_sem, device_id=device, device_id_type=MESH
    )


def blend(old, keys, values, rows):
    hd = keys.shape[1]
    hit = lax.broadcasted_iota(jnp.int32, (old.shape[0], PAD), 0) == rows
    table = jnp.concatenate([keys, values, jnp.ones((PAD, hd), BF16)], axis=1)
    new = jnp.dot(hit.astype(F32).astype(BF16), table, preferred_element_type=F32)
    there = new[:, 2 * hd :] > 0.5
    parts = [
        jnp.where(there, new[:, i * hd : (i + 1) * hd], old[:, i * hd : (i + 1) * hd].astype(F32)).astype(BF16)
        for i in (0, 1)
    ]
    return parts[0], parts[1]


def attend(q_ref, fresh_ref, blocks_ref, row_ref, ctx_ref, ks, vs, sc, top, low, out, flat):
    stretches, length = ks.shape[0], ks.shape[1]
    hd = q_ref.shape[1]
    total = q_ref.shape[0]
    group = total // stretches
    heads = ctx_ref.shape[1] // hd
    per = group // heads
    scale = math.log2(math.e) / math.sqrt(hd)
    for r in range(stretches):
        old = blocks_ref[r].reshape(length, 2 * hd)
        ks[r], vs[r] = blend(old, fresh_ref[0, r], fresh_ref[1, r], row_ref[r : r + 1, 0:PAD])
    top[...] = jnp.full_like(top, -jnp.inf)
    low[...] = jnp.zeros_like(low)
    out[...] = jnp.zeros_like(out)

    def fold(a, op):
        parts = [a[:, i * hd : (i + 1) * hd] for i in range(length // hd)]
        while len(parts) > 1:
            parts = [op(parts[i], parts[i + 1]) for i in range(0, len(parts), 2)]
        return parts[0]

    columns = jnp.transpose(row_ref[...].astype(F32))
    base = [sum(total - t * group for t in range(s)) for s in range(stretches)]
    for s in range(stretches):
        scores = lax.dot_general(
            q_ref[s * group :, :], ks[s], (((1,), (1,)), ((), ())), preferred_element_type=F32
        )
        key = lax.broadcasted_iota(jnp.int32, (group, length), 1).astype(F32)
        last = jnp.concatenate([columns[0:per, s : s + 1]] * heads, axis=0)
        first = jnp.where(key <= last, scores[:group], -jnp.inf)
        sc[base[s] : base[s] + group, :] = first
        top[s * group : (s + 1) * group, :] = jnp.maximum(
            top[s * group : (s + 1) * group, :], fold(first, jnp.maximum)
        )
        if s + 1 < stretches:
            sc[base[s] + group : base[s] + total - s * group, :] = scores[group:]
            top[(s + 1) * group :, :] = jnp.maximum(top[(s + 1) * group :, :], fold(scores[group:], jnp.maximum))
    top[...] = jnp.broadcast_to(jnp.max(top[...], axis=1, keepdims=True), top.shape)
    for s in range(stretches):
        here = slice(s * group, total)
        held = slice(base[s], base[s] + total - s * group)
        peak = top[here, :]
        expon = jnp.concatenate(
            [jnp.exp2((sc[held, i * hd : (i + 1) * hd] - peak) * scale) for i in range(length // hd)], axis=1
        )
        low[here, :] += fold(expon, jnp.add)
        out[here, :] += jnp.dot(expon.astype(BF16), vs[s], preferred_element_type=F32)
    out[...] = out[...] / jnp.sum(low[...], axis=1, keepdims=True)
    for r in range(stretches):
        for j in range(heads):
            at_row = (r * heads + j) * per
            flat[r * per : (r + 1) * per, j * hd : (j + 1) * hd] = out[at_row : at_row + per, :]
    ctx_ref[...] = flat[...].astype(BF16)


def prefill(
    table_ref, req_ref, hid_hbm, gain_ref, qw_hbm, kvw_hbm, qb_ref, kvb_ref, ow_hbm, store_hbm, rec_ref,
    out_ref, new_hbm,
    hid, acts, w, acc, part, sums, hop_in, hop_out, qs, fpad, my_rows, slot_rows,
    queries, own_fresh, fresh, blocks, ks, vs, sc, top, low, res, flat, ctx,
    ow, ctxs, chunk, r_out, l_out, r_in, l_in, done, f_out, f_in, back, old, new,
    loc, w_send, w_recv, a_send, a_recv, c_send, c_recv, s_send, s_recv,
    h1_send, h1_recv, h2_send, h2_recv, x_send, x_recv,
    o_send, o_recv, oo_send, oo_recv, t_send, t_recv,
    r_send, r_recv, l_send, l_recv, f_send, f_recv, n_sem,
):
    me = lax.axis_index("cache")
    head = lax.axis_index("heads")
    core = lax.rem(head, 2)
    partner = (me, head + 1 - 2 * core)
    x, y = me // SIDE, lax.rem(me, SIDE)
    z = head // 2
    owners = SIDE * SIDE
    levels = lax.axis_size("heads") // 2
    right = (me, lax.rem(z + 1, levels) * 2 + core)
    left = (me, lax.rem(z + levels - 1, levels) * 2 + core)
    turn = lax.rem(head, SIDE)
    mirror = (x * SIDE + turn, head - turn + y)
    rows = hid.shape[0]
    depth, width = w.shape[1], w.shape[2]
    q_cols = qw_hbm.shape[1]
    hd = width - q_cols
    per = rows // 8

    def ring(i, d):
        return lax.rem(i + d, SIDE)

    own_hid = pltpu.make_async_copy(hid_hbm, hid, loc.at[2])
    own_q = pltpu.make_async_copy(qw_hbm, w.at[x, :, 0:q_cols], loc.at[0])
    own_kv = pltpu.make_async_copy(
        kvw_hbm.at[:, pl.ds(pl.multiple_of(head * hd, hd), hd)], w.at[x, :, q_cols:width], loc.at[1]
    )
    own_hop = pltpu.make_async_copy(store_hbm.at[:, me, core], hop_in.at[pl.ds(me * 8, 8)], loc.at[3])
    own_hid.start()
    own_q.start()
    own_kv.start()
    own_hop.start()
    own_ow = pltpu.make_async_copy(ow_hbm, ow.at[core, x], loc.at[5 + SIDE])
    own_ow.start()
    old_in = pltpu.make_async_copy(store_hbm, old, loc.at[6 + SIDE])
    old_in.start()

    barrier = pltpu.get_barrier_semaphore()

    @pl.loop(1, owners)
    def _(o):
        pl.semaphore_signal(barrier, inc=1, device_id=(lax.rem(me + o, owners), head), device_id_type=MESH)

    for peer in (partner, left, right):
        pl.semaphore_signal(barrier, inc=1, device_id=peer, device_id_type=MESH)
    for d in (RIGHT, OPPOSITE, LEFT):
        across = (x * SIDE + ring(y, d), head + 1 - 2 * core)
        pl.semaphore_signal(barrier, inc=1, device_id=across, device_id_type=MESH)

    @pl.when(turn != y)
    def _():
        pl.semaphore_signal(barrier, inc=1, device_id=mirror, device_id_type=MESH)

    @pl.when(turn != y)
    def _():
        pl.semaphore_wait(barrier, owners + 6)

    @pl.when(turn == y)
    def _():
        pl.semaphore_wait(barrier, owners + 5)

    def slice_of(c):
        return hid.at[:, pl.ds(pl.multiple_of(c * depth, depth), depth)]

    def rows_to(d, i):
        to = ring(y, d)
        return remote(
            slice_of((2 * core + i) * SIDE + to), acts.at[2 * core + i, y], a_send.at[d, i], a_recv.at[d, i],
            (x * SIDE + to, head),
        )

    def hop1(o):
        to = lax.rem(me + o, owners)
        return remote(
            store_hbm.at[:, to, core], hop_in.at[pl.ds(me * 8, 8)], h1_send.at[o], h1_recv.at[me], (to, head)
        )

    def hop1_from(o):
        src = lax.rem(me + owners - o, owners)
        return remote(
            store_hbm.at[:, src, core], hop_in.at[pl.ds(src * 8, 8)], h1_send.at[o], h1_recv.at[src], (src, head)
        )

    def hop2(o):
        to = lax.rem(me + o, owners)
        return remote(hop_out.at[to], blocks.at[:, me, core], h2_send.at[o], h2_recv.at[me], (to, head))

    def hop2_from(o):
        src = lax.rem(me + owners - o, owners)
        return remote(hop_out.at[src], blocks.at[:, src, core], h2_send.at[o], h2_recv.at[src], (src, head))

    class Ring4:
        def __init__(self, source, place, send_sem, recv_sem):
            self.source, self.place, self.send_sem, self.recv_sem = source, place, send_sem, recv_sem
            self.deep = place(0).shape[0] // 2

        def part(self, ref, half):
            return ref.at[pl.ds(half * self.deep, self.deep)]

        def copy(self, d, half, passed=False):
            to = (ring(x, d) * SIDE + y, head)
            src = self.part(self.place(ring(x, SIDE - d)) if passed else self.source, half)
            dst = self.part(self.place(ring(x, SIDE - d) if passed else x), half)
            k = OPPOSITE if passed else d
            return remote(src, dst, self.send_sem.at[k, half], self.recv_sem.at[k, half], to)

        def wait(self, d, half):
            place = self.part(self.place(ring(x, SIDE - d)), half)
            remote(
                place, place, self.send_sem.at[d, half], self.recv_sem.at[d, half],
                (ring(x, SIDE - d) * SIDE + y, head),
            ).wait_recv()

        def start(self):
            self.copy(RIGHT, 0).start()
            self.copy(LEFT, 1).start()

        def rest(self):
            self.copy(RIGHT, 1).start()
            self.copy(LEFT, 0).start()

        def forward(self):
            self.wait(RIGHT, 0)
            self.copy(RIGHT, 0, True).start()
            self.wait(LEFT, 1)
            self.copy(LEFT, 1, True).start()

        def wait_rest(self):
            self.wait(RIGHT, 1)
            self.wait(LEFT, 0)

        def wait_opposite(self):
            self.wait(OPPOSITE, 0)
            self.wait(OPPOSITE, 1)

        def finish(self):
            for half in (0, 1):
                self.copy(RIGHT, half).wait_send()
                self.copy(LEFT, half).wait_send()
            self.copy(RIGHT, 0, True).wait_send()
            self.copy(LEFT, 1, True).wait_send()

    weights = Ring4(w.at[x], lambda i: w.at[i], w_send, w_recv)
    ow_blocks = Ring4(ow_hbm, lambda i: ow.at[core, i], o_send, o_recv)

    steps = (RIGHT, LEFT, OPPOSITE)
    own_q.wait()
    own_kv.wait()
    weights.start()

    @pl.loop(1, owners)
    def _(o):
        hop1(o).start()

    own_hid.wait()
    tall = 16

    @pl.loop(0, rows // tall)
    def _(i):
        lines = pl.ds(pl.multiple_of(i * tall, tall), tall)
        total = jnp.zeros((tall, 1), F32)
        for c in range(owners):
            v = hid[lines, c * depth : (c + 1) * depth].astype(F32)
            total += jnp.sum(v * v, axis=-1, keepdims=True)
        factor = lax.rsqrt(total / (owners * depth) + 1e-06)
        for c in range(owners):
            v = hid[lines, c * depth : (c + 1) * depth].astype(F32)
            g = gain_ref[c * depth : (c + 1) * depth].astype(F32).reshape(1, depth)
            hid[lines, c * depth : (c + 1) * depth] = (v * factor * g).astype(BF16)

    for i in (0, 1):
        for d in steps:
            rows_to(d, i).start()
    weights.rest()

    for i in range(SIDE):
        pltpu.make_async_copy(slice_of(i * SIDE + y), acts.at[i, y], loc.at[5 + i]).start()

    def place_of(i, r):
        return table_ref[req_ref[i, r]]

    my_owner = [place_of(me, r) // 8 for r in range(8)]
    my_rank = [sum([(my_owner[q] == my_owner[r]).astype(jnp.int32) for q in range(r)], 0) for r in range(8)]

    def find(n, found):
        here = place_of(n // 8, lax.rem(n, 8)) - me * 8
        return tuple(jnp.where(here == s, n, found[s]) for s in range(8))

    found = lax.fori_loop(0, owners * 8, find, (jnp.int32(0),) * 8)
    my_rows[...] = jnp.full_like(my_rows, -1)
    slot_rows[...] = jnp.full_like(slot_rows, -1)
    my_rows[:, 0:per] = rec_ref[me]
    picks = []
    for s in range(8):
        i, r = found[s] // 8, lax.rem(found[s], 8)
        slot_rows[s : s + 1, 0:per] = rec_ref[i, pl.ds(r, 1), :]
        rank = sum([((q < r) & (place_of(i, q) // 8 == me)).astype(jnp.int32) for q in range(8)], 0)
        picks.append(2 * i + jnp.minimum(rank, 1))

    weights.forward()

    def rows_from(d, i, which):
        src = ring(y, SIDE - d)
        place = acts.at[2 * which + i, src]
        return remote(place, place, a_send.at[d, i], a_recv.at[d, i], (x * SIDE + src, head))

    def rows_over(d, i, which):
        place = acts.at[2 * which + i, ring(y, SIDE - d)]
        return remote(place, place, c_send.at[d, i], c_recv.at[d, i], partner)

    for i in (0, 1):
        for d in steps:
            rows_from(d, i, core).wait_recv()
            rows_over(d, i, core).start()

    own_hop.wait()

    @pl.loop(1, owners)
    def _(o):
        hop1_from(o).wait_recv()

    @pl.loop(0, owners)
    def _(i):
        for r in range(8):
            hop_out[i, r] = hop_in[place_of(i, r)]

    @pl.loop(1, owners)
    def _(o):
        hop2(o).start()

    own_out = pltpu.make_async_copy(hop_out.at[me], blocks.at[:, me, core], loc.at[4])
    own_out.start()

    for i in range(SIDE):
        pltpu.make_async_copy(slice_of(i * SIDE + y), acts.at[i, y], loc.at[5 + i]).wait()
    weights.wait_rest()
    weights.wait_opposite()

    def product(i, j):
        return jnp.dot(acts[i, j], w[i], preferred_element_type=F32)

    @pl.loop(0, SIDE)
    def _(j):
        acc[j] = product(2 * core, j)
        acc[j] += product(2 * core + 1, j)

    for i in (0, 1):
        for d in steps:
            rows_over(d, i, 1 - core).wait_recv()

    def sums_to(d):
        to = ring(y, d)
        return remote(part.at[d], sums.at[d], s_send.at[d], s_recv.at[d], (x * SIDE + to, head))

    for d in (OPPOSITE, RIGHT, LEFT):
        j = ring(y, d)
        acc[j] += product(2 - 2 * core, j)
        part[d] = (acc[j] + product(3 - 2 * core, j)).astype(BF16)
        sums_to(d).start()

    def block_from(d, which):
        place = ow.at[which, ring(x, SIDE - d)]
        return remote(place, place, oo_send.at[d], oo_recv.at[d], partner)

    ow_blocks.start()
    ow_blocks.rest()
    own_ow.wait()
    block_from(0, core).start()
    acc[y] += product(2 - 2 * core, y)
    acc[y] += product(3 - 2 * core, y)

    def core_swap(which):
        return remote(
            blocks.at[:, :, which], blocks.at[:, :, which], x_send.at[0], x_recv.at[0], partner
        )

    own_out.wait()

    @pl.loop(1, owners)
    def _(o):
        hop2_from(o).wait_recv()

    core_swap(core).start()

    for d in steps:
        remote(part.at[d], sums.at[d], s_send.at[d], s_recv.at[d], (x * SIDE + ring(y, SIDE - d), head)).wait_recv()
        acc[y] += sums[d].astype(F32)

    heads = q_cols // hd
    bias = qb_ref[...].astype(F32).reshape(1, q_cols)
    both = kvb_ref[pl.ds(pl.multiple_of(z * 2 * hd, 2 * hd), 2 * hd)].astype(F32).reshape(1, 2 * hd)
    kv_bias = jnp.where(core == 0, both[:, 0:hd], both[:, hd:])
    for r in range(8):
        lines = slice(per * r, per * (r + 1))
        for j in range(heads):
            at_row = (r * heads + j) * per
            qs[at_row : at_row + per, :] = acc[y, lines, j * hd : (j + 1) * hd] + bias[:, j * hd : (j + 1) * hd]
        fpad[r * PAD : r * PAD + per, :] = acc[y, lines, q_cols:width] + kv_bias
        fpad[r * PAD + per : (r + 1) * PAD, :] = jnp.zeros((PAD - per, hd), F32)
    own_fresh[...] = fpad[...].astype(BF16).reshape(own_fresh.shape)
    fresh[core] = own_fresh[...]
    swap = remote(own_fresh, fresh.at[core], x_send.at[1], x_recv.at[1], partner)
    swap.start()
    queries[...] = qs[...].astype(BF16)

    @pl.loop(0, owners)
    def _(o):
        for m in range(2):
            row = sum([jnp.where((my_owner[r] == o) & (my_rank[r] == m), r, 0) for r in range(8)], 0)
            f_out[2 * o + m] = own_fresh[row]

    def give(o):
        to = lax.rem(me + o, owners)
        return remote(
            f_out.at[pl.ds(2 * to, 2)], f_in.at[pl.ds(2 * me, 2)], f_send.at[o], f_recv.at[me], (to, head)
        )

    def take(o):
        src = lax.rem(me + owners - o, owners)
        return remote(
            f_out.at[pl.ds(2 * src, 2)], f_in.at[pl.ds(2 * src, 2)], f_send.at[o], f_recv.at[src], (src, head)
        )

    @pl.loop(1, owners)
    def _(o):
        give(o).start()

    for m in range(2):
        f_in[2 * me + m] = f_out[2 * me + m]

    core_swap(1 - core).wait_recv()
    remote(fresh.at[1 - core], fresh.at[1 - core], x_send.at[1], x_recv.at[1], partner).wait_recv()

    attend(queries, fresh, blocks, my_rows, ctx, ks, vs, sc, top, low, res, flat)

    def ctx_to(d):
        to = ring(y, d)
        return remote(
            ctx, ctxs.at[y // 2, core], t_send.at[d], t_recv.at[d, core], (x * SIDE + to, 2 * z + lax.rem(y, 2))
        )

    def ctx_from(d, which):
        src = ring(y, SIDE - d)
        place = ctxs.at[src // 2, which]
        return remote(place, place, t_send.at[d], t_recv.at[d, which], (x * SIDE + src, 2 * z + which))

    for d in (RIGHT, LEFT, OPPOSITE):
        ctx_to(d).start()

    mine = lax.rem(y, 2) == core

    @pl.when(mine)
    def _():
        ctxs[y // 2, core] = ctx[...]

    @pl.when(jnp.logical_not(mine))
    def _():
        ctx_to(0).start()

    ow_blocks.forward()
    ow_blocks.wait_rest()
    block_from(RIGHT, core).start()
    block_from(LEFT, core).start()

    @pl.loop(1, owners)
    def _(o):
        take(o).wait_recv()

    for s in range(8):
        back[core, s] = f_in[picks[s]]
    swap_back = remote(back.at[core], back.at[core], x_send.at[2], x_recv.at[2], partner)
    swap_back.start()

    @pl.when(mine)
    def _():
        ctx_from(0, 1 - core).wait_recv()
        for which in (0, 1):
            ctx_from(OPPOSITE, which).wait_recv()

    @pl.when(jnp.logical_not(mine))
    def _():
        for d in (RIGHT, LEFT):
            for which in (0, 1):
                ctx_from(d, which).wait_recv()

    ow_blocks.wait_opposite()
    block_from(OPPOSITE, core).start()
    for d in (0,) + steps:
        block_from(d, 1 - core).wait_recv()

    hrow = rows // 2
    order = (4, 3, -3, 2, -2, 1, -1, 0)

    def compute(n):
        target = lax.rem(z + order[n] + levels, levels)
        column, request = target // 2, lax.rem(target, 2)
        chunk[n] = jnp.dot(ctxs[request, 0], ow[0, column], preferred_element_type=F32)
        chunk[n] += jnp.dot(ctxs[request, 1], ow[1, column], preferred_element_type=F32)

    def lines_of(half):
        return slice(half * hrow, (half + 1) * hrow)

    def ring_copy(step, half, out, into, send_sem, recv_sem, to):
        return remote(
            out.at[step, pl.ds(half * hrow, hrow)],
            into.at[step, pl.ds(half * hrow, hrow)],
            send_sem.at[step, half],
            recv_sem.at[step, half],
            to,
        )

    def rightward(step, half):
        return ring_copy(step, half, r_out, r_in, r_send, r_recv, right)

    def leftward(step, half):
        return ring_copy(step, half, l_out, l_in, l_send, l_recv, left)

    def renew(s):
        keys, values = blend(old[s].reshape(new.shape[1], 2 * hd), back[0, s], back[1, s], slot_rows[s : s + 1, 0:PAD])
        new[s, :, 0:hd] = keys
        new[s, :, hd : 2 * hd] = values
        pltpu.make_async_copy(new.at[s], new_hbm.at[s], n_sem.at[s]).start()

    compute(0)
    r_out[0, lines_of(0), :] = chunk[0, lines_of(0), :].astype(BF16)
    rightward(0, 0).start()
    l_out[0, lines_of(1), :] = chunk[0, lines_of(1), :].astype(BF16)
    leftward(0, 1).start()
    compute(1)
    compute(2)
    for step in (1, 2, 3):
        n_right, n_left = 2 * step - 1, 2 * step
        halves = ((1, 0), (0, 1)) if step == 1 else ((0, 1), (1, 0))
        for right_half, left_half in halves:
            value = chunk[n_right, lines_of(right_half), :]
            if step > 1 or right_half == 0:
                rightward(step - 1, right_half).wait_recv()
                value += r_in[step - 1, lines_of(right_half), :].astype(F32)
            r_out[step, lines_of(right_half), :] = value.astype(BF16)
            rightward(step, right_half).start()
            value = chunk[n_left, lines_of(left_half), :]
            if step > 1 or left_half == 1:
                leftward(step - 1, left_half).wait_recv()
                value += l_in[step - 1, lines_of(left_half), :].astype(F32)
            l_out[step, lines_of(left_half), :] = value.astype(BF16)
            leftward(step, left_half).start()
        if step == 1:
            old_in.wait()
            remote(back.at[1 - core], back.at[1 - core], x_send.at[2], x_recv.at[2], partner).wait_recv()
        if step < 3:
            compute(2 * step + 1)
            compute(2 * step + 2)
            for s in range(4 * step - 4, 4 * step):
                renew(s)
        else:
            compute(7)

    def flip(half):
        return remote(
            done.at[pl.ds(half * hrow, hrow)], out_ref.at[pl.ds(half * hrow, hrow)],
            x_send.at[3 + half], x_recv.at[3 + half], mirror,
        )

    for half in (0, 1):
        rightward(3, half).wait_recv()
        leftward(3, half).wait_recv()
        value = chunk[7, lines_of(half), :] + r_in[3, lines_of(half), :].astype(F32)
        value += l_in[3, lines_of(half), :].astype(F32)
        done[lines_of(half), :] = value.astype(BF16)

        @pl.when(turn != y)
        def _():
            flip(half).start()

    @pl.when(turn == y)
    def _():
        out_ref[...] = done[...]

    for i in (0, 1):
        for d in steps:
            rows_to(d, i).wait_send()
            rows_over(d, i, core).wait_send()
    for d in steps:
        sums_to(d).wait_send()
        ctx_to(d).wait_send()
    weights.finish()
    ow_blocks.finish()
    for d in (0,) + steps:
        block_from(d, core).wait_send()

    @pl.when(jnp.logical_not(mine))
    def _():
        ctx_to(0).wait_send()

    @pl.loop(1, owners)
    def _(o):
        hop1(o).wait_send()
        hop2(o).wait_send()
        give(o).wait_send()

    core_swap(core).wait_send()
    swap.wait_send()
    swap_back.wait_send()
    rightward(0, 0).wait_send()
    leftward(0, 1).wait_send()
    for step in (1, 2, 3):
        for half in (0, 1):
            rightward(step, half).wait_send()
            leftward(step, half).wait_send()
    for s in range(8):
        pltpu.make_async_copy(new.at[s], new_hbm.at[s], n_sem.at[s]).wait()

    @pl.when(turn != y)
    def _():
        for half in (0, 1):
            flip(half).wait()


def hand_over(out_ref, store_ref, out_copy, store_copy, sem):
    copies = [pltpu.make_async_copy(out_ref, out_copy, sem.at[0])]
    for s in range(store_ref.shape[0]):
        copies.append(pltpu.make_async_copy(store_ref.at[s], store_copy.at[s, 0], sem.at[s + 1]))
    for copy in copies:
        copy.start()
    for copy in copies:
        copy.wait()


def shards(
    hidden, norm_gain, q_weight, q_bias, kv_weight, kv_bias, out_weight, kv_store, stretch_place, req_stretches, rec_rows
):
    owners = lax.axis_size("cache")
    me = lax.axis_index("cache")
    rows, width = hidden.shape
    stretches, _, length, kv_width = kv_store.shape
    hd = kv_width // 2
    per = rec_rows.shape[2]
    depth, q_cols = q_weight.shape
    levels = lax.axis_size("heads") // 2
    heads = q_cols // hd
    vmem = pl.BlockSpec(memory_space=pltpu.VMEM)
    smem = pl.BlockSpec(memory_space=pltpu.SMEM)
    hbm = pl.BlockSpec(memory_space=pl.ANY)
    dma = pltpu.SemaphoreType.DMA

    store = kv_store.reshape(stretches, owners, 2, length // (2 * owners), kv_width)
    piece = length // (2 * owners)

    attn_out, new_store = pl.pallas_call(
        prefill,
        out_shape=(
            jax.ShapeDtypeStruct((rows, q_cols), BF16),
            jax.ShapeDtypeStruct((stretches, length, kv_width), BF16),
        ),
        in_specs=[smem, smem, hbm, vmem, hbm, hbm, vmem, vmem, hbm, hbm, vmem],
        out_specs=(vmem, hbm),
        scratch_shapes=[
            pltpu.VMEM((rows, width), BF16),
            pltpu.VMEM((SIDE, SIDE, rows, depth), BF16),
            pltpu.VMEM((SIDE, depth, q_cols + hd), BF16),
            pltpu.VMEM((SIDE, rows, q_cols + hd), F32),
            pltpu.VMEM((SIDE, rows, q_cols + hd), BF16),
            pltpu.VMEM((SIDE, rows, q_cols + hd), BF16),
            pltpu.VMEM((owners * stretches, piece, kv_width), BF16),
            pltpu.VMEM((owners, stretches, piece, kv_width), BF16),
            pltpu.VMEM((rows * heads, hd), F32),
            pltpu.VMEM((stretches * PAD, hd), F32),
            pltpu.VMEM((stretches, hd), jnp.int32),
            pltpu.VMEM((stretches, hd), jnp.int32),
            pltpu.VMEM((rows * heads, hd), BF16),
            pltpu.VMEM((stretches, PAD, hd), BF16),
            pltpu.VMEM((2, stretches, PAD, hd), BF16),
            pltpu.VMEM((stretches, owners, 2, piece, kv_width), BF16),
            pltpu.VMEM((stretches, length, hd), BF16),
            pltpu.VMEM((stretches, length, hd), BF16),
            pltpu.VMEM((rows * heads * (stretches + 1) // 2, length), F32),
            pltpu.VMEM((rows * heads, hd), F32),
            pltpu.VMEM((rows * heads, hd), F32),
            pltpu.VMEM((rows * heads, hd), F32),
            pltpu.VMEM((rows, q_cols), F32),
            pltpu.VMEM((rows, q_cols), BF16),
            pltpu.VMEM((2, SIDE, depth, q_cols), BF16),
            pltpu.VMEM((2, 2, rows, q_cols), BF16),
            pltpu.VMEM((levels, rows, q_cols), F32),
            pltpu.VMEM((4, rows, q_cols), BF16),
            pltpu.VMEM((4, rows, q_cols), BF16),
            pltpu.VMEM((4, rows, q_cols), BF16),
            pltpu.VMEM((4, rows, q_cols), BF16),
            pltpu.VMEM((rows, q_cols), BF16),
            pltpu.VMEM((2 * owners, PAD, hd), BF16),
            pltpu.VMEM((2 * owners, PAD, hd), BF16),
            pltpu.VMEM((2, stretches, PAD, hd), BF16),
            pltpu.VMEM((stretches, owners, 2, piece, kv_width), BF16),
            pltpu.VMEM((stretches, length, kv_width), BF16),
            dma((7 + SIDE,)),
            dma((SIDE, 2)),
            dma((SIDE, 2)),
            dma((SIDE, 2)),
            dma((SIDE, 2)),
            dma((SIDE, 2)),
            dma((SIDE, 2)),
            dma((SIDE,)),
            dma((SIDE,)),
            dma((owners,)),
            dma((owners,)),
            dma((owners,)),
            dma((owners,)),
            dma((5,)),
            dma((5,)),
            dma((SIDE, 2)),
            dma((SIDE, 2)),
            dma((SIDE,)),
            dma((SIDE,)),
            dma((SIDE,)),
            dma((SIDE, 2)),
            dma((4, 2)),
            dma((4, 2)),
            dma((4, 2)),
            dma((4, 2)),
            dma((owners,)),
            dma((owners,)),
            dma((8,)),
        ],
        compiler_params=pltpu.CompilerParams(collective_id=0, has_side_effects=True, vmem_limit_bytes=58 << 20),
        name="prefill",
    )(
        stretch_place, req_stretches, hidden, norm_gain, q_weight, kv_weight, q_bias, kv_bias, out_weight, store, rec_rows
    )
    return pl.pallas_call(
        hand_over,
        out_shape=(
            jax.ShapeDtypeStruct((rows, q_cols), BF16),
            jax.ShapeDtypeStruct((stretches, 1, length, kv_width), BF16),
        ),
        in_specs=[hbm, hbm],
        out_specs=(hbm, hbm),
        scratch_shapes=[dma((stretches + 1,))],
        name="hand_over",
    )(attn_out, new_store)


def solution(mesh):
    placed = (
        P("cache", None),
        P(),
        P("cache", "heads"),
        P("heads"),
        P("cache", None),
        P(),
        P("heads", "cache"),
        P("cache", "heads", None, None),
        P(),
        P(),
        P(),
    )
    return jax.shard_map(
        shards,
        mesh=mesh,
        in_specs=placed,
        out_specs=(P("cache", "heads"), P("cache", "heads", None, None)),
        check_vma=False,
    )
```

```python
import functools
import math

import jax
import jax.numpy as jnp
from jax import lax
from jax.experimental import pallas as pl
from jax.experimental.pallas import tpu as pltpu
from jax.sharding import PartitionSpec as P

MESH = pl.DeviceIdType.MESH
SIDE = 4
BF16 = jnp.bfloat16
F32 = jnp.float32
RIGHT, OPPOSITE, LEFT = 1, 2, 3
PAD = 32


def remote(src, dst, send_sem, recv_sem, device):
    return pltpu.make_async_remote_copy(
        src_ref=src, dst_ref=dst, send_sem=send_sem, recv_sem=recv_sem, device_id=device, device_id_type=MESH
    )


def blend(old, keys, values, rows):
    hd = keys.shape[1]
    hit = lax.broadcasted_iota(jnp.int32, (old.shape[0], PAD), 0) == rows
    table = jnp.concatenate([keys, values, jnp.ones((PAD, hd), BF16)], axis=1)
    new = jnp.dot(hit.astype(F32).astype(BF16), table, preferred_element_type=F32)
    there = new[:, 2 * hd :] > 0.5
    parts = [
        jnp.where(there, new[:, i * hd : (i + 1) * hd], old[:, i * hd : (i + 1) * hd].astype(F32)).astype(BF16)
        for i in (0, 1)
    ]
    return parts[0], parts[1]


def attend(q_ref, fresh_ref, blocks_ref, row_ref, ctx_ref, ks, vs, sc, top, low, out, flat):
    stretches, length = ks.shape[0], ks.shape[1]
    hd = q_ref.shape[1]
    total = q_ref.shape[0]
    group = total // stretches
    heads = ctx_ref.shape[1] // hd
    per = group // heads
    scale = math.log2(math.e) / math.sqrt(hd)
    for r in range(stretches):
        old = blocks_ref[r].reshape(length, 2 * hd)
        ks[r], vs[r] = blend(old, fresh_ref[0, r], fresh_ref[1, r], row_ref[r : r + 1, 0:PAD])
    top[...] = jnp.full_like(top, -jnp.inf)
    low[...] = jnp.zeros_like(low)
    out[...] = jnp.zeros_like(out)

    def fold(a, op):
        parts = [a[:, i * hd : (i + 1) * hd] for i in range(length // hd)]
        while len(parts) > 1:
            parts = [op(parts[i], parts[i + 1]) for i in range(0, len(parts), 2)]
        return parts[0]

    columns = jnp.transpose(row_ref[...].astype(F32))
    base = [sum(total - t * group for t in range(s)) for s in range(stretches)]
    for s in range(stretches):
        scores = lax.dot_general(
            q_ref[s * group :, :], ks[s], (((1,), (1,)), ((), ())), preferred_element_type=F32
        )
        key = lax.broadcasted_iota(jnp.int32, (group, length), 1).astype(F32)
        last = jnp.concatenate([columns[0:per, s : s + 1]] * heads, axis=0)
        first = jnp.where(key <= last, scores[:group], -jnp.inf)
        sc[base[s] : base[s] + group, :] = first
        top[s * group : (s + 1) * group, :] = jnp.maximum(
            top[s * group : (s + 1) * group, :], fold(first, jnp.maximum)
        )
        if s + 1 < stretches:
            sc[base[s] + group : base[s] + total - s * group, :] = scores[group:]
            top[(s + 1) * group :, :] = jnp.maximum(top[(s + 1) * group :, :], fold(scores[group:], jnp.maximum))
    top[...] = jnp.broadcast_to(jnp.max(top[...], axis=1, keepdims=True), top.shape)
    for s in range(stretches):
        here = slice(s * group, total)
        held = slice(base[s], base[s] + total - s * group)
        peak = top[here, :]
        expon = jnp.concatenate(
            [jnp.exp2((sc[held, i * hd : (i + 1) * hd] - peak) * scale) for i in range(length // hd)], axis=1
        )
        low[here, :] += fold(expon, jnp.add)
        out[here, :] += jnp.dot(expon.astype(BF16), vs[s], preferred_element_type=F32)
    out[...] = out[...] / jnp.sum(low[...], axis=1, keepdims=True)
    for r in range(stretches):
        for j in range(heads):
            at_row = (r * heads + j) * per
            flat[r * per : (r + 1) * per, j * hd : (j + 1) * hd] = out[at_row : at_row + per, :]
    ctx_ref[...] = flat[...].astype(BF16)


def prefill(
    table_ref, req_ref, hid_hbm, gain_ref, qw_hbm, kvw_hbm, qb_ref, kvb_ref, ow_hbm, store_hbm, rec_ref,
    out_ref, new_hbm,
    hid, acts, w, acc, part, sums, hop_in, hop_out, qs, fpad, my_rows, slot_rows,
    queries, own_fresh, fresh, blocks, ks, vs, sc, top, low, res, flat, ctx,
    ow, ctxs, chunk, r_out, l_out, r_in, l_in, done, f_out, f_in, back, old, new,
    loc, w_send, w_recv, a_send, a_recv, c_send, c_recv, s_send, s_recv,
    h1_send, h1_recv, h2_send, h2_recv, x_send, x_recv,
    o_send, o_recv, oo_send, oo_recv, t_send, t_recv,
    r_send, r_recv, l_send, l_recv, f_send, f_recv, n_sem,
):
    me = lax.axis_index("cache")
    head = lax.axis_index("heads")
    core = lax.rem(head, 2)
    partner = (me, head + 1 - 2 * core)
    x, y = me // SIDE, lax.rem(me, SIDE)
    z = head // 2
    owners = SIDE * SIDE
    levels = lax.axis_size("heads") // 2
    right = (me, lax.rem(z + 1, levels) * 2 + core)
    left = (me, lax.rem(z + levels - 1, levels) * 2 + core)
    turn = lax.rem(head, SIDE)
    mirror = (x * SIDE + turn, head - turn + y)
    rows = hid.shape[0]
    depth, width = w.shape[1], w.shape[2]
    q_cols = qw_hbm.shape[1]
    hd = width - q_cols
    per = rows // 8

    def ring(i, d):
        return lax.rem(i + d, SIDE)

    own_hid = pltpu.make_async_copy(hid_hbm, hid, loc.at[2])
    own_q = pltpu.make_async_copy(qw_hbm, w.at[x, :, 0:q_cols], loc.at[0])
    own_kv = pltpu.make_async_copy(
        kvw_hbm.at[:, pl.ds(pl.multiple_of(head * hd, hd), hd)], w.at[x, :, q_cols:width], loc.at[1]
    )
    own_hop = pltpu.make_async_copy(store_hbm.at[:, me, core], hop_in.at[pl.ds(me * 8, 8)], loc.at[3])
    own_hid.start()
    own_q.start()
    own_kv.start()
    own_hop.start()
    own_ow = pltpu.make_async_copy(ow_hbm, ow.at[core, x], loc.at[5 + SIDE])
    own_ow.start()
    old_in = pltpu.make_async_copy(store_hbm, old, loc.at[6 + SIDE])
    old_in.start()

    barrier = pltpu.get_barrier_semaphore()

    @pl.loop(1, owners)
    def _(o):
        pl.semaphore_signal(barrier, inc=1, device_id=(lax.rem(me + o, owners), head), device_id_type=MESH)

    for peer in (partner, left, right):
        pl.semaphore_signal(barrier, inc=1, device_id=peer, device_id_type=MESH)
    for d in (RIGHT, OPPOSITE, LEFT):
        across = (x * SIDE + ring(y, d), head + 1 - 2 * core)
        pl.semaphore_signal(barrier, inc=1, device_id=across, device_id_type=MESH)

    @pl.when(turn != y)
    def _():
        pl.semaphore_signal(barrier, inc=1, device_id=mirror, device_id_type=MESH)

    @pl.when(turn != y)
    def _():
        pl.semaphore_wait(barrier, owners + 6)

    @pl.when(turn == y)
    def _():
        pl.semaphore_wait(barrier, owners + 5)

    def slice_of(c):
        return hid.at[:, pl.ds(pl.multiple_of(c * depth, depth), depth)]

    def rows_to(d, i):
        to = ring(y, d)
        return remote(
            slice_of((2 * core + i) * SIDE + to), acts.at[2 * core + i, y], a_send.at[d, i], a_recv.at[d, i],
            (x * SIDE + to, head),
        )

    def hop1(o):
        to = lax.rem(me + o, owners)
        return remote(
            store_hbm.at[:, to, core], hop_in.at[pl.ds(me * 8, 8)], h1_send.at[o], h1_recv.at[me], (to, head)
        )

    def hop1_from(o):
        src = lax.rem(me + owners - o, owners)
        return remote(
            store_hbm.at[:, src, core], hop_in.at[pl.ds(src * 8, 8)], h1_send.at[o], h1_recv.at[src], (src, head)
        )

    def hop2(o):
        to = lax.rem(me + o, owners)
        return remote(hop_out.at[to], blocks.at[:, me, core], h2_send.at[o], h2_recv.at[me], (to, head))

    def hop2_from(o):
        src = lax.rem(me + owners - o, owners)
        return remote(hop_out.at[src], blocks.at[:, src, core], h2_send.at[o], h2_recv.at[src], (src, head))

    class Ring4:
        def __init__(self, source, place, send_sem, recv_sem):
            self.source, self.place, self.send_sem, self.recv_sem = source, place, send_sem, recv_sem
            self.deep = place(0).shape[0] // 2

        def part(self, ref, half):
            return ref.at[pl.ds(half * self.deep, self.deep)]

        def copy(self, d, half, passed=False):
            to = (ring(x, d) * SIDE + y, head)
            src = self.part(self.place(ring(x, SIDE - d)) if passed else self.source, half)
            dst = self.part(self.place(ring(x, SIDE - d) if passed else x), half)
            k = OPPOSITE if passed else d
            return remote(src, dst, self.send_sem.at[k, half], self.recv_sem.at[k, half], to)

        def wait(self, d, half):
            place = self.part(self.place(ring(x, SIDE - d)), half)
            remote(
                place, place, self.send_sem.at[d, half], self.recv_sem.at[d, half],
                (ring(x, SIDE - d) * SIDE + y, head),
            ).wait_recv()

        def start(self):
            self.copy(RIGHT, 0).start()
            self.copy(LEFT, 1).start()

        def rest(self):
            self.copy(RIGHT, 1).start()
            self.copy(LEFT, 0).start()

        def forward(self):
            self.wait(RIGHT, 0)
            self.copy(RIGHT, 0, True).start()
            self.wait(LEFT, 1)
            self.copy(LEFT, 1, True).start()

        def wait_rest(self):
            self.wait(RIGHT, 1)
            self.wait(LEFT, 0)

        def wait_opposite(self):
            self.wait(OPPOSITE, 0)
            self.wait(OPPOSITE, 1)

        def finish(self):
            for half in (0, 1):
                self.copy(RIGHT, half).wait_send()
                self.copy(LEFT, half).wait_send()
            self.copy(RIGHT, 0, True).wait_send()
            self.copy(LEFT, 1, True).wait_send()

    weights = Ring4(w.at[x], lambda i: w.at[i], w_send, w_recv)
    ow_blocks = Ring4(ow_hbm, lambda i: ow.at[core, i], o_send, o_recv)

    steps = (RIGHT, LEFT, OPPOSITE)
    own_q.wait()
    own_kv.wait()
    weights.start()

    @pl.loop(1, owners)
    def _(o):
        hop1(o).start()

    own_hid.wait()
    tall = 16

    @pl.loop(0, rows // tall)
    def _(i):
        lines = pl.ds(pl.multiple_of(i * tall, tall), tall)
        total = jnp.zeros((tall, 1), F32)
        for c in range(owners):
            v = hid[lines, c * depth : (c + 1) * depth].astype(F32)
            total += jnp.sum(v * v, axis=-1, keepdims=True)
        factor = lax.rsqrt(total / (owners * depth) + 1e-06)
        for c in range(owners):
            v = hid[lines, c * depth : (c + 1) * depth].astype(F32)
            g = gain_ref[c * depth : (c + 1) * depth].astype(F32).reshape(1, depth)
            hid[lines, c * depth : (c + 1) * depth] = (v * factor * g).astype(BF16)

    for i in (0, 1):
        for d in steps:
            rows_to(d, i).start()
    weights.rest()

    for i in range(SIDE):
        pltpu.make_async_copy(slice_of(i * SIDE + y), acts.at[i, y], loc.at[5 + i]).start()

    def place_of(i, r):
        return table_ref[req_ref[i, r]]

    my_owner = [place_of(me, r) // 8 for r in range(8)]
    my_rank = [sum([(my_owner[q] == my_owner[r]).astype(jnp.int32) for q in range(r)], 0) for r in range(8)]

    def find(n, found):
        here = place_of(n // 8, lax.rem(n, 8)) - me * 8
        return tuple(jnp.where(here == s, n, found[s]) for s in range(8))

    found = lax.fori_loop(0, owners * 8, find, (jnp.int32(0),) * 8)
    my_rows[...] = jnp.full_like(my_rows, -1)
    slot_rows[...] = jnp.full_like(slot_rows, -1)
    my_rows[:, 0:per] = rec_ref[me]
    picks = []
    for s in range(8):
        i, r = found[s] // 8, lax.rem(found[s], 8)
        slot_rows[s : s + 1, 0:per] = rec_ref[i, pl.ds(r, 1), :]
        rank = sum([((q < r) & (place_of(i, q) // 8 == me)).astype(jnp.int32) for q in range(8)], 0)
        picks.append(2 * i + jnp.minimum(rank, 1))

    weights.forward()

    def rows_from(d, i, which):
        src = ring(y, SIDE - d)
        place = acts.at[2 * which + i, src]
        return remote(place, place, a_send.at[d, i], a_recv.at[d, i], (x * SIDE + src, head))

    def rows_over(d, i, which):
        place = acts.at[2 * which + i, ring(y, SIDE - d)]
        return remote(place, place, c_send.at[d, i], c_recv.at[d, i], partner)

    for i in (0, 1):
        for d in steps:
            rows_from(d, i, core).wait_recv()
            rows_over(d, i, core).start()

    own_hop.wait()

    @pl.loop(1, owners)
    def _(o):
        hop1_from(o).wait_recv()

    @pl.loop(0, owners)
    def _(i):
        for r in range(8):
            hop_out[i, r] = hop_in[place_of(i, r)]

    @pl.loop(1, owners)
    def _(o):
        hop2(o).start()

    own_out = pltpu.make_async_copy(hop_out.at[me], blocks.at[:, me, core], loc.at[4])
    own_out.start()

    for i in range(SIDE):
        pltpu.make_async_copy(slice_of(i * SIDE + y), acts.at[i, y], loc.at[5 + i]).wait()
    weights.wait_rest()
    weights.wait_opposite()

    def product(i, j):
        return jnp.dot(acts[i, j], w[i], preferred_element_type=F32)

    @pl.loop(0, SIDE)
    def _(j):
        acc[j] = product(2 * core, j)
        acc[j] += product(2 * core + 1, j)

    for i in (0, 1):
        for d in steps:
            rows_over(d, i, 1 - core).wait_recv()

    def sums_to(d):
        to = ring(y, d)
        return remote(part.at[d], sums.at[d], s_send.at[d], s_recv.at[d], (x * SIDE + to, head))

    for d in (OPPOSITE, RIGHT, LEFT):
        j = ring(y, d)
        acc[j] += product(2 - 2 * core, j)
        part[d] = (acc[j] + product(3 - 2 * core, j)).astype(BF16)
        sums_to(d).start()

    def block_from(d, which):
        place = ow.at[which, ring(x, SIDE - d)]
        return remote(place, place, oo_send.at[d], oo_recv.at[d], partner)

    ow_blocks.start()
    ow_blocks.rest()
    own_ow.wait()
    block_from(0, core).start()
    acc[y] += product(2 - 2 * core, y)
    acc[y] += product(3 - 2 * core, y)

    def core_swap(which):
        return remote(
            blocks.at[:, :, which], blocks.at[:, :, which], x_send.at[0], x_recv.at[0], partner
        )

    own_out.wait()

    @pl.loop(1, owners)
    def _(o):
        hop2_from(o).wait_recv()

    core_swap(core).start()

    for d in steps:
        remote(part.at[d], sums.at[d], s_send.at[d], s_recv.at[d], (x * SIDE + ring(y, SIDE - d), head)).wait_recv()
        acc[y] += sums[d].astype(F32)

    heads = q_cols // hd
    bias = qb_ref[...].astype(F32).reshape(1, q_cols)
    both = kvb_ref[pl.ds(pl.multiple_of(z * 2 * hd, 2 * hd), 2 * hd)].astype(F32).reshape(1, 2 * hd)
    kv_bias = jnp.where(core == 0, both[:, 0:hd], both[:, hd:])
    for r in range(8):
        lines = slice(per * r, per * (r + 1))
        for j in range(heads):
            at_row = (r * heads + j) * per
            qs[at_row : at_row + per, :] = acc[y, lines, j * hd : (j + 1) * hd] + bias[:, j * hd : (j + 1) * hd]
        fpad[r * PAD : r * PAD + per, :] = acc[y, lines, q_cols:width] + kv_bias
        fpad[r * PAD + per : (r + 1) * PAD, :] = jnp.zeros((PAD - per, hd), F32)
    own_fresh[...] = fpad[...].astype(BF16).reshape(own_fresh.shape)
    fresh[core] = own_fresh[...]
    swap = remote(own_fresh, fresh.at[core], x_send.at[1], x_recv.at[1], partner)
    swap.start()
    queries[...] = qs[...].astype(BF16)

    @pl.loop(0, owners)
    def _(o):
        for m in range(2):
            row = sum([jnp.where((my_owner[r] == o) & (my_rank[r] == m), r, 0) for r in range(8)], 0)
            f_out[2 * o + m] = own_fresh[row]

    def give(o):
        to = lax.rem(me + o, owners)
        return remote(
            f_out.at[pl.ds(2 * to, 2)], f_in.at[pl.ds(2 * me, 2)], f_send.at[o], f_recv.at[me], (to, head)
        )

    def take(o):
        src = lax.rem(me + owners - o, owners)
        return remote(
            f_out.at[pl.ds(2 * src, 2)], f_in.at[pl.ds(2 * src, 2)], f_send.at[o], f_recv.at[src], (src, head)
        )

    @pl.loop(1, owners)
    def _(o):
        give(o).start()

    for m in range(2):
        f_in[2 * me + m] = f_out[2 * me + m]

    core_swap(1 - core).wait_recv()
    remote(fresh.at[1 - core], fresh.at[1 - core], x_send.at[1], x_recv.at[1], partner).wait_recv()

    attend(queries, fresh, blocks, my_rows, ctx, ks, vs, sc, top, low, res, flat)

    def ctx_to(d):
        to = ring(y, d)
        return remote(
            ctx, ctxs.at[y // 2, core], t_send.at[d], t_recv.at[d, core], (x * SIDE + to, 2 * z + lax.rem(y, 2))
        )

    def ctx_from(d, which):
        src = ring(y, SIDE - d)
        place = ctxs.at[src // 2, which]
        return remote(place, place, t_send.at[d], t_recv.at[d, which], (x * SIDE + src, 2 * z + which))

    for d in (RIGHT, LEFT, OPPOSITE):
        ctx_to(d).start()

    mine = lax.rem(y, 2) == core

    @pl.when(mine)
    def _():
        ctxs[y // 2, core] = ctx[...]

    @pl.when(jnp.logical_not(mine))
    def _():
        ctx_to(0).start()

    ow_blocks.forward()
    ow_blocks.wait_rest()
    block_from(RIGHT, core).start()
    block_from(LEFT, core).start()

    @pl.loop(1, owners)
    def _(o):
        take(o).wait_recv()

    for s in range(8):
        back[core, s] = f_in[picks[s]]
    swap_back = remote(back.at[core], back.at[core], x_send.at[2], x_recv.at[2], partner)
    swap_back.start()

    @pl.when(mine)
    def _():
        ctx_from(0, 1 - core).wait_recv()
        for which in (0, 1):
            ctx_from(OPPOSITE, which).wait_recv()

    @pl.when(jnp.logical_not(mine))
    def _():
        for d in (RIGHT, LEFT):
            for which in (0, 1):
                ctx_from(d, which).wait_recv()

    ow_blocks.wait_opposite()
    block_from(OPPOSITE, core).start()
    for d in (0,) + steps:
        block_from(d, 1 - core).wait_recv()

    hrow = rows // 2
    order = (4, 3, -3, 2, -2, 1, -1, 0)

    def compute(n):
        target = lax.rem(z + order[n] + levels, levels)
        column, request = target // 2, lax.rem(target, 2)
        chunk[n] = jnp.dot(ctxs[request, 0], ow[0, column], preferred_element_type=F32)
        chunk[n] += jnp.dot(ctxs[request, 1], ow[1, column], preferred_element_type=F32)

    def lines_of(half):
        return slice(half * hrow, (half + 1) * hrow)

    def ring_copy(step, half, out, into, send_sem, recv_sem, to):
        return remote(
            out.at[step, pl.ds(half * hrow, hrow)],
            into.at[step, pl.ds(half * hrow, hrow)],
            send_sem.at[step, half],
            recv_sem.at[step, half],
            to,
        )

    def rightward(step, half):
        return ring_copy(step, half, r_out, r_in, r_send, r_recv, right)

    def leftward(step, half):
        return ring_copy(step, half, l_out, l_in, l_send, l_recv, left)

    def renew(s):
        keys, values = blend(old[s].reshape(new.shape[1], 2 * hd), back[0, s], back[1, s], slot_rows[s : s + 1, 0:PAD])
        new[s, :, 0:hd] = keys
        new[s, :, hd : 2 * hd] = values
        pltpu.make_async_copy(new.at[s], new_hbm.at[s], n_sem.at[s]).start()

    compute(0)
    r_out[0, lines_of(0), :] = chunk[0, lines_of(0), :].astype(BF16)
    rightward(0, 0).start()
    l_out[0, lines_of(1), :] = chunk[0, lines_of(1), :].astype(BF16)
    leftward(0, 1).start()
    compute(1)
    compute(2)
    for step in (1, 2, 3):
        n_right, n_left = 2 * step - 1, 2 * step
        halves = ((1, 0), (0, 1)) if step == 1 else ((0, 1), (1, 0))
        for right_half, left_half in halves:
            value = chunk[n_right, lines_of(right_half), :]
            if step > 1 or right_half == 0:
                rightward(step - 1, right_half).wait_recv()
                value += r_in[step - 1, lines_of(right_half), :].astype(F32)
            r_out[step, lines_of(right_half), :] = value.astype(BF16)
            rightward(step, right_half).start()
            value = chunk[n_left, lines_of(left_half), :]
            if step > 1 or left_half == 1:
                leftward(step - 1, left_half).wait_recv()
                value += l_in[step - 1, lines_of(left_half), :].astype(F32)
            l_out[step, lines_of(left_half), :] = value.astype(BF16)
            leftward(step, left_half).start()
        if step == 1:
            old_in.wait()
            remote(back.at[1 - core], back.at[1 - core], x_send.at[2], x_recv.at[2], partner).wait_recv()
        if step < 3:
            compute(2 * step + 1)
            compute(2 * step + 2)
            for s in range(4 * step - 4, 4 * step):
                renew(s)
        else:
            compute(7)

    def flip(half):
        return remote(
            done.at[pl.ds(half * hrow, hrow)], out_ref.at[pl.ds(half * hrow, hrow)],
            x_send.at[3 + half], x_recv.at[3 + half], mirror,
        )

    for half in (0, 1):
        rightward(3, half).wait_recv()
        leftward(3, half).wait_recv()
        value = chunk[7, lines_of(half), :] + r_in[3, lines_of(half), :].astype(F32)
        value += l_in[3, lines_of(half), :].astype(F32)
        done[lines_of(half), :] = value.astype(BF16)

        @pl.when(turn != y)
        def _():
            flip(half).start()

    @pl.when(turn == y)
    def _():
        out_ref[...] = done[...]

    for i in (0, 1):
        for d in steps:
            rows_to(d, i).wait_send()
            rows_over(d, i, core).wait_send()
    for d in steps:
        sums_to(d).wait_send()
        ctx_to(d).wait_send()
    weights.finish()
    ow_blocks.finish()
    for d in (0,) + steps:
        block_from(d, core).wait_send()

    @pl.when(jnp.logical_not(mine))
    def _():
        ctx_to(0).wait_send()

    @pl.loop(1, owners)
    def _(o):
        hop1(o).wait_send()
        hop2(o).wait_send()
        give(o).wait_send()

    core_swap(core).wait_send()
    swap.wait_send()
    swap_back.wait_send()
    rightward(0, 0).wait_send()
    leftward(0, 1).wait_send()
    for step in (1, 2, 3):
        for half in (0, 1):
            rightward(step, half).wait_send()
            leftward(step, half).wait_send()
    for s in range(8):
        pltpu.make_async_copy(new.at[s], new_hbm.at[s], n_sem.at[s]).wait()

    @pl.when(turn != y)
    def _():
        for half in (0, 1):
            flip(half).wait()


def hand_over(out_ref, store_ref, out_copy, store_copy, out_held, held, sem_in, sem_out):
    count = store_ref.shape[0]
    ins = [pltpu.make_async_copy(store_ref.at[s], held.at[s], sem_in.at[s]) for s in range(count)]
    ins.append(pltpu.make_async_copy(out_ref, out_held, sem_in.at[count]))
    outs = [pltpu.make_async_copy(held.at[s], store_copy.at[s, 0], sem_out.at[s]) for s in range(count)]
    outs.append(pltpu.make_async_copy(out_held, out_copy, sem_out.at[count]))
    for copy in ins:
        copy.start()
    for copy_in, copy_out in zip(ins, outs):
        copy_in.wait()
        copy_out.start()
    for copy in outs:
        copy.wait()


def shards(
    hidden, norm_gain, q_weight, q_bias, kv_weight, kv_bias, out_weight, kv_store, stretch_place, req_stretches, rec_rows
):
    owners = lax.axis_size("cache")
    me = lax.axis_index("cache")
    rows, width = hidden.shape
    stretches, _, length, kv_width = kv_store.shape
    hd = kv_width // 2
    per = rec_rows.shape[2]
    depth, q_cols = q_weight.shape
    levels = lax.axis_size("heads") // 2
    heads = q_cols // hd
    vmem = pl.BlockSpec(memory_space=pltpu.VMEM)
    smem = pl.BlockSpec(memory_space=pltpu.SMEM)
    hbm = pl.BlockSpec(memory_space=pl.ANY)
    dma = pltpu.SemaphoreType.DMA

    store = kv_store.reshape(stretches, owners, 2, length // (2 * owners), kv_width)
    piece = length // (2 * owners)

    attn_out, new_store = pl.pallas_call(
        prefill,
        out_shape=(
            jax.ShapeDtypeStruct((rows, q_cols), BF16),
            jax.ShapeDtypeStruct((stretches, length, kv_width), BF16),
        ),
        in_specs=[smem, smem, hbm, vmem, hbm, hbm, vmem, vmem, hbm, hbm, vmem],
        out_specs=(vmem, hbm),
        scratch_shapes=[
            pltpu.VMEM((rows, width), BF16),
            pltpu.VMEM((SIDE, SIDE, rows, depth), BF16),
            pltpu.VMEM((SIDE, depth, q_cols + hd), BF16),
            pltpu.VMEM((SIDE, rows, q_cols + hd), F32),
            pltpu.VMEM((SIDE, rows, q_cols + hd), BF16),
            pltpu.VMEM((SIDE, rows, q_cols + hd), BF16),
            pltpu.VMEM((owners * stretches, piece, kv_width), BF16),
            pltpu.VMEM((owners, stretches, piece, kv_width), BF16),
            pltpu.VMEM((rows * heads, hd), F32),
            pltpu.VMEM((stretches * PAD, hd), F32),
            pltpu.VMEM((stretches, hd), jnp.int32),
            pltpu.VMEM((stretches, hd), jnp.int32),
            pltpu.VMEM((rows * heads, hd), BF16),
            pltpu.VMEM((stretches, PAD, hd), BF16),
            pltpu.VMEM((2, stretches, PAD, hd), BF16),
            pltpu.VMEM((stretches, owners, 2, piece, kv_width), BF16),
            pltpu.VMEM((stretches, length, hd), BF16),
            pltpu.VMEM((stretches, length, hd), BF16),
            pltpu.VMEM((rows * heads * (stretches + 1) // 2, length), F32),
            pltpu.VMEM((rows * heads, hd), F32),
            pltpu.VMEM((rows * heads, hd), F32),
            pltpu.VMEM((rows * heads, hd), F32),
            pltpu.VMEM((rows, q_cols), F32),
            pltpu.VMEM((rows, q_cols), BF16),
            pltpu.VMEM((2, SIDE, depth, q_cols), BF16),
            pltpu.VMEM((2, 2, rows, q_cols), BF16),
            pltpu.VMEM((levels, rows, q_cols), F32),
            pltpu.VMEM((4, rows, q_cols), BF16),
            pltpu.VMEM((4, rows, q_cols), BF16),
            pltpu.VMEM((4, rows, q_cols), BF16),
            pltpu.VMEM((4, rows, q_cols), BF16),
            pltpu.VMEM((rows, q_cols), BF16),
            pltpu.VMEM((2 * owners, PAD, hd), BF16),
            pltpu.VMEM((2 * owners, PAD, hd), BF16),
            pltpu.VMEM((2, stretches, PAD, hd), BF16),
            pltpu.VMEM((stretches, owners, 2, piece, kv_width), BF16),
            pltpu.VMEM((stretches, length, kv_width), BF16),
            dma((7 + SIDE,)),
            dma((SIDE, 2)),
            dma((SIDE, 2)),
            dma((SIDE, 2)),
            dma((SIDE, 2)),
            dma((SIDE, 2)),
            dma((SIDE, 2)),
            dma((SIDE,)),
            dma((SIDE,)),
            dma((owners,)),
            dma((owners,)),
            dma((owners,)),
            dma((owners,)),
            dma((5,)),
            dma((5,)),
            dma((SIDE, 2)),
            dma((SIDE, 2)),
            dma((SIDE,)),
            dma((SIDE,)),
            dma((SIDE,)),
            dma((SIDE, 2)),
            dma((4, 2)),
            dma((4, 2)),
            dma((4, 2)),
            dma((4, 2)),
            dma((owners,)),
            dma((owners,)),
            dma((8,)),
        ],
        compiler_params=pltpu.CompilerParams(collective_id=0, has_side_effects=True, vmem_limit_bytes=58 << 20),
        name="prefill",
    )(
        stretch_place, req_stretches, hidden, norm_gain, q_weight, kv_weight, q_bias, kv_bias, out_weight, store, rec_rows
    )
    return pl.pallas_call(
        hand_over,
        out_shape=(
            jax.ShapeDtypeStruct((rows, q_cols), BF16),
            jax.ShapeDtypeStruct((stretches, 1, length, kv_width), BF16),
        ),
        in_specs=[hbm, hbm],
        out_specs=(hbm, hbm),
        scratch_shapes=[
            pltpu.VMEM((rows, q_cols), BF16),
            pltpu.VMEM((stretches, length, kv_width), BF16),
            dma((stretches + 1,)),
            dma((stretches + 1,)),
        ],
        name="hand_over",
    )(attn_out, new_store)


def solution(mesh):
    placed = (
        P("cache", None),
        P(),
        P("cache", "heads"),
        P("heads"),
        P("cache", None),
        P(),
        P("heads", "cache"),
        P("cache", "heads", None, None),
        P(),
        P(),
        P(),
    )
    return jax.shard_map(
        shards,
        mesh=mesh,
        in_specs=placed,
        out_specs=(P("cache", "heads"), P("cache", "heads", None, None)),
        check_vma=False,
    )
```

```python
import functools
import math

import jax
import jax.numpy as jnp
from jax import lax
from jax.experimental import pallas as pl
from jax.experimental.pallas import tpu as pltpu
from jax.sharding import PartitionSpec as P

MESH = pl.DeviceIdType.MESH
SIDE = 4
BF16 = jnp.bfloat16
F32 = jnp.float32
RIGHT, OPPOSITE, LEFT = 1, 2, 3
PAD = 32


def remote(src, dst, send_sem, recv_sem, device):
    return pltpu.make_async_remote_copy(
        src_ref=src, dst_ref=dst, send_sem=send_sem, recv_sem=recv_sem, device_id=device, device_id_type=MESH
    )


def blend(old, keys, values, rows):
    hd = keys.shape[1]
    hit = lax.broadcasted_iota(jnp.int32, (old.shape[0], PAD), 0) == rows
    table = jnp.concatenate([keys, values, jnp.ones((PAD, hd), BF16)], axis=1)
    new = jnp.dot(hit.astype(F32).astype(BF16), table, preferred_element_type=F32)
    there = new[:, 2 * hd :] > 0.5
    parts = [
        jnp.where(there, new[:, i * hd : (i + 1) * hd], old[:, i * hd : (i + 1) * hd].astype(F32)).astype(BF16)
        for i in (0, 1)
    ]
    return parts[0], parts[1]


def attend(q_ref, fresh_ref, blocks_ref, row_ref, ctx_ref, ks, vs, sc, top, low, out, flat):
    stretches, length = ks.shape[0], ks.shape[1]
    hd = q_ref.shape[1]
    total = q_ref.shape[0]
    group = total // stretches
    heads = ctx_ref.shape[1] // hd
    per = group // heads
    scale = math.log2(math.e) / math.sqrt(hd)
    for r in range(stretches):
        old = blocks_ref[r].reshape(length, 2 * hd)
        ks[r], vs[r] = blend(old, fresh_ref[0, r], fresh_ref[1, r], row_ref[r : r + 1, 0:PAD])
    top[...] = jnp.full_like(top, -jnp.inf)
    low[...] = jnp.zeros_like(low)
    out[...] = jnp.zeros_like(out)

    def fold(a, op):
        parts = [a[:, i * hd : (i + 1) * hd] for i in range(length // hd)]
        while len(parts) > 1:
            parts = [op(parts[i], parts[i + 1]) for i in range(0, len(parts), 2)]
        return parts[0]

    columns = jnp.transpose(row_ref[...].astype(F32))
    base = [sum(total - t * group for t in range(s)) for s in range(stretches)]
    for s in range(stretches):
        scores = lax.dot_general(
            q_ref[s * group :, :], ks[s], (((1,), (1,)), ((), ())), preferred_element_type=F32
        )
        key = lax.broadcasted_iota(jnp.int32, (group, length), 1).astype(F32)
        last = jnp.concatenate([columns[0:per, s : s + 1]] * heads, axis=0)
        first = jnp.where(key <= last, scores[:group], -jnp.inf)
        sc[base[s] : base[s] + group, :] = first
        top[s * group : (s + 1) * group, :] = jnp.maximum(
            top[s * group : (s + 1) * group, :], fold(first, jnp.maximum)
        )
        if s + 1 < stretches:
            sc[base[s] + group : base[s] + total - s * group, :] = scores[group:]
            top[(s + 1) * group :, :] = jnp.maximum(top[(s + 1) * group :, :], fold(scores[group:], jnp.maximum))
    top[...] = jnp.broadcast_to(jnp.max(top[...], axis=1, keepdims=True), top.shape)
    for s in range(stretches):
        here = slice(s * group, total)
        held = slice(base[s], base[s] + total - s * group)
        peak = top[here, :]
        expon = jnp.concatenate(
            [jnp.exp2((sc[held, i * hd : (i + 1) * hd] - peak) * scale) for i in range(length // hd)], axis=1
        )
        low[here, :] += fold(expon, jnp.add)
        out[here, :] += jnp.dot(expon.astype(BF16), vs[s], preferred_element_type=F32)
    out[...] = out[...] / jnp.sum(low[...], axis=1, keepdims=True)
    for r in range(stretches):
        for j in range(heads):
            at_row = (r * heads + j) * per
            flat[r * per : (r + 1) * per, j * hd : (j + 1) * hd] = out[at_row : at_row + per, :]
    ctx_ref[...] = flat[...].astype(BF16)


def prefill(
    table_ref, req_ref, hid_hbm, gain_ref, qw_hbm, kvw_hbm, qb_ref, kvb_ref, ow_hbm, store_hbm, rec_ref,
    out_ref, new_hbm,
    hid, acts, w, acc, part, sums, hop_in, hop_out, qs, fpad, my_rows, slot_rows,
    queries, own_fresh, fresh, blocks, ks, vs, sc, top, low, res, flat, ctx,
    ow, ctxs, chunk, r_out, l_out, r_in, l_in, done, f_out, f_in, back, old, new,
    loc, w_send, w_recv, a_send, a_recv, zr_send, zr_recv, zl_send, zl_recv, c_send, c_recv, s_send, s_recv,
    h1_send, h1_recv, h2_send, h2_recv, x_send, x_recv,
    o_send, o_recv, oo_send, oo_recv, t_send, t_recv,
    r_send, r_recv, l_send, l_recv, f_send, f_recv, n_sem,
):
    me = lax.axis_index("cache")
    head = lax.axis_index("heads")
    core = lax.rem(head, 2)
    partner = (me, head + 1 - 2 * core)
    x, y = me // SIDE, lax.rem(me, SIDE)
    z = head // 2
    owners = SIDE * SIDE
    levels = lax.axis_size("heads") // 2
    right = (me, lax.rem(z + 1, levels) * 2 + core)
    left = (me, lax.rem(z + levels - 1, levels) * 2 + core)
    turn = lax.rem(head, SIDE)
    mirror = (x * SIDE + turn, head - turn + y)
    rows = hid.shape[0]
    depth, width = w.shape[1], w.shape[2]
    q_cols = qw_hbm.shape[1]
    hd = width - q_cols
    per = rows // 8

    def ring(i, d):
        return lax.rem(i + d, SIDE)

    own_hid = pltpu.make_async_copy(hid_hbm, hid, loc.at[2])
    own_q = pltpu.make_async_copy(qw_hbm, w.at[x, :, 0:q_cols], loc.at[0])
    own_kv = pltpu.make_async_copy(
        kvw_hbm.at[:, pl.ds(pl.multiple_of(head * hd, hd), hd)], w.at[x, :, q_cols:width], loc.at[1]
    )
    own_hop = pltpu.make_async_copy(store_hbm.at[:, me, core], hop_in.at[pl.ds(me * 8, 8)], loc.at[3])
    own_hid.start()
    own_q.start()
    own_kv.start()
    own_hop.start()
    own_ow = pltpu.make_async_copy(ow_hbm, ow.at[core, x], loc.at[5 + SIDE])
    own_ow.start()
    old_in = pltpu.make_async_copy(store_hbm, old, loc.at[6 + SIDE])
    old_in.start()

    barrier = pltpu.get_barrier_semaphore()

    @pl.loop(1, owners)
    def _(o):
        pl.semaphore_signal(barrier, inc=1, device_id=(lax.rem(me + o, owners), head), device_id_type=MESH)

    for peer in (partner, left, right):
        pl.semaphore_signal(barrier, inc=1, device_id=peer, device_id_type=MESH)
    for d in (RIGHT, OPPOSITE, LEFT):
        across = (x * SIDE + ring(y, d), head + 1 - 2 * core)
        pl.semaphore_signal(barrier, inc=1, device_id=across, device_id_type=MESH)

    @pl.when(turn != y)
    def _():
        pl.semaphore_signal(barrier, inc=1, device_id=mirror, device_id_type=MESH)

    @pl.when(turn != y)
    def _():
        pl.semaphore_wait(barrier, owners + 6)

    @pl.when(turn == y)
    def _():
        pl.semaphore_wait(barrier, owners + 5)

    def slice_of(c):
        return hid.at[:, pl.ds(pl.multiple_of(c * depth, depth), depth)]

    few = rows // 4

    def eighth(level, d):
        lines = pl.ds(pl.multiple_of(level // 2 * few, few), few)
        return acts.at[2 * core + lax.rem(level, 2), ring(y, SIDE - d), lines]

    def rows_to(d):
        to = ring(y, d)
        lines = pl.ds(pl.multiple_of(z // 2 * few, few), few)
        column = ((2 * core + lax.rem(z, 2)) * SIDE + to) * depth
        return remote(
            hid.at[lines, pl.ds(pl.multiple_of(column, depth), depth)], acts.at[2 * core + lax.rem(z, 2), y, lines],
            a_send.at[d], a_recv.at[d], (x * SIDE + to, head),
        )

    def rows_from(d):
        place = eighth(z, d)
        return remote(place, place, a_send.at[d], a_recv.at[d], (x * SIDE + ring(y, SIDE - d), head))

    def upward(step, d, arriving=False):
        place = eighth(lax.rem(z + levels + 1 - step - (1 if arriving else 0), levels), d)
        return remote(place, place, zr_send.at[step, d], zr_recv.at[step, d], right)

    def downward(step, d, arriving=False):
        place = eighth(lax.rem(z - 1 + step + (1 if arriving else 0), levels), d)
        return remote(place, place, zl_send.at[step, d], zl_recv.at[step, d], left)

    def goes_up(step, d):
        return step < 4 or d != LEFT

    def goes_down(step, d):
        return step < 4 or d == LEFT

    def level_step(step):
        for d in steps:
            if step == 1:
                rows_from(d).wait_recv()
            else:
                upward(step - 1, d, True).wait_recv()
            if goes_up(step, d):
                upward(step, d).start()
            if step > 1:
                downward(step - 1, d, True).wait_recv()
            if goes_down(step, d):
                downward(step, d).start()

    def hop1(o):
        to = lax.rem(me + o, owners)
        return remote(
            store_hbm.at[:, to, core], hop_in.at[pl.ds(me * 8, 8)], h1_send.at[o], h1_recv.at[me], (to, head)
        )

    def hop1_from(o):
        src = lax.rem(me + owners - o, owners)
        return remote(
            store_hbm.at[:, src, core], hop_in.at[pl.ds(src * 8, 8)], h1_send.at[o], h1_recv.at[src], (src, head)
        )

    def hop2(o):
        to = lax.rem(me + o, owners)
        return remote(hop_out.at[to], blocks.at[:, me, core], h2_send.at[o], h2_recv.at[me], (to, head))

    def hop2_from(o):
        src = lax.rem(me + owners - o, owners)
        return remote(hop_out.at[src], blocks.at[:, src, core], h2_send.at[o], h2_recv.at[src], (src, head))

    class Ring4:
        def __init__(self, source, place, send_sem, recv_sem):
            self.source, self.place, self.send_sem, self.recv_sem = source, place, send_sem, recv_sem
            self.deep = place(0).shape[0] // 2

        def part(self, ref, half):
            return ref.at[pl.ds(half * self.deep, self.deep)]

        def copy(self, d, half, passed=False):
            to = (ring(x, d) * SIDE + y, head)
            src = self.part(self.place(ring(x, SIDE - d)) if passed else self.source, half)
            dst = self.part(self.place(ring(x, SIDE - d) if passed else x), half)
            k = OPPOSITE if passed else d
            return remote(src, dst, self.send_sem.at[k, half], self.recv_sem.at[k, half], to)

        def wait(self, d, half):
            place = self.part(self.place(ring(x, SIDE - d)), half)
            remote(
                place, place, self.send_sem.at[d, half], self.recv_sem.at[d, half],
                (ring(x, SIDE - d) * SIDE + y, head),
            ).wait_recv()

        def start(self):
            self.copy(RIGHT, 0).start()
            self.copy(LEFT, 1).start()

        def rest(self):
            self.copy(RIGHT, 1).start()
            self.copy(LEFT, 0).start()

        def forward(self):
            self.wait(RIGHT, 0)
            self.copy(RIGHT, 0, True).start()
            self.wait(LEFT, 1)
            self.copy(LEFT, 1, True).start()

        def wait_rest(self):
            self.wait(RIGHT, 1)
            self.wait(LEFT, 0)

        def wait_opposite(self):
            self.wait(OPPOSITE, 0)
            self.wait(OPPOSITE, 1)

        def finish(self):
            for half in (0, 1):
                self.copy(RIGHT, half).wait_send()
                self.copy(LEFT, half).wait_send()
            self.copy(RIGHT, 0, True).wait_send()
            self.copy(LEFT, 1, True).wait_send()

    weights = Ring4(w.at[x], lambda i: w.at[i], w_send, w_recv)
    ow_blocks = Ring4(ow_hbm, lambda i: ow.at[core, i], o_send, o_recv)

    steps = (RIGHT, LEFT, OPPOSITE)
    own_q.wait()
    own_kv.wait()
    weights.start()

    @pl.loop(1, owners)
    def _(o):
        hop1(o).start()

    own_hid.wait()
    tall = 16

    @pl.loop(0, rows // tall)
    def _(i):
        lines = pl.ds(pl.multiple_of(i * tall, tall), tall)
        total = jnp.zeros((tall, 1), F32)
        for c in range(owners):
            v = hid[lines, c * depth : (c + 1) * depth].astype(F32)
            total += jnp.sum(v * v, axis=-1, keepdims=True)
        factor = lax.rsqrt(total / (owners * depth) + 1e-06)
        for c in range(owners):
            v = hid[lines, c * depth : (c + 1) * depth].astype(F32)
            g = gain_ref[c * depth : (c + 1) * depth].astype(F32).reshape(1, depth)
            hid[lines, c * depth : (c + 1) * depth] = (v * factor * g).astype(BF16)

    for d in steps:
        rows_to(d).start()
    weights.rest()

    for i in range(SIDE):
        pltpu.make_async_copy(slice_of(i * SIDE + y), acts.at[i, y], loc.at[5 + i]).start()

    def place_of(i, r):
        return table_ref[req_ref[i, r]]

    my_owner = [place_of(me, r) // 8 for r in range(8)]
    my_rank = [sum([(my_owner[q] == my_owner[r]).astype(jnp.int32) for q in range(r)], 0) for r in range(8)]

    def find(n, found):
        here = place_of(n // 8, lax.rem(n, 8)) - me * 8
        return tuple(jnp.where(here == s, n, found[s]) for s in range(8))

    found = lax.fori_loop(0, owners * 8, find, (jnp.int32(0),) * 8)
    my_rows[...] = jnp.full_like(my_rows, -1)
    slot_rows[...] = jnp.full_like(slot_rows, -1)
    my_rows[:, 0:per] = rec_ref[me]
    picks = []
    for s in range(8):
        i, r = found[s] // 8, lax.rem(found[s], 8)
        slot_rows[s : s + 1, 0:per] = rec_ref[i, pl.ds(r, 1), :]
        rank = sum([((q < r) & (place_of(i, q) // 8 == me)).astype(jnp.int32) for q in range(8)], 0)
        picks.append(2 * i + jnp.minimum(rank, 1))

    level_step(1)
    weights.forward()

    level_step(2)

    own_hop.wait()

    @pl.loop(1, owners)
    def _(o):
        hop1_from(o).wait_recv()

    @pl.loop(0, owners)
    def _(i):
        for r in range(8):
            hop_out[i, r] = hop_in[place_of(i, r)]

    @pl.loop(1, owners)
    def _(o):
        hop2(o).start()

    own_out = pltpu.make_async_copy(hop_out.at[me], blocks.at[:, me, core], loc.at[4])
    own_out.start()

    level_step(3)
    level_step(4)
    for d in steps:
        if goes_up(4, d):
            upward(4, d, True).wait_recv()
        if goes_down(4, d):
            downward(4, d, True).wait_recv()

    def rows_over(d, i, which):
        place = acts.at[2 * which + i, ring(y, SIDE - d)]
        return remote(place, place, c_send.at[d, i], c_recv.at[d, i], partner)

    for i in (0, 1):
        for d in steps:
            rows_over(d, i, core).start()

    for i in range(SIDE):
        pltpu.make_async_copy(slice_of(i * SIDE + y), acts.at[i, y], loc.at[5 + i]).wait()
    weights.wait_rest()
    weights.wait_opposite()

    def product(i, j):
        return jnp.dot(acts[i, j], w[i], preferred_element_type=F32)

    @pl.loop(0, SIDE)
    def _(j):
        acc[j] = product(2 * core, j)
        acc[j] += product(2 * core + 1, j)

    for i in (0, 1):
        for d in steps:
            rows_over(d, i, 1 - core).wait_recv()

    def sums_to(d):
        to = ring(y, d)
        return remote(part.at[d], sums.at[d], s_send.at[d], s_recv.at[d], (x * SIDE + to, head))

    for d in (OPPOSITE, RIGHT, LEFT):
        j = ring(y, d)
        acc[j] += product(2 - 2 * core, j)
        part[d] = (acc[j] + product(3 - 2 * core, j)).astype(BF16)
        sums_to(d).start()

    def block_from(d, which):
        place = ow.at[which, ring(x, SIDE - d)]
        return remote(place, place, oo_send.at[d], oo_recv.at[d], partner)

    ow_blocks.start()
    ow_blocks.rest()
    own_ow.wait()
    block_from(0, core).start()
    acc[y] += product(2 - 2 * core, y)
    acc[y] += product(3 - 2 * core, y)

    def core_swap(which):
        return remote(
            blocks.at[:, :, which], blocks.at[:, :, which], x_send.at[0], x_recv.at[0], partner
        )

    own_out.wait()

    @pl.loop(1, owners)
    def _(o):
        hop2_from(o).wait_recv()

    core_swap(core).start()

    for d in steps:
        remote(part.at[d], sums.at[d], s_send.at[d], s_recv.at[d], (x * SIDE + ring(y, SIDE - d), head)).wait_recv()
        acc[y] += sums[d].astype(F32)

    heads = q_cols // hd
    bias = qb_ref[...].astype(F32).reshape(1, q_cols)
    both = kvb_ref[pl.ds(pl.multiple_of(z * 2 * hd, 2 * hd), 2 * hd)].astype(F32).reshape(1, 2 * hd)
    kv_bias = jnp.where(core == 0, both[:, 0:hd], both[:, hd:])
    for r in range(8):
        lines = slice(per * r, per * (r + 1))
        for j in range(heads):
            at_row = (r * heads + j) * per
            qs[at_row : at_row + per, :] = acc[y, lines, j * hd : (j + 1) * hd] + bias[:, j * hd : (j + 1) * hd]
        fpad[r * PAD : r * PAD + per, :] = acc[y, lines, q_cols:width] + kv_bias
        fpad[r * PAD + per : (r + 1) * PAD, :] = jnp.zeros((PAD - per, hd), F32)
    own_fresh[...] = fpad[...].astype(BF16).reshape(own_fresh.shape)
    fresh[core] = own_fresh[...]
    swap = remote(own_fresh, fresh.at[core], x_send.at[1], x_recv.at[1], partner)
    swap.start()
    queries[...] = qs[...].astype(BF16)

    @pl.loop(0, owners)
    def _(o):
        for m in range(2):
            row = sum([jnp.where((my_owner[r] == o) & (my_rank[r] == m), r, 0) for r in range(8)], 0)
            f_out[2 * o + m] = own_fresh[row]

    def give(o):
        to = lax.rem(me + o, owners)
        return remote(
            f_out.at[pl.ds(2 * to, 2)], f_in.at[pl.ds(2 * me, 2)], f_send.at[o], f_recv.at[me], (to, head)
        )

    def take(o):
        src = lax.rem(me + owners - o, owners)
        return remote(
            f_out.at[pl.ds(2 * src, 2)], f_in.at[pl.ds(2 * src, 2)], f_send.at[o], f_recv.at[src], (src, head)
        )

    @pl.loop(1, owners)
    def _(o):
        give(o).start()

    for m in range(2):
        f_in[2 * me + m] = f_out[2 * me + m]

    core_swap(1 - core).wait_recv()
    remote(fresh.at[1 - core], fresh.at[1 - core], x_send.at[1], x_recv.at[1], partner).wait_recv()

    attend(queries, fresh, blocks, my_rows, ctx, ks, vs, sc, top, low, res, flat)

    def ctx_to(d):
        to = ring(y, d)
        return remote(
            ctx, ctxs.at[y // 2, core], t_send.at[d], t_recv.at[d, core], (x * SIDE + to, 2 * z + lax.rem(y, 2))
        )

    def ctx_from(d, which):
        src = ring(y, SIDE - d)
        place = ctxs.at[src // 2, which]
        return remote(place, place, t_send.at[d], t_recv.at[d, which], (x * SIDE + src, 2 * z + which))

    for d in (RIGHT, LEFT, OPPOSITE):
        ctx_to(d).start()

    mine = lax.rem(y, 2) == core

    @pl.when(mine)
    def _():
        ctxs[y // 2, core] = ctx[...]

    @pl.when(jnp.logical_not(mine))
    def _():
        ctx_to(0).start()

    ow_blocks.forward()
    ow_blocks.wait_rest()
    block_from(RIGHT, core).start()
    block_from(LEFT, core).start()

    @pl.loop(1, owners)
    def _(o):
        take(o).wait_recv()

    for s in range(8):
        back[core, s] = f_in[picks[s]]
    swap_back = remote(back.at[core], back.at[core], x_send.at[2], x_recv.at[2], partner)
    swap_back.start()

    @pl.when(mine)
    def _():
        ctx_from(0, 1 - core).wait_recv()
        for which in (0, 1):
            ctx_from(OPPOSITE, which).wait_recv()

    @pl.when(jnp.logical_not(mine))
    def _():
        for d in (RIGHT, LEFT):
            for which in (0, 1):
                ctx_from(d, which).wait_recv()

    ow_blocks.wait_opposite()
    block_from(OPPOSITE, core).start()
    for d in (0,) + steps:
        block_from(d, 1 - core).wait_recv()

    hrow = rows // 2
    order = (4, 3, -3, 2, -2, 1, -1, 0)

    def compute(n):
        target = lax.rem(z + order[n] + levels, levels)
        column, request = target // 2, lax.rem(target, 2)
        chunk[n] = jnp.dot(ctxs[request, 0], ow[0, column], preferred_element_type=F32)
        chunk[n] += jnp.dot(ctxs[request, 1], ow[1, column], preferred_element_type=F32)

    def lines_of(half):
        return slice(half * hrow, (half + 1) * hrow)

    def ring_copy(step, half, out, into, send_sem, recv_sem, to):
        return remote(
            out.at[step, pl.ds(half * hrow, hrow)],
            into.at[step, pl.ds(half * hrow, hrow)],
            send_sem.at[step, half],
            recv_sem.at[step, half],
            to,
        )

    def rightward(step, half):
        return ring_copy(step, half, r_out, r_in, r_send, r_recv, right)

    def leftward(step, half):
        return ring_copy(step, half, l_out, l_in, l_send, l_recv, left)

    def renew(s):
        keys, values = blend(old[s].reshape(new.shape[1], 2 * hd), back[0, s], back[1, s], slot_rows[s : s + 1, 0:PAD])
        new[s, :, 0:hd] = keys
        new[s, :, hd : 2 * hd] = values
        pltpu.make_async_copy(new.at[s], new_hbm.at[s], n_sem.at[s]).start()

    compute(0)
    r_out[0, lines_of(0), :] = chunk[0, lines_of(0), :].astype(BF16)
    rightward(0, 0).start()
    l_out[0, lines_of(1), :] = chunk[0, lines_of(1), :].astype(BF16)
    leftward(0, 1).start()
    compute(1)
    compute(2)
    for step in (1, 2, 3):
        n_right, n_left = 2 * step - 1, 2 * step
        halves = ((1, 0), (0, 1)) if step == 1 else ((0, 1), (1, 0))
        for right_half, left_half in halves:
            value = chunk[n_right, lines_of(right_half), :]
            if step > 1 or right_half == 0:
                rightward(step - 1, right_half).wait_recv()
                value += r_in[step - 1, lines_of(right_half), :].astype(F32)
            r_out[step, lines_of(right_half), :] = value.astype(BF16)
            rightward(step, right_half).start()
            value = chunk[n_left, lines_of(left_half), :]
            if step > 1 or left_half == 1:
                leftward(step - 1, left_half).wait_recv()
                value += l_in[step - 1, lines_of(left_half), :].astype(F32)
            l_out[step, lines_of(left_half), :] = value.astype(BF16)
            leftward(step, left_half).start()
        if step == 1:
            old_in.wait()
            remote(back.at[1 - core], back.at[1 - core], x_send.at[2], x_recv.at[2], partner).wait_recv()
        if step < 3:
            compute(2 * step + 1)
            compute(2 * step + 2)
            for s in range(4 * step - 4, 4 * step):
                renew(s)
        else:
            compute(7)

    def flip(half):
        return remote(
            done.at[pl.ds(half * hrow, hrow)], out_ref.at[pl.ds(half * hrow, hrow)],
            x_send.at[3 + half], x_recv.at[3 + half], mirror,
        )

    for half in (0, 1):
        rightward(3, half).wait_recv()
        leftward(3, half).wait_recv()
        value = chunk[7, lines_of(half), :] + r_in[3, lines_of(half), :].astype(F32)
        value += l_in[3, lines_of(half), :].astype(F32)
        done[lines_of(half), :] = value.astype(BF16)

        @pl.when(turn != y)
        def _():
            flip(half).start()

    @pl.when(turn == y)
    def _():
        out_ref[...] = done[...]

    for i in (0, 1):
        for d in steps:
            rows_over(d, i, core).wait_send()
    for d in steps:
        rows_to(d).wait_send()
        for step in (1, 2, 3, 4):
            if goes_up(step, d):
                upward(step, d).wait_send()
            if goes_down(step, d):
                downward(step, d).wait_send()
    for d in steps:
        sums_to(d).wait_send()
        ctx_to(d).wait_send()
    weights.finish()
    ow_blocks.finish()
    for d in (0,) + steps:
        block_from(d, core).wait_send()

    @pl.when(jnp.logical_not(mine))
    def _():
        ctx_to(0).wait_send()

    @pl.loop(1, owners)
    def _(o):
        hop1(o).wait_send()
        hop2(o).wait_send()
        give(o).wait_send()

    core_swap(core).wait_send()
    swap.wait_send()
    swap_back.wait_send()
    rightward(0, 0).wait_send()
    leftward(0, 1).wait_send()
    for step in (1, 2, 3):
        for half in (0, 1):
            rightward(step, half).wait_send()
            leftward(step, half).wait_send()
    for s in range(8):
        pltpu.make_async_copy(new.at[s], new_hbm.at[s], n_sem.at[s]).wait()

    @pl.when(turn != y)
    def _():
        for half in (0, 1):
            flip(half).wait()


def hand_over(out_ref, store_ref, out_copy, store_copy, out_held, held, sem_in, sem_out):
    count = store_ref.shape[0]
    ins = [pltpu.make_async_copy(store_ref.at[s], held.at[s], sem_in.at[s]) for s in range(count)]
    ins.append(pltpu.make_async_copy(out_ref, out_held, sem_in.at[count]))
    outs = [pltpu.make_async_copy(held.at[s], store_copy.at[s, 0], sem_out.at[s]) for s in range(count)]
    outs.append(pltpu.make_async_copy(out_held, out_copy, sem_out.at[count]))
    for copy in ins:
        copy.start()
    for copy_in, copy_out in zip(ins, outs):
        copy_in.wait()
        copy_out.start()
    for copy in outs:
        copy.wait()


def shards(
    hidden, norm_gain, q_weight, q_bias, kv_weight, kv_bias, out_weight, kv_store, stretch_place, req_stretches, rec_rows
):
    owners = lax.axis_size("cache")
    me = lax.axis_index("cache")
    rows, width = hidden.shape
    stretches, _, length, kv_width = kv_store.shape
    hd = kv_width // 2
    per = rec_rows.shape[2]
    depth, q_cols = q_weight.shape
    levels = lax.axis_size("heads") // 2
    heads = q_cols // hd
    vmem = pl.BlockSpec(memory_space=pltpu.VMEM)
    smem = pl.BlockSpec(memory_space=pltpu.SMEM)
    hbm = pl.BlockSpec(memory_space=pl.ANY)
    dma = pltpu.SemaphoreType.DMA

    store = kv_store.reshape(stretches, owners, 2, length // (2 * owners), kv_width)
    piece = length // (2 * owners)

    attn_out, new_store = pl.pallas_call(
        prefill,
        out_shape=(
            jax.ShapeDtypeStruct((rows, q_cols), BF16),
            jax.ShapeDtypeStruct((stretches, length, kv_width), BF16),
        ),
        in_specs=[smem, smem, hbm, vmem, hbm, hbm, vmem, vmem, hbm, hbm, vmem],
        out_specs=(vmem, hbm),
        scratch_shapes=[
            pltpu.VMEM((rows, width), BF16),
            pltpu.VMEM((SIDE, SIDE, rows, depth), BF16),
            pltpu.VMEM((SIDE, depth, q_cols + hd), BF16),
            pltpu.VMEM((SIDE, rows, q_cols + hd), F32),
            pltpu.VMEM((SIDE, rows, q_cols + hd), BF16),
            pltpu.VMEM((SIDE, rows, q_cols + hd), BF16),
            pltpu.VMEM((owners * stretches, piece, kv_width), BF16),
            pltpu.VMEM((owners, stretches, piece, kv_width), BF16),
            pltpu.VMEM((rows * heads, hd), F32),
            pltpu.VMEM((stretches * PAD, hd), F32),
            pltpu.VMEM((stretches, hd), jnp.int32),
            pltpu.VMEM((stretches, hd), jnp.int32),
            pltpu.VMEM((rows * heads, hd), BF16),
            pltpu.VMEM((stretches, PAD, hd), BF16),
            pltpu.VMEM((2, stretches, PAD, hd), BF16),
            pltpu.VMEM((stretches, owners, 2, piece, kv_width), BF16),
            pltpu.VMEM((stretches, length, hd), BF16),
            pltpu.VMEM((stretches, length, hd), BF16),
            pltpu.VMEM((rows * heads * (stretches + 1) // 2, length), F32),
            pltpu.VMEM((rows * heads, hd), F32),
            pltpu.VMEM((rows * heads, hd), F32),
            pltpu.VMEM((rows * heads, hd), F32),
            pltpu.VMEM((rows, q_cols), F32),
            pltpu.VMEM((rows, q_cols), BF16),
            pltpu.VMEM((2, SIDE, depth, q_cols), BF16),
            pltpu.VMEM((2, 2, rows, q_cols), BF16),
            pltpu.VMEM((levels, rows, q_cols), F32),
            pltpu.VMEM((4, rows, q_cols), BF16),
            pltpu.VMEM((4, rows, q_cols), BF16),
            pltpu.VMEM((4, rows, q_cols), BF16),
            pltpu.VMEM((4, rows, q_cols), BF16),
            pltpu.VMEM((rows, q_cols), BF16),
            pltpu.VMEM((2 * owners, PAD, hd), BF16),
            pltpu.VMEM((2 * owners, PAD, hd), BF16),
            pltpu.VMEM((2, stretches, PAD, hd), BF16),
            pltpu.VMEM((stretches, owners, 2, piece, kv_width), BF16),
            pltpu.VMEM((stretches, length, kv_width), BF16),
            dma((7 + SIDE,)),
            dma((SIDE, 2)),
            dma((SIDE, 2)),
            dma((SIDE,)),
            dma((SIDE,)),
            dma((SIDE + 1, SIDE)),
            dma((SIDE + 1, SIDE)),
            dma((SIDE + 1, SIDE)),
            dma((SIDE + 1, SIDE)),
            dma((SIDE, 2)),
            dma((SIDE, 2)),
            dma((SIDE,)),
            dma((SIDE,)),
            dma((owners,)),
            dma((owners,)),
            dma((owners,)),
            dma((owners,)),
            dma((5,)),
            dma((5,)),
            dma((SIDE, 2)),
            dma((SIDE, 2)),
            dma((SIDE,)),
            dma((SIDE,)),
            dma((SIDE,)),
            dma((SIDE, 2)),
            dma((4, 2)),
            dma((4, 2)),
            dma((4, 2)),
            dma((4, 2)),
            dma((owners,)),
            dma((owners,)),
            dma((8,)),
        ],
        compiler_params=pltpu.CompilerParams(collective_id=0, has_side_effects=True, vmem_limit_bytes=58 << 20),
        name="prefill",
    )(
        stretch_place, req_stretches, hidden, norm_gain, q_weight, kv_weight, q_bias, kv_bias, out_weight, store, rec_rows
    )
    return pl.pallas_call(
        hand_over,
        out_shape=(
            jax.ShapeDtypeStruct((rows, q_cols), BF16),
            jax.ShapeDtypeStruct((stretches, 1, length, kv_width), BF16),
        ),
        in_specs=[hbm, hbm],
        out_specs=(hbm, hbm),
        scratch_shapes=[
            pltpu.VMEM((rows, q_cols), BF16),
            pltpu.VMEM((stretches, length, kv_width), BF16),
            dma((stretches + 1,)),
            dma((stretches + 1,)),
        ],
        name="hand_over",
    )(attn_out, new_store)


def solution(mesh):
    placed = (
        P("cache", None),
        P(),
        P("cache", "heads"),
        P("heads"),
        P("cache", None),
        P(),
        P("heads", "cache"),
        P("cache", "heads", None, None),
        P(),
        P(),
        P(),
    )
    return jax.shard_map(
        shards,
        mesh=mesh,
        in_specs=placed,
        out_specs=(P("cache", "heads"), P("cache", "heads", None, None)),
        check_vma=False,
    )
```

```python
import functools
import math

import jax
import jax.numpy as jnp
from jax import lax
from jax.experimental import pallas as pl
from jax.experimental.pallas import tpu as pltpu
from jax.sharding import PartitionSpec as P

MESH = pl.DeviceIdType.MESH
SIDE = 4
BF16 = jnp.bfloat16
F32 = jnp.float32
RIGHT, OPPOSITE, LEFT = 1, 2, 3
PAD = 32


def remote(src, dst, send_sem, recv_sem, device):
    return pltpu.make_async_remote_copy(
        src_ref=src, dst_ref=dst, send_sem=send_sem, recv_sem=recv_sem, device_id=device, device_id_type=MESH
    )


def blend(old, keys, values, rows):
    hd = keys.shape[1]
    hit = lax.broadcasted_iota(jnp.int32, (old.shape[0], PAD), 0) == rows
    table = jnp.concatenate([keys, values, jnp.ones((PAD, hd), BF16)], axis=1)
    new = jnp.dot(hit.astype(F32).astype(BF16), table, preferred_element_type=F32)
    there = new[:, 2 * hd :] > 0.5
    parts = [
        jnp.where(there, new[:, i * hd : (i + 1) * hd], old[:, i * hd : (i + 1) * hd].astype(F32)).astype(BF16)
        for i in (0, 1)
    ]
    return parts[0], parts[1]


def attend(q_ref, fresh_ref, blocks_ref, row_ref, ctx_ref, ks, vs, sc, top, low, out, flat):
    stretches, length = ks.shape[0], ks.shape[1]
    hd = q_ref.shape[1]
    total = q_ref.shape[0]
    group = total // stretches
    heads = ctx_ref.shape[1] // hd
    per = group // heads
    scale = math.log2(math.e) / math.sqrt(hd)
    for r in range(stretches):
        old = blocks_ref[r].reshape(length, 2 * hd)
        ks[r], vs[r] = blend(old, fresh_ref[0, r], fresh_ref[1, r], row_ref[r : r + 1, 0:PAD])
    top[...] = jnp.full_like(top, -jnp.inf)
    low[...] = jnp.zeros_like(low)
    out[...] = jnp.zeros_like(out)

    def fold(a, op):
        parts = [a[:, i * hd : (i + 1) * hd] for i in range(length // hd)]
        while len(parts) > 1:
            parts = [op(parts[i], parts[i + 1]) for i in range(0, len(parts), 2)]
        return parts[0]

    columns = jnp.transpose(row_ref[...].astype(F32))
    base = [sum(total - t * group for t in range(s)) for s in range(stretches)]
    for s in range(stretches):
        scores = lax.dot_general(
            q_ref[s * group :, :], ks[s], (((1,), (1,)), ((), ())), preferred_element_type=F32
        )
        key = lax.broadcasted_iota(jnp.int32, (group, length), 1).astype(F32)
        last = jnp.concatenate([columns[0:per, s : s + 1]] * heads, axis=0)
        first = jnp.where(key <= last, scores[:group], -jnp.inf)
        sc[base[s] : base[s] + group, :] = first
        top[s * group : (s + 1) * group, :] = jnp.maximum(
            top[s * group : (s + 1) * group, :], fold(first, jnp.maximum)
        )
        if s + 1 < stretches:
            sc[base[s] + group : base[s] + total - s * group, :] = scores[group:]
            top[(s + 1) * group :, :] = jnp.maximum(top[(s + 1) * group :, :], fold(scores[group:], jnp.maximum))
    top[...] = jnp.broadcast_to(jnp.max(top[...], axis=1, keepdims=True), top.shape)
    for s in range(stretches):
        here = slice(s * group, total)
        held = slice(base[s], base[s] + total - s * group)
        peak = top[here, :]
        expon = jnp.concatenate(
            [jnp.exp2((sc[held, i * hd : (i + 1) * hd] - peak) * scale) for i in range(length // hd)], axis=1
        )
        low[here, :] += fold(expon, jnp.add)
        out[here, :] += jnp.dot(expon.astype(BF16), vs[s], preferred_element_type=F32)
    out[...] = out[...] / jnp.sum(low[...], axis=1, keepdims=True)
    for r in range(stretches):
        for j in range(heads):
            at_row = (r * heads + j) * per
            flat[r * per : (r + 1) * per, j * hd : (j + 1) * hd] = out[at_row : at_row + per, :]
    ctx_ref[...] = flat[...].astype(BF16)


def prefill(
    table_ref, req_ref, hid_hbm, gain_ref, qw_hbm, kvw_hbm, qb_ref, kvb_ref, ow_hbm, store_hbm, rec_ref,
    out_ref, new_hbm,
    hid, acts, w, acc, part, sums, hop_in, hop_out, qs, fpad, my_rows, slot_rows,
    queries, own_fresh, fresh, blocks, ks, vs, sc, top, low, res, flat, ctx,
    ow, ctxs, chunk, r_out, l_out, r_in, l_in, done, f_out, f_in, back, old, new,
    loc, w_send, w_recv, a_send, a_recv, zr_send, zr_recv, zl_send, zl_recv, c_send, c_recv, s_send, s_recv,
    h1_send, h1_recv, h2_send, h2_recv, k_send, k_recv, x_send, x_recv,
    o_send, o_recv, oo_send, oo_recv, t_send, t_recv,
    r_send, r_recv, l_send, l_recv, f_send, f_recv, n_sem,
):
    me = lax.axis_index("cache")
    head = lax.axis_index("heads")
    core = lax.rem(head, 2)
    partner = (me, head + 1 - 2 * core)
    x, y = me // SIDE, lax.rem(me, SIDE)
    z = head // 2
    owners = SIDE * SIDE
    levels = lax.axis_size("heads") // 2
    right = (me, lax.rem(z + 1, levels) * 2 + core)
    left = (me, lax.rem(z + levels - 1, levels) * 2 + core)
    goal = (lax.rem(head, SIDE) * SIDE + y, x * SIDE + head // SIDE)
    origin = (head // SIDE * SIDE + y, lax.rem(head, SIDE) * SIDE + x)
    stays = (goal[0] == me) & (goal[1] == head)
    rows = hid.shape[0]
    depth, width = w.shape[1], w.shape[2]
    q_cols = qw_hbm.shape[1]
    hd = width - q_cols
    per = rows // 8

    def ring(i, d):
        return lax.rem(i + d, SIDE)

    own_hid = pltpu.make_async_copy(hid_hbm, hid, loc.at[2])
    own_q = pltpu.make_async_copy(qw_hbm, w.at[x, :, 0:q_cols], loc.at[0])
    own_kv = pltpu.make_async_copy(
        kvw_hbm.at[:, pl.ds(pl.multiple_of(head * hd, hd), hd)], w.at[x, :, q_cols:width], loc.at[1]
    )
    own_hop = pltpu.make_async_copy(store_hbm.at[:, me, core], hop_in.at[pl.ds(me * 8, 8)], loc.at[3])
    own_hid.start()
    own_q.start()
    own_kv.start()
    own_hop.start()
    own_ow = pltpu.make_async_copy(ow_hbm, ow.at[core, y], loc.at[5 + SIDE])
    own_ow.start()
    old_in = pltpu.make_async_copy(store_hbm, old, loc.at[6 + SIDE])
    old_in.start()

    barrier = pltpu.get_barrier_semaphore()

    @pl.loop(1, owners)
    def _(o):
        pl.semaphore_signal(barrier, inc=1, device_id=(lax.rem(me + o, owners), head), device_id_type=MESH)

    for peer in (partner, left, right):
        pl.semaphore_signal(barrier, inc=1, device_id=peer, device_id_type=MESH)
    for d in (RIGHT, OPPOSITE, LEFT):
        across = (ring(x, d) * SIDE + y, head + 1 - 2 * core)
        pl.semaphore_signal(barrier, inc=1, device_id=across, device_id_type=MESH)

    @pl.when(jnp.logical_not(stays))
    def _():
        pl.semaphore_signal(barrier, inc=1, device_id=origin, device_id_type=MESH)
        pl.semaphore_wait(barrier, owners + 6)

    @pl.when(stays)
    def _():
        pl.semaphore_wait(barrier, owners + 5)

    def slice_of(c):
        return hid.at[:, pl.ds(pl.multiple_of(c * depth, depth), depth)]

    few = rows // 4

    def eighth(level, d):
        lines = pl.ds(pl.multiple_of(level // 2 * few, few), few)
        return acts.at[2 * core + lax.rem(level, 2), ring(y, SIDE - d), lines]

    def rows_to(d):
        to = ring(y, d)
        lines = pl.ds(pl.multiple_of(z // 2 * few, few), few)
        column = ((2 * core + lax.rem(z, 2)) * SIDE + to) * depth
        return remote(
            hid.at[lines, pl.ds(pl.multiple_of(column, depth), depth)], acts.at[2 * core + lax.rem(z, 2), y, lines],
            a_send.at[d], a_recv.at[d], (x * SIDE + to, head),
        )

    def rows_from(d):
        place = eighth(z, d)
        return remote(place, place, a_send.at[d], a_recv.at[d], (x * SIDE + ring(y, SIDE - d), head))

    def upward(step, d, arriving=False):
        place = eighth(lax.rem(z + levels + 1 - step - (1 if arriving else 0), levels), d)
        return remote(place, place, zr_send.at[step, d], zr_recv.at[step, d], right)

    def downward(step, d, arriving=False):
        place = eighth(lax.rem(z - 1 + step + (1 if arriving else 0), levels), d)
        return remote(place, place, zl_send.at[step, d], zl_recv.at[step, d], left)

    def goes_up(step, d):
        return step < 4 or d != LEFT

    def goes_down(step, d):
        return step < 4 or d == LEFT

    def level_step(step):
        for d in steps:
            if step == 1:
                rows_from(d).wait_recv()
            else:
                upward(step - 1, d, True).wait_recv()
            if goes_up(step, d):
                upward(step, d).start()
            if step > 1:
                downward(step - 1, d, True).wait_recv()
            if goes_down(step, d):
                downward(step, d).start()

    def hop1(o):
        to = lax.rem(me + o, owners)
        return remote(
            store_hbm.at[:, to, core], hop_in.at[pl.ds(me * 8, 8)], h1_send.at[o], h1_recv.at[me], (to, head)
        )

    def hop1_from(o):
        src = lax.rem(me + owners - o, owners)
        return remote(
            store_hbm.at[:, src, core], hop_in.at[pl.ds(src * 8, 8)], h1_send.at[o], h1_recv.at[src], (src, head)
        )

    def hop2(o):
        to = lax.rem(me + o, owners)
        return remote(hop_out.at[to], blocks.at[:, me, core], h2_send.at[o], h2_recv.at[me], (to, head))

    def hop2_from(o):
        src = lax.rem(me + owners - o, owners)
        return remote(hop_out.at[src], blocks.at[:, src, core], h2_send.at[o], h2_recv.at[src], (src, head))

    class Ring4:
        def __init__(self, source, place, send_sem, recv_sem, axis):
            self.source, self.place, self.send_sem, self.recv_sem = source, place, send_sem, recv_sem
            self.axis, self.here = axis, (x, y)[axis]
            self.deep = place(0).shape[0] // 2

        def device(self, d):
            return ((ring(x, d) * SIDE + y, x * SIDE + ring(y, d))[self.axis], head)

        def part(self, ref, half):
            return ref.at[pl.ds(half * self.deep, self.deep)]

        def copy(self, d, half, passed=False):
            before = ring(self.here, SIDE - d)
            src = self.part(self.place(before) if passed else self.source, half)
            dst = self.part(self.place(before if passed else self.here), half)
            k = OPPOSITE if passed else d
            return remote(src, dst, self.send_sem.at[k, half], self.recv_sem.at[k, half], self.device(d))

        def wait(self, d, half):
            place = self.part(self.place(ring(self.here, SIDE - d)), half)
            remote(
                place, place, self.send_sem.at[d, half], self.recv_sem.at[d, half], self.device(SIDE - d)
            ).wait_recv()

        def start(self):
            self.copy(RIGHT, 0).start()
            self.copy(LEFT, 1).start()

        def rest(self):
            self.copy(RIGHT, 1).start()
            self.copy(LEFT, 0).start()

        def forward(self):
            self.wait(RIGHT, 0)
            self.copy(RIGHT, 0, True).start()
            self.wait(LEFT, 1)
            self.copy(LEFT, 1, True).start()

        def wait_rest(self):
            self.wait(RIGHT, 1)
            self.wait(LEFT, 0)

        def wait_opposite(self):
            self.wait(OPPOSITE, 0)
            self.wait(OPPOSITE, 1)

        def finish(self):
            for half in (0, 1):
                self.copy(RIGHT, half).wait_send()
                self.copy(LEFT, half).wait_send()
            self.copy(RIGHT, 0, True).wait_send()
            self.copy(LEFT, 1, True).wait_send()

    weights = Ring4(w.at[x], lambda i: w.at[i], w_send, w_recv, 0)
    ow_blocks = Ring4(ow_hbm, lambda i: ow.at[core, i], o_send, o_recv, 1)

    steps = (RIGHT, LEFT, OPPOSITE)
    own_q.wait()
    own_kv.wait()
    weights.start()
    ow_blocks.start()

    @pl.loop(1, owners)
    def _(o):
        hop1(o).start()

    own_hid.wait()
    tall = 16

    @pl.loop(0, rows // tall)
    def _(i):
        lines = pl.ds(pl.multiple_of(i * tall, tall), tall)
        total = jnp.zeros((tall, 1), F32)
        for c in range(owners):
            v = hid[lines, c * depth : (c + 1) * depth].astype(F32)
            total += jnp.sum(v * v, axis=-1, keepdims=True)
        factor = lax.rsqrt(total / (owners * depth) + 1e-06)
        for c in range(owners):
            v = hid[lines, c * depth : (c + 1) * depth].astype(F32)
            g = gain_ref[c * depth : (c + 1) * depth].astype(F32).reshape(1, depth)
            hid[lines, c * depth : (c + 1) * depth] = (v * factor * g).astype(BF16)

    for d in steps:
        rows_to(d).start()
    weights.rest()
    ow_blocks.rest()

    for i in range(SIDE):
        pltpu.make_async_copy(slice_of(i * SIDE + y), acts.at[i, y], loc.at[5 + i]).start()

    def place_of(i, r):
        return table_ref[req_ref[i, r]]

    my_owner = [place_of(me, r) // 8 for r in range(8)]
    my_rank = [sum([(my_owner[q] == my_owner[r]).astype(jnp.int32) for q in range(r)], 0) for r in range(8)]

    def find(n, found):
        here = place_of(n // 8, lax.rem(n, 8)) - me * 8
        return tuple(jnp.where(here == s, n, found[s]) for s in range(8))

    found = lax.fori_loop(0, owners * 8, find, (jnp.int32(0),) * 8)
    my_rows[...] = jnp.full_like(my_rows, -1)
    slot_rows[...] = jnp.full_like(slot_rows, -1)
    my_rows[:, 0:per] = rec_ref[me]
    picks = []
    for s in range(8):
        i, r = found[s] // 8, lax.rem(found[s], 8)
        slot_rows[s : s + 1, 0:per] = rec_ref[i, pl.ds(r, 1), :]
        rank = sum([((q < r) & (place_of(i, q) // 8 == me)).astype(jnp.int32) for q in range(8)], 0)
        picks.append(2 * i + jnp.minimum(rank, 1))

    level_step(1)
    weights.forward()

    level_step(2)
    ow_blocks.forward()

    own_hop.wait()

    @pl.loop(1, owners)
    def _(o):
        hop1_from(o).wait_recv()

    @pl.loop(0, owners)
    def _(i):
        for r in range(8):
            hop_out[i, r] = hop_in[place_of(i, r)]

    @pl.loop(1, owners)
    def _(o):
        hop2(o).start()

    own_out = pltpu.make_async_copy(hop_out.at[me], blocks.at[:, me, core], loc.at[4])
    own_out.start()

    level_step(3)
    level_step(4)
    for d in steps:
        if goes_up(4, d):
            upward(4, d, True).wait_recv()
        if goes_down(4, d):
            downward(4, d, True).wait_recv()

    def rows_over(d, i, which):
        place = acts.at[2 * which + i, ring(y, SIDE - d)]
        return remote(place, place, c_send.at[d, i], c_recv.at[d, i], partner)

    for i in (0, 1):
        for d in steps:
            rows_over(d, i, core).start()

    for i in range(SIDE):
        pltpu.make_async_copy(slice_of(i * SIDE + y), acts.at[i, y], loc.at[5 + i]).wait()
    weights.wait_rest()
    weights.wait_opposite()

    def product(i, j):
        return jnp.dot(acts[i, j], w[i], preferred_element_type=F32)

    @pl.loop(0, SIDE)
    def _(j):
        acc[j] = product(2 * core, j)
        acc[j] += product(2 * core + 1, j)

    for i in (0, 1):
        for d in steps:
            rows_over(d, i, 1 - core).wait_recv()

    def sums_to(d):
        to = ring(y, d)
        return remote(part.at[d], sums.at[d], s_send.at[d], s_recv.at[d], (x * SIDE + to, head))

    for d in (OPPOSITE, RIGHT, LEFT):
        j = ring(y, d)
        acc[j] += product(2 - 2 * core, j)
        part[d] = (acc[j] + product(3 - 2 * core, j)).astype(BF16)
        sums_to(d).start()

    def block_from(d, which):
        place = ow.at[which, ring(y, SIDE - d)]
        return remote(place, place, oo_send.at[d], oo_recv.at[d], partner)

    own_ow.wait()
    block_from(0, core).start()
    acc[y] += product(2 - 2 * core, y)
    acc[y] += product(3 - 2 * core, y)

    ow_blocks.wait_rest()
    ow_blocks.wait_opposite()
    for d in steps:
        block_from(d, core).start()

    def core_piece(c, which):
        place = blocks.at[:, c, which]
        return remote(place, place, k_send.at[c], k_recv.at[c], partner)

    for d in steps:
        remote(part.at[d], sums.at[d], s_send.at[d], s_recv.at[d], (x * SIDE + ring(y, SIDE - d), head)).wait_recv()
        acc[y] += sums[d].astype(F32)

    heads = q_cols // hd
    bias = qb_ref[...].astype(F32).reshape(1, q_cols)
    both = kvb_ref[pl.ds(pl.multiple_of(z * 2 * hd, 2 * hd), 2 * hd)].astype(F32).reshape(1, 2 * hd)
    kv_bias = jnp.where(core == 0, both[:, 0:hd], both[:, hd:])
    for r in range(8):
        lines = slice(per * r, per * (r + 1))
        for j in range(heads):
            at_row = (r * heads + j) * per
            qs[at_row : at_row + per, :] = acc[y, lines, j * hd : (j + 1) * hd] + bias[:, j * hd : (j + 1) * hd]
        fpad[r * PAD : r * PAD + per, :] = acc[y, lines, q_cols:width] + kv_bias
        fpad[r * PAD + per : (r + 1) * PAD, :] = jnp.zeros((PAD - per, hd), F32)
    own_fresh[...] = fpad[...].astype(BF16).reshape(own_fresh.shape)
    fresh[core] = own_fresh[...]
    swap = remote(own_fresh, fresh.at[core], x_send.at[1], x_recv.at[1], partner)
    swap.start()
    queries[...] = qs[...].astype(BF16)

    @pl.loop(0, owners)
    def _(o):
        for m in range(2):
            row = sum([jnp.where((my_owner[r] == o) & (my_rank[r] == m), r, 0) for r in range(8)], 0)
            f_out[2 * o + m] = own_fresh[row]

    def give(o):
        to = lax.rem(me + o, owners)
        return remote(
            f_out.at[pl.ds(2 * to, 2)], f_in.at[pl.ds(2 * me, 2)], f_send.at[o], f_recv.at[me], (to, head)
        )

    def take(o):
        src = lax.rem(me + owners - o, owners)
        return remote(
            f_out.at[pl.ds(2 * src, 2)], f_in.at[pl.ds(2 * src, 2)], f_send.at[o], f_recv.at[src], (src, head)
        )

    @pl.loop(1, owners)
    def _(o):
        give(o).start()

    for m in range(2):
        f_in[2 * me + m] = f_out[2 * me + m]

    own_out.wait()
    core_piece(me, core).start()

    @pl.loop(1, owners)
    def _(o):
        hop2_from(o).wait_recv()
        core_piece(lax.rem(me + owners - o, owners), core).start()

    @pl.loop(0, owners)
    def _(c):
        core_piece(c, 1 - core).wait_recv()

    remote(fresh.at[1 - core], fresh.at[1 - core], x_send.at[1], x_recv.at[1], partner).wait_recv()

    attend(queries, fresh, blocks, my_rows, ctx, ks, vs, sc, top, low, res, flat)

    def ctx_to(d):
        return remote(
            ctx, ctxs.at[x // 2, core], t_send.at[d], t_recv.at[d, core],
            (ring(x, d) * SIDE + y, 2 * z + lax.rem(x, 2)),
        )

    def ctx_from(d, which):
        src = ring(x, SIDE - d)
        place = ctxs.at[src // 2, which]
        return remote(place, place, t_send.at[d], t_recv.at[d, which], (src * SIDE + y, 2 * z + which))

    for d in (RIGHT, LEFT, OPPOSITE):
        ctx_to(d).start()

    mine = lax.rem(x, 2) == core

    @pl.when(mine)
    def _():
        ctxs[x // 2, core] = ctx[...]

    @pl.when(jnp.logical_not(mine))
    def _():
        ctx_to(0).start()

    @pl.loop(1, owners)
    def _(o):
        take(o).wait_recv()

    for s in range(8):
        back[core, s] = f_in[picks[s]]
    swap_back = remote(back.at[core], back.at[core], x_send.at[2], x_recv.at[2], partner)
    swap_back.start()

    @pl.when(mine)
    def _():
        ctx_from(0, 1 - core).wait_recv()
        for which in (0, 1):
            ctx_from(OPPOSITE, which).wait_recv()

    @pl.when(jnp.logical_not(mine))
    def _():
        for d in (RIGHT, LEFT):
            for which in (0, 1):
                ctx_from(d, which).wait_recv()

    for d in (0,) + steps:
        block_from(d, 1 - core).wait_recv()

    hrow = rows // 2
    order = (4, 3, -3, 2, -2, 1, -1, 0)

    def compute(n):
        target = lax.rem(z + order[n] + levels, levels)
        column, request = target // 2, lax.rem(target, 2)
        chunk[n] = jnp.dot(ctxs[request, 0], ow[0, column], preferred_element_type=F32)
        chunk[n] += jnp.dot(ctxs[request, 1], ow[1, column], preferred_element_type=F32)

    def lines_of(half):
        return slice(half * hrow, (half + 1) * hrow)

    def ring_copy(step, half, out, into, send_sem, recv_sem, to):
        return remote(
            out.at[step, pl.ds(half * hrow, hrow)],
            into.at[step, pl.ds(half * hrow, hrow)],
            send_sem.at[step, half],
            recv_sem.at[step, half],
            to,
        )

    def rightward(step, half):
        return ring_copy(step, half, r_out, r_in, r_send, r_recv, right)

    def leftward(step, half):
        return ring_copy(step, half, l_out, l_in, l_send, l_recv, left)

    def renew(s):
        keys, values = blend(old[s].reshape(new.shape[1], 2 * hd), back[0, s], back[1, s], slot_rows[s : s + 1, 0:PAD])
        new[s, :, 0:hd] = keys
        new[s, :, hd : 2 * hd] = values
        pltpu.make_async_copy(new.at[s], new_hbm.at[s], n_sem.at[s]).start()

    compute(0)
    r_out[0, lines_of(0), :] = chunk[0, lines_of(0), :].astype(BF16)
    rightward(0, 0).start()
    l_out[0, lines_of(1), :] = chunk[0, lines_of(1), :].astype(BF16)
    leftward(0, 1).start()
    compute(1)
    compute(2)
    for step in (1, 2, 3):
        n_right, n_left = 2 * step - 1, 2 * step
        halves = ((1, 0), (0, 1)) if step == 1 else ((0, 1), (1, 0))
        for right_half, left_half in halves:
            value = chunk[n_right, lines_of(right_half), :]
            if step > 1 or right_half == 0:
                rightward(step - 1, right_half).wait_recv()
                value += r_in[step - 1, lines_of(right_half), :].astype(F32)
            r_out[step, lines_of(right_half), :] = value.astype(BF16)
            rightward(step, right_half).start()
            value = chunk[n_left, lines_of(left_half), :]
            if step > 1 or left_half == 1:
                leftward(step - 1, left_half).wait_recv()
                value += l_in[step - 1, lines_of(left_half), :].astype(F32)
            l_out[step, lines_of(left_half), :] = value.astype(BF16)
            leftward(step, left_half).start()
        if step == 1:
            old_in.wait()
            remote(back.at[1 - core], back.at[1 - core], x_send.at[2], x_recv.at[2], partner).wait_recv()
        if step < 3:
            compute(2 * step + 1)
            compute(2 * step + 2)
            for s in range(4 * step - 4, 4 * step):
                renew(s)
        else:
            compute(7)

    def flip(half):
        return remote(
            done.at[pl.ds(half * hrow, hrow)], out_ref.at[pl.ds(half * hrow, hrow)],
            x_send.at[3 + half], x_recv.at[3 + half], goal,
        )

    for half in (0, 1):
        rightward(3, half).wait_recv()
        leftward(3, half).wait_recv()
        value = chunk[7, lines_of(half), :] + r_in[3, lines_of(half), :].astype(F32)
        value += l_in[3, lines_of(half), :].astype(F32)
        done[lines_of(half), :] = value.astype(BF16)

        @pl.when(jnp.logical_not(stays))
        def _():
            flip(half).start()

    @pl.when(stays)
    def _():
        out_ref[...] = done[...]

    for i in (0, 1):
        for d in steps:
            rows_over(d, i, core).wait_send()
    for d in steps:
        rows_to(d).wait_send()
        for step in (1, 2, 3, 4):
            if goes_up(step, d):
                upward(step, d).wait_send()
            if goes_down(step, d):
                downward(step, d).wait_send()
    for d in steps:
        sums_to(d).wait_send()
        ctx_to(d).wait_send()
    weights.finish()
    ow_blocks.finish()
    for d in (0,) + steps:
        block_from(d, core).wait_send()

    @pl.when(jnp.logical_not(mine))
    def _():
        ctx_to(0).wait_send()

    @pl.loop(1, owners)
    def _(o):
        hop1(o).wait_send()
        hop2(o).wait_send()
        give(o).wait_send()

    @pl.loop(0, owners)
    def _(c):
        core_piece(c, core).wait_send()

    swap.wait_send()
    swap_back.wait_send()
    rightward(0, 0).wait_send()
    leftward(0, 1).wait_send()
    for step in (1, 2, 3):
        for half in (0, 1):
            rightward(step, half).wait_send()
            leftward(step, half).wait_send()
    for s in range(8):
        pltpu.make_async_copy(new.at[s], new_hbm.at[s], n_sem.at[s]).wait()

    @pl.when(jnp.logical_not(stays))
    def _():
        for half in (0, 1):
            flip(half).wait()


def hand_over(out_ref, store_ref, out_copy, store_copy, out_held, held, sem_in, sem_out):
    count = store_ref.shape[0]
    ins = [pltpu.make_async_copy(store_ref.at[s], held.at[s], sem_in.at[s]) for s in range(count)]
    ins.append(pltpu.make_async_copy(out_ref, out_held, sem_in.at[count]))
    outs = [pltpu.make_async_copy(held.at[s], store_copy.at[s, 0], sem_out.at[s]) for s in range(count)]
    outs.append(pltpu.make_async_copy(out_held, out_copy, sem_out.at[count]))
    for copy in ins:
        copy.start()
    for copy_in, copy_out in zip(ins, outs):
        copy_in.wait()
        copy_out.start()
    for copy in outs:
        copy.wait()


def shards(
    hidden, norm_gain, q_weight, q_bias, kv_weight, kv_bias, out_weight, kv_store, stretch_place, req_stretches, rec_rows
):
    owners = lax.axis_size("cache")
    me = lax.axis_index("cache")
    rows, width = hidden.shape
    stretches, _, length, kv_width = kv_store.shape
    hd = kv_width // 2
    per = rec_rows.shape[2]
    depth, q_cols = q_weight.shape
    levels = lax.axis_size("heads") // 2
    heads = q_cols // hd
    vmem = pl.BlockSpec(memory_space=pltpu.VMEM)
    smem = pl.BlockSpec(memory_space=pltpu.SMEM)
    hbm = pl.BlockSpec(memory_space=pl.ANY)
    dma = pltpu.SemaphoreType.DMA

    store = kv_store.reshape(stretches, owners, 2, length // (2 * owners), kv_width)
    piece = length // (2 * owners)

    attn_out, new_store = pl.pallas_call(
        prefill,
        out_shape=(
            jax.ShapeDtypeStruct((rows, q_cols), BF16),
            jax.ShapeDtypeStruct((stretches, length, kv_width), BF16),
        ),
        in_specs=[smem, smem, hbm, vmem, hbm, hbm, vmem, vmem, hbm, hbm, vmem],
        out_specs=(vmem, hbm),
        scratch_shapes=[
            pltpu.VMEM((rows, width), BF16),
            pltpu.VMEM((SIDE, SIDE, rows, depth), BF16),
            pltpu.VMEM((SIDE, depth, q_cols + hd), BF16),
            pltpu.VMEM((SIDE, rows, q_cols + hd), F32),
            pltpu.VMEM((SIDE, rows, q_cols + hd), BF16),
            pltpu.VMEM((SIDE, rows, q_cols + hd), BF16),
            pltpu.VMEM((owners * stretches, piece, kv_width), BF16),
            pltpu.VMEM((owners, stretches, piece, kv_width), BF16),
            pltpu.VMEM((rows * heads, hd), F32),
            pltpu.VMEM((stretches * PAD, hd), F32),
            pltpu.VMEM((stretches, hd), jnp.int32),
            pltpu.VMEM((stretches, hd), jnp.int32),
            pltpu.VMEM((rows * heads, hd), BF16),
            pltpu.VMEM((stretches, PAD, hd), BF16),
            pltpu.VMEM((2, stretches, PAD, hd), BF16),
            pltpu.VMEM((stretches, owners, 2, piece, kv_width), BF16),
            pltpu.VMEM((stretches, length, hd), BF16),
            pltpu.VMEM((stretches, length, hd), BF16),
            pltpu.VMEM((rows * heads * (stretches + 1) // 2, length), F32),
            pltpu.VMEM((rows * heads, hd), F32),
            pltpu.VMEM((rows * heads, hd), F32),
            pltpu.VMEM((rows * heads, hd), F32),
            pltpu.VMEM((rows, q_cols), F32),
            pltpu.VMEM((rows, q_cols), BF16),
            pltpu.VMEM((2, SIDE, depth, q_cols), BF16),
            pltpu.VMEM((2, 2, rows, q_cols), BF16),
            pltpu.VMEM((levels, rows, q_cols), F32),
            pltpu.VMEM((4, rows, q_cols), BF16),
            pltpu.VMEM((4, rows, q_cols), BF16),
            pltpu.VMEM((4, rows, q_cols), BF16),
            pltpu.VMEM((4, rows, q_cols), BF16),
            pltpu.VMEM((rows, q_cols), BF16),
            pltpu.VMEM((2 * owners, PAD, hd), BF16),
            pltpu.VMEM((2 * owners, PAD, hd), BF16),
            pltpu.VMEM((2, stretches, PAD, hd), BF16),
            pltpu.VMEM((stretches, owners, 2, piece, kv_width), BF16),
            pltpu.VMEM((stretches, length, kv_width), BF16),
            dma((7 + SIDE,)),
            dma((SIDE, 2)),
            dma((SIDE, 2)),
            dma((SIDE,)),
            dma((SIDE,)),
            dma((SIDE + 1, SIDE)),
            dma((SIDE + 1, SIDE)),
            dma((SIDE + 1, SIDE)),
            dma((SIDE + 1, SIDE)),
            dma((SIDE, 2)),
            dma((SIDE, 2)),
            dma((SIDE,)),
            dma((SIDE,)),
            dma((owners,)),
            dma((owners,)),
            dma((owners,)),
            dma((owners,)),
            dma((owners,)),
            dma((owners,)),
            dma((5,)),
            dma((5,)),
            dma((SIDE, 2)),
            dma((SIDE, 2)),
            dma((SIDE,)),
            dma((SIDE,)),
            dma((SIDE,)),
            dma((SIDE, 2)),
            dma((4, 2)),
            dma((4, 2)),
            dma((4, 2)),
            dma((4, 2)),
            dma((owners,)),
            dma((owners,)),
            dma((8,)),
        ],
        compiler_params=pltpu.CompilerParams(collective_id=0, has_side_effects=True, vmem_limit_bytes=58 << 20),
        name="prefill",
    )(
        stretch_place, req_stretches, hidden, norm_gain, q_weight, kv_weight, q_bias, kv_bias, out_weight, store, rec_rows
    )
    return pl.pallas_call(
        hand_over,
        out_shape=(
            jax.ShapeDtypeStruct((rows, q_cols), BF16),
            jax.ShapeDtypeStruct((stretches, 1, length, kv_width), BF16),
        ),
        in_specs=[hbm, hbm],
        out_specs=(hbm, hbm),
        scratch_shapes=[
            pltpu.VMEM((rows, q_cols), BF16),
            pltpu.VMEM((stretches, length, kv_width), BF16),
            dma((stretches + 1,)),
            dma((stretches + 1,)),
        ],
        name="hand_over",
    )(attn_out, new_store)


def solution(mesh):
    placed = (
        P("cache", None),
        P(),
        P("cache", "heads"),
        P("heads"),
        P("cache", None),
        P(),
        P("heads", "cache"),
        P("cache", "heads", None, None),
        P(),
        P(),
        P(),
    )
    return jax.shard_map(
        shards,
        mesh=mesh,
        in_specs=placed,
        out_specs=(P("cache", "heads"), P("cache", "heads", None, None)),
        check_vma=False,
    )
```

```python
import functools
import math

import jax
import jax.numpy as jnp
from jax import lax
from jax.experimental import pallas as pl
from jax.experimental.pallas import tpu as pltpu
from jax.sharding import PartitionSpec as P

MESH = pl.DeviceIdType.MESH
SIDE = 4
BF16 = jnp.bfloat16
F32 = jnp.float32
RIGHT, OPPOSITE, LEFT = 1, 2, 3
PAD = 32


def remote(src, dst, send_sem, recv_sem, device):
    return pltpu.make_async_remote_copy(
        src_ref=src, dst_ref=dst, send_sem=send_sem, recv_sem=recv_sem, device_id=device, device_id_type=MESH
    )


def blend(old, keys, values, rows):
    hd = keys.shape[1]
    hit = lax.broadcasted_iota(jnp.int32, (old.shape[0], PAD), 0) == rows
    table = jnp.concatenate([keys, values, jnp.ones((PAD, hd), BF16)], axis=1)
    new = jnp.dot(hit.astype(F32).astype(BF16), table, preferred_element_type=F32)
    there = new[:, 2 * hd :] > 0.5
    parts = [
        jnp.where(there, new[:, i * hd : (i + 1) * hd], old[:, i * hd : (i + 1) * hd].astype(F32)).astype(BF16)
        for i in (0, 1)
    ]
    return parts[0], parts[1]


def attend(q_ref, row_ref, ctx_ref, ks, vs, sc, top, low, out, flat):
    stretches, length = ks.shape[0], ks.shape[1]
    hd = q_ref.shape[1]
    total = q_ref.shape[0]
    group = total // stretches
    heads = ctx_ref.shape[1] // hd
    per = group // heads
    scale = math.log2(math.e) / math.sqrt(hd)
    top[...] = jnp.full_like(top, -jnp.inf)
    low[...] = jnp.zeros_like(low)
    out[...] = jnp.zeros_like(out)

    def fold(a, op):
        parts = [a[:, i * hd : (i + 1) * hd] for i in range(length // hd)]
        while len(parts) > 1:
            parts = [op(parts[i], parts[i + 1]) for i in range(0, len(parts), 2)]
        return parts[0]

    columns = jnp.transpose(row_ref[...].astype(F32))
    base = [sum(total - t * group for t in range(s)) for s in range(stretches)]
    for s in range(stretches):
        scores = lax.dot_general(
            q_ref[s * group :, :], ks[s], (((1,), (1,)), ((), ())), preferred_element_type=F32
        )
        key = lax.broadcasted_iota(jnp.int32, (group, length), 1).astype(F32)
        last = jnp.concatenate([columns[0:per, s : s + 1]] * heads, axis=0)
        first = jnp.where(key <= last, scores[:group], -jnp.inf)
        sc[base[s] : base[s] + group, :] = first
        top[s * group : (s + 1) * group, :] = jnp.maximum(
            top[s * group : (s + 1) * group, :], fold(first, jnp.maximum)
        )
        if s + 1 < stretches:
            sc[base[s] + group : base[s] + total - s * group, :] = scores[group:]
            top[(s + 1) * group :, :] = jnp.maximum(top[(s + 1) * group :, :], fold(scores[group:], jnp.maximum))
    top[...] = jnp.broadcast_to(jnp.max(top[...], axis=1, keepdims=True), top.shape)
    for s in range(stretches):
        here = slice(s * group, total)
        held = slice(base[s], base[s] + total - s * group)
        peak = top[here, :]
        expon = jnp.concatenate(
            [jnp.exp2((sc[held, i * hd : (i + 1) * hd] - peak) * scale) for i in range(length // hd)], axis=1
        )
        low[here, :] += fold(expon, jnp.add)
        out[here, :] += jnp.dot(expon.astype(BF16), vs[s], preferred_element_type=F32)
    out[...] = out[...] / jnp.sum(low[...], axis=1, keepdims=True)
    for r in range(stretches):
        for j in range(heads):
            at_row = (r * heads + j) * per
            flat[r * per : (r + 1) * per, j * hd : (j + 1) * hd] = out[at_row : at_row + per, :]
    ctx_ref[...] = flat[...].astype(BF16)


def prefill(
    table_ref, req_ref, hid_hbm, gain_ref, qw_hbm, kvw_hbm, qb_ref, kvb_ref, ow_hbm, store_hbm, rec_ref,
    out_ref, new_hbm,
    hid, acts, w, acc, part, sums, hop_in, hop_out, qs, fpad, my_rows, slot_rows,
    queries, own_fresh, fresh, blocks, ks, vs, sc, top, low, res, flat, ctx,
    ow, ctxs, chunk, r_out, l_out, r_in, l_in, done, f_out, f_in, back, old, new,
    loc, w_send, w_recv, a_send, a_recv, zr_send, zr_recv, zl_send, zl_recv, c_send, c_recv, s_send, s_recv,
    h1_send, h1_recv, h2_send, h2_recv, x_send, x_recv,
    o_send, o_recv, oo_send, oo_recv, t_send, t_recv,
    r_send, r_recv, l_send, l_recv, f_send, f_recv, n_sem,
):
    me = lax.axis_index("cache")
    head = lax.axis_index("heads")
    core = lax.rem(head, 2)
    partner = (me, head + 1 - 2 * core)
    x, y = me // SIDE, lax.rem(me, SIDE)
    z = head // 2
    owners = SIDE * SIDE
    levels = lax.axis_size("heads") // 2
    right = (me, lax.rem(z + 1, levels) * 2 + core)
    left = (me, lax.rem(z + levels - 1, levels) * 2 + core)
    turn = lax.rem(head, SIDE)
    mirror = (x * SIDE + turn, head - turn + y)
    rows = hid.shape[0]
    depth, width = w.shape[1], w.shape[2]
    q_cols = qw_hbm.shape[1]
    hd = width - q_cols
    per = rows // 8

    def ring(i, d):
        return lax.rem(i + d, SIDE)

    own_hid = pltpu.make_async_copy(hid_hbm, hid, loc.at[2])
    own_q = pltpu.make_async_copy(qw_hbm, w.at[x, :, 0:q_cols], loc.at[0])
    own_kv = pltpu.make_async_copy(
        kvw_hbm.at[:, pl.ds(pl.multiple_of(head * hd, hd), hd)], w.at[x, :, q_cols:width], loc.at[1]
    )
    own_hop = pltpu.make_async_copy(store_hbm.at[:, me, core], hop_in.at[pl.ds(me * 8, 8)], loc.at[3])
    own_hid.start()
    own_q.start()
    own_kv.start()
    own_hop.start()
    own_ow = pltpu.make_async_copy(ow_hbm, ow.at[core, x], loc.at[5 + SIDE])
    own_ow.start()
    old_in = pltpu.make_async_copy(store_hbm, old, loc.at[6 + SIDE])
    old_in.start()

    barrier = pltpu.get_barrier_semaphore()

    @pl.loop(1, owners)
    def _(o):
        pl.semaphore_signal(barrier, inc=1, device_id=(lax.rem(me + o, owners), head), device_id_type=MESH)

    for peer in (partner, left, right):
        pl.semaphore_signal(barrier, inc=1, device_id=peer, device_id_type=MESH)
    for d in (RIGHT, OPPOSITE, LEFT):
        across = (x * SIDE + ring(y, d), head + 1 - 2 * core)
        pl.semaphore_signal(barrier, inc=1, device_id=across, device_id_type=MESH)

    @pl.when(turn != y)
    def _():
        pl.semaphore_signal(barrier, inc=1, device_id=mirror, device_id_type=MESH)

    @pl.when(turn != y)
    def _():
        pl.semaphore_wait(barrier, owners + 6)

    @pl.when(turn == y)
    def _():
        pl.semaphore_wait(barrier, owners + 5)

    def slice_of(c):
        return hid.at[:, pl.ds(pl.multiple_of(c * depth, depth), depth)]

    few = rows // 4

    def eighth(level, d):
        lines = pl.ds(pl.multiple_of(level // 2 * few, few), few)
        return acts.at[2 * core + lax.rem(level, 2), ring(y, SIDE - d), lines]

    def rows_to(d):
        to = ring(y, d)
        lines = pl.ds(pl.multiple_of(z // 2 * few, few), few)
        column = ((2 * core + lax.rem(z, 2)) * SIDE + to) * depth
        return remote(
            hid.at[lines, pl.ds(pl.multiple_of(column, depth), depth)], acts.at[2 * core + lax.rem(z, 2), y, lines],
            a_send.at[d], a_recv.at[d], (x * SIDE + to, head),
        )

    def rows_from(d):
        place = eighth(z, d)
        return remote(place, place, a_send.at[d], a_recv.at[d], (x * SIDE + ring(y, SIDE - d), head))

    def upward(step, d, arriving=False):
        place = eighth(lax.rem(z + levels + 1 - step - (1 if arriving else 0), levels), d)
        return remote(place, place, zr_send.at[step, d], zr_recv.at[step, d], right)

    def downward(step, d, arriving=False):
        place = eighth(lax.rem(z - 1 + step + (1 if arriving else 0), levels), d)
        return remote(place, place, zl_send.at[step, d], zl_recv.at[step, d], left)

    def goes_up(step, d):
        return step < 4 or d != LEFT

    def goes_down(step, d):
        return step < 4 or d == LEFT

    def level_step(step):
        for d in steps:
            if step == 1:
                rows_from(d).wait_recv()
            else:
                upward(step - 1, d, True).wait_recv()
            if goes_up(step, d):
                upward(step, d).start()
            if step > 1:
                downward(step - 1, d, True).wait_recv()
            if goes_down(step, d):
                downward(step, d).start()

    def hop1(o):
        to = lax.rem(me + o, owners)
        return remote(
            store_hbm.at[:, to, core], hop_in.at[pl.ds(me * 8, 8)], h1_send.at[o], h1_recv.at[me], (to, head)
        )

    def hop1_from(o):
        src = lax.rem(me + owners - o, owners)
        return remote(
            store_hbm.at[:, src, core], hop_in.at[pl.ds(src * 8, 8)], h1_send.at[o], h1_recv.at[src], (src, head)
        )

    def hop2(o):
        to = lax.rem(me + o, owners)
        return remote(hop_out.at[to], blocks.at[:, me, core], h2_send.at[o], h2_recv.at[me], (to, head))

    def hop2_from(o):
        src = lax.rem(me + owners - o, owners)
        return remote(hop_out.at[src], blocks.at[:, src, core], h2_send.at[o], h2_recv.at[src], (src, head))

    class Ring4:
        def __init__(self, source, place, send_sem, recv_sem):
            self.source, self.place, self.send_sem, self.recv_sem = source, place, send_sem, recv_sem
            self.deep = place(0).shape[0] // 2

        def part(self, ref, half):
            return ref.at[pl.ds(half * self.deep, self.deep)]

        def copy(self, d, half, passed=False):
            to = (ring(x, d) * SIDE + y, head)
            src = self.part(self.place(ring(x, SIDE - d)) if passed else self.source, half)
            dst = self.part(self.place(ring(x, SIDE - d) if passed else x), half)
            k = OPPOSITE if passed else d
            return remote(src, dst, self.send_sem.at[k, half], self.recv_sem.at[k, half], to)

        def wait(self, d, half):
            place = self.part(self.place(ring(x, SIDE - d)), half)
            remote(
                place, place, self.send_sem.at[d, half], self.recv_sem.at[d, half],
                (ring(x, SIDE - d) * SIDE + y, head),
            ).wait_recv()

        def start(self):
            self.copy(RIGHT, 0).start()
            self.copy(LEFT, 1).start()

        def rest(self):
            self.copy(RIGHT, 1).start()
            self.copy(LEFT, 0).start()

        def forward(self):
            self.wait(RIGHT, 0)
            self.copy(RIGHT, 0, True).start()
            self.wait(LEFT, 1)
            self.copy(LEFT, 1, True).start()

        def wait_rest(self):
            self.wait(RIGHT, 1)
            self.wait(LEFT, 0)

        def wait_opposite(self):
            self.wait(OPPOSITE, 0)
            self.wait(OPPOSITE, 1)

        def finish(self):
            for half in (0, 1):
                self.copy(RIGHT, half).wait_send()
                self.copy(LEFT, half).wait_send()
            self.copy(RIGHT, 0, True).wait_send()
            self.copy(LEFT, 1, True).wait_send()

    weights = Ring4(w.at[x], lambda i: w.at[i], w_send, w_recv)
    ow_blocks = Ring4(ow_hbm, lambda i: ow.at[core, i], o_send, o_recv)

    steps = (RIGHT, LEFT, OPPOSITE)
    own_q.wait()
    own_kv.wait()
    weights.start()

    @pl.loop(1, owners)
    def _(o):
        hop1(o).start()

    own_hid.wait()
    tall = 16

    @pl.loop(0, rows // tall)
    def _(i):
        lines = pl.ds(pl.multiple_of(i * tall, tall), tall)
        total = jnp.zeros((tall, 1), F32)
        for c in range(owners):
            v = hid[lines, c * depth : (c + 1) * depth].astype(F32)
            total += jnp.sum(v * v, axis=-1, keepdims=True)
        factor = lax.rsqrt(total / (owners * depth) + 1e-06)
        for c in range(owners):
            v = hid[lines, c * depth : (c + 1) * depth].astype(F32)
            g = gain_ref[c * depth : (c + 1) * depth].astype(F32).reshape(1, depth)
            hid[lines, c * depth : (c + 1) * depth] = (v * factor * g).astype(BF16)

    for d in steps:
        rows_to(d).start()
    weights.rest()

    for i in range(SIDE):
        pltpu.make_async_copy(slice_of(i * SIDE + y), acts.at[i, y], loc.at[5 + i]).start()

    def place_of(i, r):
        return table_ref[req_ref[r, i]]

    my_owner = [place_of(me, r) // 8 for r in range(8)]
    my_rank = [sum([(my_owner[q] == my_owner[r]).astype(jnp.int32) for q in range(r)], 0) for r in range(8)]

    def find(n, found):
        here = place_of(n // 8, lax.rem(n, 8)) - me * 8
        return tuple(jnp.where(here == s, n, found[s]) for s in range(8))

    found = lax.fori_loop(0, owners * 8, find, (jnp.int32(0),) * 8)
    my_rows[...] = jnp.full_like(my_rows, -1)
    slot_rows[...] = jnp.full_like(slot_rows, -1)
    my_rows[:, 0:per] = rec_ref[me]
    picks = []
    for s in range(8):
        i, r = found[s] // 8, lax.rem(found[s], 8)
        slot_rows[s : s + 1, 0:per] = rec_ref[i, pl.ds(r, 1), :]
        rank = sum([((q < r) & (place_of(i, q) // 8 == me)).astype(jnp.int32) for q in range(8)], 0)
        picks.append(2 * i + jnp.minimum(rank, 1))

    level_step(1)
    weights.forward()

    level_step(2)

    own_hop.wait()

    @pl.loop(1, owners)
    def _(o):
        hop1_from(o).wait_recv()

    def sort(i):
        for r in range(8):
            hop_out[i, r] = hop_in[place_of(i, r)]

    @pl.loop(1, owners)
    def _(o):
        sort(lax.rem(me + o, owners))
        hop2(o).start()

    sort(me)
    own_out = pltpu.make_async_copy(hop_out.at[me], blocks.at[:, me, core], loc.at[4])
    own_out.start()

    level_step(3)
    level_step(4)
    for d in steps:
        if goes_up(4, d):
            upward(4, d, True).wait_recv()
        if goes_down(4, d):
            downward(4, d, True).wait_recv()

    def rows_over(d, i, which):
        place = acts.at[2 * which + i, ring(y, SIDE - d)]
        return remote(place, place, c_send.at[d, i], c_recv.at[d, i], partner)

    for i in (0, 1):
        for d in steps:
            rows_over(d, i, core).start()

    for i in range(SIDE):
        pltpu.make_async_copy(slice_of(i * SIDE + y), acts.at[i, y], loc.at[5 + i]).wait()
    weights.wait_rest()
    weights.wait_opposite()

    def product(i, j):
        return jnp.dot(acts[i, j], w[i], preferred_element_type=F32)

    @pl.loop(0, SIDE)
    def _(j):
        acc[j] = product(2 * core, j)
        acc[j] += product(2 * core + 1, j)

    for i in (0, 1):
        for d in steps:
            rows_over(d, i, 1 - core).wait_recv()

    def sums_to(d):
        to = ring(y, d)
        return remote(part.at[d], sums.at[d], s_send.at[d], s_recv.at[d], (x * SIDE + to, head))

    for d in (OPPOSITE, RIGHT, LEFT):
        j = ring(y, d)
        acc[j] += product(2 - 2 * core, j)
        part[d] = (acc[j] + product(3 - 2 * core, j)).astype(BF16)
        sums_to(d).start()

    def block_from(d, which):
        place = ow.at[which, ring(x, SIDE - d)]
        return remote(place, place, oo_send.at[d], oo_recv.at[d], partner)

    ow_blocks.start()
    ow_blocks.rest()
    own_ow.wait()
    block_from(0, core).start()
    acc[y] += product(2 - 2 * core, y)
    acc[y] += product(3 - 2 * core, y)

    for d in steps:
        remote(part.at[d], sums.at[d], s_send.at[d], s_recv.at[d], (x * SIDE + ring(y, SIDE - d), head)).wait_recv()
        acc[y] += sums[d].astype(F32)

    heads = q_cols // hd
    bias = qb_ref[...].astype(F32).reshape(1, q_cols)
    both = kvb_ref[pl.ds(pl.multiple_of(z * 2 * hd, 2 * hd), 2 * hd)].astype(F32).reshape(1, 2 * hd)
    kv_bias = jnp.where(core == 0, both[:, 0:hd], both[:, hd:])
    for r in range(8):
        lines = slice(per * r, per * (r + 1))
        for j in range(heads):
            at_row = (j // 2 * 16 + r * 2 + j % 2) * per
            qs[at_row : at_row + per, :] = acc[y, lines, j * hd : (j + 1) * hd] + bias[:, j * hd : (j + 1) * hd]
        fpad[r * PAD : r * PAD + per, :] = acc[y, lines, q_cols:width] + kv_bias
        fpad[r * PAD + per : (r + 1) * PAD, :] = jnp.zeros((PAD - per, hd), F32)
    own_fresh[...] = fpad[...].astype(BF16).reshape(own_fresh.shape)
    fresh[core] = own_fresh[...]
    swap = remote(own_fresh, fresh.at[core], x_send.at[1], x_recv.at[1], partner)
    swap.start()
    queries[...] = qs[...].astype(BF16)

    @pl.loop(0, owners)
    def _(o):
        for m in range(2):
            row = sum([jnp.where((my_owner[r] == o) & (my_rank[r] == m), r, 0) for r in range(8)], 0)
            f_out[2 * o + m] = own_fresh[row]

    def give(o):
        to = lax.rem(me + o, owners)
        return remote(
            f_out.at[pl.ds(2 * to, 2)], f_in.at[pl.ds(2 * me, 2)], f_send.at[o], f_recv.at[me], (to, head)
        )

    def take(o):
        src = lax.rem(me + owners - o, owners)
        return remote(
            f_out.at[pl.ds(2 * src, 2)], f_in.at[pl.ds(2 * src, 2)], f_send.at[o], f_recv.at[src], (src, head)
        )

    @pl.loop(1, owners)
    def _(o):
        give(o).start()

    for m in range(2):
        f_in[2 * me + m] = f_out[2 * me + m]

    def core_swap(which):
        return remote(
            blocks.at[:, :, which], blocks.at[:, :, which], x_send.at[0], x_recv.at[0], partner
        )

    own_out.wait()

    @pl.loop(1, owners)
    def _(o):
        hop2_from(o).wait_recv()

    core_swap(core).start()

    ow_blocks.forward()
    core_swap(1 - core).wait_recv()
    remote(fresh.at[1 - core], fresh.at[1 - core], x_send.at[1], x_recv.at[1], partner).wait_recv()

    for r in range(8):
        old_rows = blocks[r].reshape(ks.shape[1], 2 * hd)
        ks[r], vs[r] = blend(old_rows, fresh[0, r], fresh[1, r], my_rows[r : r + 1, 0:PAD])

    def ctx_to(d, pair):
        to = ring(y, d)
        return remote(
            ctx.at[pair], ctxs.at[y // 2, core, pair], t_send.at[d, pair], t_recv.at[d, core, pair],
            (x * SIDE + to, 2 * z + lax.rem(y, 2)),
        )

    def ctx_from(d, which, pair):
        src = ring(y, SIDE - d)
        place = ctxs.at[src // 2, which, pair]
        return remote(
            place, place, t_send.at[d, pair], t_recv.at[d, which, pair], (x * SIDE + src, 2 * z + which)
        )

    mine = lax.rem(y, 2) == core

    for pair in (0, 1):
        lines = pl.ds(pair * queries.shape[0] // 2, queries.shape[0] // 2)
        attend(queries.at[lines], my_rows, ctx.at[pair], ks, vs, sc, top, low, res, flat)
        for d in (RIGHT, LEFT, OPPOSITE):
            ctx_to(d, pair).start()

        @pl.when(mine)
        def _():
            ctxs[y // 2, core, pair] = ctx[pair]

        @pl.when(jnp.logical_not(mine))
        def _():
            ctx_to(0, pair).start()

    ow_blocks.wait_rest()
    block_from(RIGHT, core).start()
    block_from(LEFT, core).start()

    @pl.loop(1, owners)
    def _(o):
        take(o).wait_recv()

    for s in range(8):
        back[core, s] = f_in[picks[s]]
    swap_back = remote(back.at[core], back.at[core], x_send.at[2], x_recv.at[2], partner)
    swap_back.start()

    @pl.when(mine)
    def _():
        for pair in (0, 1):
            ctx_from(0, 1 - core, pair).wait_recv()
            for which in (0, 1):
                ctx_from(OPPOSITE, which, pair).wait_recv()

    @pl.when(jnp.logical_not(mine))
    def _():
        for d in (RIGHT, LEFT):
            for which in (0, 1):
                for pair in (0, 1):
                    ctx_from(d, which, pair).wait_recv()

    ow_blocks.wait_opposite()
    block_from(OPPOSITE, core).start()
    for d in (0,) + steps:
        block_from(d, 1 - core).wait_recv()

    hrow = rows // 2
    order = (4, 3, -3, 2, -2, 1, -1, 0)

    def compute(n):
        target = lax.rem(z + order[n] + levels, levels)
        column, request = target // 2, lax.rem(target, 2)
        total = None
        for which in (0, 1):
            both = jnp.concatenate([ctxs[request, which, 0], ctxs[request, which, 1]], axis=1)
            term = jnp.dot(both, ow[which, column], preferred_element_type=F32)
            total = term if total is None else total + term
        chunk[n] = total

    def lines_of(half):
        return slice(half * hrow, (half + 1) * hrow)

    def ring_copy(step, half, out, into, send_sem, recv_sem, to):
        return remote(
            out.at[step, pl.ds(half * hrow, hrow)],
            into.at[step, pl.ds(half * hrow, hrow)],
            send_sem.at[step, half],
            recv_sem.at[step, half],
            to,
        )

    def rightward(step, half):
        return ring_copy(step, half, r_out, r_in, r_send, r_recv, right)

    def leftward(step, half):
        return ring_copy(step, half, l_out, l_in, l_send, l_recv, left)

    def renew(s):
        keys, values = blend(old[s].reshape(new.shape[1], 2 * hd), back[0, s], back[1, s], slot_rows[s : s + 1, 0:PAD])
        new[s, :, 0:hd] = keys
        new[s, :, hd : 2 * hd] = values
        pltpu.make_async_copy(new.at[s], new_hbm.at[s], n_sem.at[s]).start()

    compute(0)
    r_out[0, lines_of(0), :] = chunk[0, lines_of(0), :].astype(BF16)
    rightward(0, 0).start()
    l_out[0, lines_of(1), :] = chunk[0, lines_of(1), :].astype(BF16)
    leftward(0, 1).start()
    compute(1)
    compute(2)
    for step in (1, 2, 3):
        n_right, n_left = 2 * step - 1, 2 * step
        halves = ((1, 0), (0, 1)) if step == 1 else ((0, 1), (1, 0))
        for right_half, left_half in halves:
            value = chunk[n_right, lines_of(right_half), :]
            if step > 1 or right_half == 0:
                rightward(step - 1, right_half).wait_recv()
                value += r_in[step - 1, lines_of(right_half), :].astype(F32)
            r_out[step, lines_of(right_half), :] = value.astype(BF16)
            rightward(step, right_half).start()
            value = chunk[n_left, lines_of(left_half), :]
            if step > 1 or left_half == 1:
                leftward(step - 1, left_half).wait_recv()
                value += l_in[step - 1, lines_of(left_half), :].astype(F32)
            l_out[step, lines_of(left_half), :] = value.astype(BF16)
            leftward(step, left_half).start()
        if step == 1:
            old_in.wait()
            remote(back.at[1 - core], back.at[1 - core], x_send.at[2], x_recv.at[2], partner).wait_recv()
        if step < 3:
            compute(2 * step + 1)
            compute(2 * step + 2)
            for s in range(4 * step - 4, 4 * step):
                renew(s)
        else:
            compute(7)

    def flip(half):
        return remote(
            done.at[pl.ds(half * hrow, hrow)], out_ref.at[pl.ds(half * hrow, hrow)],
            x_send.at[3 + half], x_recv.at[3 + half], mirror,
        )

    for half in (0, 1):
        rightward(3, half).wait_recv()
        leftward(3, half).wait_recv()
        value = chunk[7, lines_of(half), :] + r_in[3, lines_of(half), :].astype(F32)
        value += l_in[3, lines_of(half), :].astype(F32)
        done[lines_of(half), :] = value.astype(BF16)

        @pl.when(turn != y)
        def _():
            flip(half).start()

    @pl.when(turn == y)
    def _():
        out_ref[...] = done[...]

    for i in (0, 1):
        for d in steps:
            rows_over(d, i, core).wait_send()
    for d in steps:
        rows_to(d).wait_send()
        for step in (1, 2, 3, 4):
            if goes_up(step, d):
                upward(step, d).wait_send()
            if goes_down(step, d):
                downward(step, d).wait_send()
    for d in steps:
        sums_to(d).wait_send()
        for pair in (0, 1):
            ctx_to(d, pair).wait_send()
    weights.finish()
    ow_blocks.finish()
    for d in (0,) + steps:
        block_from(d, core).wait_send()

    @pl.when(jnp.logical_not(mine))
    def _():
        for pair in (0, 1):
            ctx_to(0, pair).wait_send()

    @pl.loop(1, owners)
    def _(o):
        hop1(o).wait_send()
        hop2(o).wait_send()
        give(o).wait_send()

    core_swap(core).wait_send()
    swap.wait_send()
    swap_back.wait_send()
    rightward(0, 0).wait_send()
    leftward(0, 1).wait_send()
    for step in (1, 2, 3):
        for half in (0, 1):
            rightward(step, half).wait_send()
            leftward(step, half).wait_send()
    for s in range(8):
        pltpu.make_async_copy(new.at[s], new_hbm.at[s], n_sem.at[s]).wait()

    @pl.when(turn != y)
    def _():
        for half in (0, 1):
            flip(half).wait()


def hand_over(out_ref, store_ref, out_copy, store_copy, out_held, held, sem_in, sem_out):
    count = store_ref.shape[0]
    ins = [pltpu.make_async_copy(store_ref.at[s], held.at[s], sem_in.at[s]) for s in range(count)]
    ins.append(pltpu.make_async_copy(out_ref, out_held, sem_in.at[count]))
    outs = [pltpu.make_async_copy(held.at[s], store_copy.at[s, 0], sem_out.at[s]) for s in range(count)]
    outs.append(pltpu.make_async_copy(out_held, out_copy, sem_out.at[count]))
    for copy in ins:
        copy.start()
    for copy_in, copy_out in zip(ins, outs):
        copy_in.wait()
        copy_out.start()
    for copy in outs:
        copy.wait()


def shards(
    hidden, norm_gain, q_weight, q_bias, kv_weight, kv_bias, out_weight, kv_store, stretch_place, req_stretches, rec_rows
):
    owners = lax.axis_size("cache")
    me = lax.axis_index("cache")
    rows, width = hidden.shape
    stretches, _, length, kv_width = kv_store.shape
    hd = kv_width // 2
    per = rec_rows.shape[2]
    depth, q_cols = q_weight.shape
    levels = lax.axis_size("heads") // 2
    heads = q_cols // hd
    vmem = pl.BlockSpec(memory_space=pltpu.VMEM)
    smem = pl.BlockSpec(memory_space=pltpu.SMEM)
    hbm = pl.BlockSpec(memory_space=pl.ANY)
    dma = pltpu.SemaphoreType.DMA

    store = kv_store.reshape(stretches, owners, 2, length // (2 * owners), kv_width)
    piece = length // (2 * owners)

    attn_out, new_store = pl.pallas_call(
        prefill,
        out_shape=(
            jax.ShapeDtypeStruct((rows, q_cols), BF16),
            jax.ShapeDtypeStruct((stretches, length, kv_width), BF16),
        ),
        in_specs=[smem, smem, hbm, vmem, hbm, hbm, vmem, vmem, hbm, hbm, vmem],
        out_specs=(vmem, hbm),
        scratch_shapes=[
            pltpu.VMEM((rows, width), BF16),
            pltpu.VMEM((SIDE, SIDE, rows, depth), BF16),
            pltpu.VMEM((SIDE, depth, q_cols + hd), BF16),
            pltpu.VMEM((SIDE, rows, q_cols + hd), F32),
            pltpu.VMEM((SIDE, rows, q_cols + hd), BF16),
            pltpu.VMEM((SIDE, rows, q_cols + hd), BF16),
            pltpu.VMEM((owners * stretches, piece, kv_width), BF16),
            pltpu.VMEM((owners, stretches, piece, kv_width), BF16),
            pltpu.VMEM((rows * heads, hd), F32),
            pltpu.VMEM((stretches * PAD, hd), F32),
            pltpu.VMEM((stretches, hd), jnp.int32),
            pltpu.VMEM((stretches, hd), jnp.int32),
            pltpu.VMEM((rows * heads, hd), BF16),
            pltpu.VMEM((stretches, PAD, hd), BF16),
            pltpu.VMEM((2, stretches, PAD, hd), BF16),
            pltpu.VMEM((stretches, owners, 2, piece, kv_width), BF16),
            pltpu.VMEM((stretches, length, hd), BF16),
            pltpu.VMEM((stretches, length, hd), BF16),
            pltpu.VMEM((rows * heads * (stretches + 1) // 4, length), F32),
            pltpu.VMEM((rows * heads // 2, hd), F32),
            pltpu.VMEM((rows * heads // 2, hd), F32),
            pltpu.VMEM((rows * heads // 2, hd), F32),
            pltpu.VMEM((rows, q_cols // 2), F32),
            pltpu.VMEM((2, rows, q_cols // 2), BF16),
            pltpu.VMEM((2, SIDE, depth, q_cols), BF16),
            pltpu.VMEM((2, 2, 2, rows, q_cols // 2), BF16),
            pltpu.VMEM((levels, rows, q_cols), F32),
            pltpu.VMEM((4, rows, q_cols), BF16),
            pltpu.VMEM((4, rows, q_cols), BF16),
            pltpu.VMEM((4, rows, q_cols), BF16),
            pltpu.VMEM((4, rows, q_cols), BF16),
            pltpu.VMEM((rows, q_cols), BF16),
            pltpu.VMEM((2 * owners, PAD, hd), BF16),
            pltpu.VMEM((2 * owners, PAD, hd), BF16),
            pltpu.VMEM((2, stretches, PAD, hd), BF16),
            pltpu.VMEM((stretches, owners, 2, piece, kv_width), BF16),
            pltpu.VMEM((stretches, length, kv_width), BF16),
            dma((7 + SIDE,)),
            dma((SIDE, 2)),
            dma((SIDE, 2)),
            dma((SIDE,)),
            dma((SIDE,)),
            dma((SIDE + 1, SIDE)),
            dma((SIDE + 1, SIDE)),
            dma((SIDE + 1, SIDE)),
            dma((SIDE + 1, SIDE)),
            dma((SIDE, 2)),
            dma((SIDE, 2)),
            dma((SIDE,)),
            dma((SIDE,)),
            dma((owners,)),
            dma((owners,)),
            dma((owners,)),
            dma((owners,)),
            dma((5,)),
            dma((5,)),
            dma((SIDE, 2)),
            dma((SIDE, 2)),
            dma((SIDE,)),
            dma((SIDE,)),
            dma((SIDE, 2)),
            dma((SIDE, 2, 2)),
            dma((4, 2)),
            dma((4, 2)),
            dma((4, 2)),
            dma((4, 2)),
            dma((owners,)),
            dma((owners,)),
            dma((8,)),
        ],
        compiler_params=pltpu.CompilerParams(collective_id=0, has_side_effects=True, vmem_limit_bytes=58 << 20),
        name="prefill",
    )(
        stretch_place, req_stretches.T, hidden, norm_gain, q_weight, kv_weight, q_bias, kv_bias, out_weight, store, rec_rows
    )
    return pl.pallas_call(
        hand_over,
        out_shape=(
            jax.ShapeDtypeStruct((rows, q_cols), BF16),
            jax.ShapeDtypeStruct((stretches, 1, length, kv_width), BF16),
        ),
        in_specs=[hbm, hbm],
        out_specs=(hbm, hbm),
        scratch_shapes=[
            pltpu.VMEM((rows, q_cols), BF16),
            pltpu.VMEM((stretches, length, kv_width), BF16),
            dma((stretches + 1,)),
            dma((stretches + 1,)),
        ],
        name="hand_over",
    )(attn_out, new_store)


def solution(mesh):
    placed = (
        P("cache", None),
        P(),
        P("cache", "heads"),
        P("heads"),
        P("cache", None),
        P(),
        P("heads", "cache"),
        P("cache", "heads", None, None),
        P(),
        P(),
        P(),
    )
    return jax.shard_map(
        shards,
        mesh=mesh,
        in_specs=placed,
        out_specs=(P("cache", "heads"), P("cache", "heads", None, None)),
        check_vma=False,
    )
```

```python
import functools
import math

import jax
import jax.numpy as jnp
from jax import lax
from jax.experimental import pallas as pl
from jax.experimental.pallas import tpu as pltpu
from jax.sharding import PartitionSpec as P

MESH = pl.DeviceIdType.MESH
SIDE = 4
BF16 = jnp.bfloat16
F32 = jnp.float32
RIGHT, OPPOSITE, LEFT = 1, 2, 3
PAD = 32


def remote(src, dst, send_sem, recv_sem, device):
    return pltpu.make_async_remote_copy(
        src_ref=src, dst_ref=dst, send_sem=send_sem, recv_sem=recv_sem, device_id=device, device_id_type=MESH
    )


def blend(old, keys, values, rows):
    hd = keys.shape[1]
    hit = lax.broadcasted_iota(jnp.int32, (old.shape[0], PAD), 0) == rows
    table = jnp.concatenate([keys, values, jnp.ones((PAD, hd), BF16)], axis=1)
    new = jnp.dot(hit.astype(F32).astype(BF16), table, preferred_element_type=F32)
    there = new[:, 2 * hd :] > 0.5
    parts = [
        jnp.where(there, new[:, i * hd : (i + 1) * hd], old[:, i * hd : (i + 1) * hd].astype(F32)).astype(BF16)
        for i in (0, 1)
    ]
    return parts[0], parts[1]


def attend(q_ref, row_ref, ctx_ref, ks, vs, sc, top, low, out, flat):
    stretches, length = ks.shape[0], ks.shape[1]
    hd = q_ref.shape[1]
    total = q_ref.shape[0]
    group = total // stretches
    heads = ctx_ref.shape[1] // hd
    per = group // heads
    scale = math.log2(math.e) / math.sqrt(hd)
    top[...] = jnp.full_like(top, -jnp.inf)
    low[...] = jnp.zeros_like(low)
    out[...] = jnp.zeros_like(out)

    def fold(a, op):
        parts = [a[:, i * hd : (i + 1) * hd] for i in range(length // hd)]
        while len(parts) > 1:
            parts = [op(parts[i], parts[i + 1]) for i in range(0, len(parts), 2)]
        return parts[0]

    columns = jnp.transpose(row_ref[...].astype(F32))
    base = [sum(total - t * group for t in range(s)) for s in range(stretches)]
    for s in range(stretches):
        scores = lax.dot_general(
            q_ref[s * group :, :], ks[s], (((1,), (1,)), ((), ())), preferred_element_type=F32
        )
        key = lax.broadcasted_iota(jnp.int32, (group, length), 1).astype(F32)
        last = jnp.concatenate([columns[0:per, s : s + 1]] * heads, axis=0)
        first = jnp.where(key <= last, scores[:group], -jnp.inf)
        sc[base[s] : base[s] + group, :] = first
        top[s * group : (s + 1) * group, :] = jnp.maximum(
            top[s * group : (s + 1) * group, :], fold(first, jnp.maximum)
        )
        if s + 1 < stretches:
            sc[base[s] + group : base[s] + total - s * group, :] = scores[group:]
            top[(s + 1) * group :, :] = jnp.maximum(top[(s + 1) * group :, :], fold(scores[group:], jnp.maximum))
    top[...] = jnp.broadcast_to(jnp.max(top[...], axis=1, keepdims=True), top.shape)
    for s in range(stretches):
        here = slice(s * group, total)
        held = slice(base[s], base[s] + total - s * group)
        peak = top[here, :]
        expon = jnp.concatenate(
            [jnp.exp2((sc[held, i * hd : (i + 1) * hd] - peak) * scale) for i in range(length // hd)], axis=1
        )
        low[here, :] += fold(expon, jnp.add)
        out[here, :] += jnp.dot(expon.astype(BF16), vs[s], preferred_element_type=F32)
    out[...] = out[...] / jnp.sum(low[...], axis=1, keepdims=True)
    for r in range(stretches):
        for j in range(heads):
            at_row = (r * heads + j) * per
            flat[r * per : (r + 1) * per, j * hd : (j + 1) * hd] = out[at_row : at_row + per, :]
    ctx_ref[...] = flat[...].astype(BF16)


def prefill(
    table_ref, req_ref, hid_hbm, gain_ref, qw_hbm, kvw_hbm, qb_ref, kvb_ref, ow_hbm, store_hbm, rec_ref,
    out_ref, new_hbm,
    hid, acts, w, acc, part, sums, hop_in, hop_out, qs, fpad, my_rows, slot_rows,
    queries, own_fresh, fresh, blocks, ks, vs, sc, top, low, res, flat, ctx,
    ow, ctxs, chunk, r_out, l_out, r_in, l_in, done, f_out, f_in, back, old, new,
    loc, w_send, w_recv, a_send, a_recv, c_send, c_recv, s_send, s_recv,
    h1_send, h1_recv, h2_send, h2_recv, x_send, x_recv,
    o_send, o_recv, oo_send, oo_recv, t_send, t_recv,
    r_send, r_recv, l_send, l_recv, f_send, f_recv, n_sem,
):
    me = lax.axis_index("cache")
    head = lax.axis_index("heads")
    core = lax.rem(head, 2)
    partner = (me, head + 1 - 2 * core)
    x, y = me // SIDE, lax.rem(me, SIDE)
    z = head // 2
    owners = SIDE * SIDE
    levels = lax.axis_size("heads") // 2
    right = (me, lax.rem(z + 1, levels) * 2 + core)
    left = (me, lax.rem(z + levels - 1, levels) * 2 + core)
    turn = lax.rem(head, SIDE)
    mirror = (x * SIDE + turn, head - turn + y)
    rows = hid.shape[0]
    depth, width = w.shape[1], w.shape[2]
    q_cols = qw_hbm.shape[1]
    hd = width - q_cols
    per = rows // 8

    def ring(i, d):
        return lax.rem(i + d, SIDE)

    own_hid = pltpu.make_async_copy(hid_hbm, hid, loc.at[2])
    own_q = pltpu.make_async_copy(qw_hbm, w.at[x, :, 0:q_cols], loc.at[0])
    own_kv = pltpu.make_async_copy(
        kvw_hbm.at[:, pl.ds(pl.multiple_of(head * hd, hd), hd)], w.at[x, :, q_cols:width], loc.at[1]
    )
    own_hop = pltpu.make_async_copy(store_hbm.at[:, me, core], hop_in.at[pl.ds(me * 8, 8)], loc.at[3])
    own_hid.start()
    own_q.start()
    own_kv.start()
    own_hop.start()
    own_ow = pltpu.make_async_copy(ow_hbm, ow.at[core, x], loc.at[5 + SIDE])
    own_ow.start()
    old_in = pltpu.make_async_copy(store_hbm, old, loc.at[6 + SIDE])
    old_in.start()

    barrier = pltpu.get_barrier_semaphore()

    @pl.loop(1, owners)
    def _(o):
        pl.semaphore_signal(barrier, inc=1, device_id=(lax.rem(me + o, owners), head), device_id_type=MESH)

    for peer in (partner, left, right):
        pl.semaphore_signal(barrier, inc=1, device_id=peer, device_id_type=MESH)
    for d in (RIGHT, OPPOSITE, LEFT):
        across = (x * SIDE + ring(y, d), head + 1 - 2 * core)
        pl.semaphore_signal(barrier, inc=1, device_id=across, device_id_type=MESH)

    @pl.when(turn != y)
    def _():
        pl.semaphore_signal(barrier, inc=1, device_id=mirror, device_id_type=MESH)

    @pl.when(turn != y)
    def _():
        pl.semaphore_wait(barrier, owners + 6)

    @pl.when(turn == y)
    def _():
        pl.semaphore_wait(barrier, owners + 5)

    def slice_of(c):
        return hid.at[:, pl.ds(pl.multiple_of(c * depth, depth), depth)]

    def rows_to(d, i):
        to = ring(y, d)
        return remote(
            slice_of((2 * core + i) * SIDE + to), acts.at[2 * core + i, y], a_send.at[d, i], a_recv.at[d, i],
            (x * SIDE + to, head),
        )

    def hop1(o):
        to = lax.rem(me + o, owners)
        return remote(
            store_hbm.at[:, to, core], hop_in.at[pl.ds(me * 8, 8)], h1_send.at[o], h1_recv.at[me], (to, head)
        )

    def hop1_from(o):
        src = lax.rem(me + owners - o, owners)
        return remote(
            store_hbm.at[:, src, core], hop_in.at[pl.ds(src * 8, 8)], h1_send.at[o], h1_recv.at[src], (src, head)
        )

    def hop2(o):
        to = lax.rem(me + o, owners)
        return remote(hop_out.at[to], blocks.at[:, me, core], h2_send.at[o], h2_recv.at[me], (to, head))

    def hop2_from(o):
        src = lax.rem(me + owners - o, owners)
        return remote(hop_out.at[src], blocks.at[:, src, core], h2_send.at[o], h2_recv.at[src], (src, head))

    class Ring4:
        def __init__(self, source, place, send_sem, recv_sem):
            self.source, self.place, self.send_sem, self.recv_sem = source, place, send_sem, recv_sem
            self.deep = place(0).shape[0] // 2

        def part(self, ref, half):
            return ref.at[pl.ds(half * self.deep, self.deep)]

        def copy(self, d, half, passed=False):
            to = (ring(x, d) * SIDE + y, head)
            src = self.part(self.place(ring(x, SIDE - d)) if passed else self.source, half)
            dst = self.part(self.place(ring(x, SIDE - d) if passed else x), half)
            k = OPPOSITE if passed else d
            return remote(src, dst, self.send_sem.at[k, half], self.recv_sem.at[k, half], to)

        def wait(self, d, half):
            place = self.part(self.place(ring(x, SIDE - d)), half)
            remote(
                place, place, self.send_sem.at[d, half], self.recv_sem.at[d, half],
                (ring(x, SIDE - d) * SIDE + y, head),
            ).wait_recv()

        def start(self):
            self.copy(RIGHT, 0).start()
            self.copy(LEFT, 1).start()

        def rest(self):
            self.copy(RIGHT, 1).start()
            self.copy(LEFT, 0).start()

        def forward(self):
            self.wait(RIGHT, 0)
            self.copy(RIGHT, 0, True).start()
            self.wait(LEFT, 1)
            self.copy(LEFT, 1, True).start()

        def wait_rest(self):
            self.wait(RIGHT, 1)
            self.wait(LEFT, 0)

        def wait_opposite(self):
            self.wait(OPPOSITE, 0)
            self.wait(OPPOSITE, 1)

        def finish(self):
            for half in (0, 1):
                self.copy(RIGHT, half).wait_send()
                self.copy(LEFT, half).wait_send()
            self.copy(RIGHT, 0, True).wait_send()
            self.copy(LEFT, 1, True).wait_send()

    weights = Ring4(w.at[x], lambda i: w.at[i], w_send, w_recv)
    ow_blocks = Ring4(ow_hbm, lambda i: ow.at[core, i], o_send, o_recv)

    steps = (RIGHT, LEFT, OPPOSITE)
    own_q.wait()
    own_kv.wait()
    weights.start()

    @pl.loop(1, owners)
    def _(o):
        hop1(o).start()

    own_hid.wait()
    tall = 16

    @pl.loop(0, rows // tall)
    def _(i):
        lines = pl.ds(pl.multiple_of(i * tall, tall), tall)
        total = jnp.zeros((tall, 1), F32)
        for c in range(owners):
            v = hid[lines, c * depth : (c + 1) * depth].astype(F32)
            total += jnp.sum(v * v, axis=-1, keepdims=True)
        factor = lax.rsqrt(total / (owners * depth) + 1e-06)
        for c in range(owners):
            v = hid[lines, c * depth : (c + 1) * depth].astype(F32)
            g = gain_ref[c * depth : (c + 1) * depth].astype(F32).reshape(1, depth)
            hid[lines, c * depth : (c + 1) * depth] = (v * factor * g).astype(BF16)

    for i in (0, 1):
        for d in steps:
            rows_to(d, i).start()
    weights.rest()

    for i in range(SIDE):
        pltpu.make_async_copy(slice_of(i * SIDE + y), acts.at[i, y], loc.at[5 + i]).start()

    def place_of(i, r):
        return table_ref[req_ref[r, i]]

    my_owner = [place_of(me, r) // 8 for r in range(8)]
    my_rank = [sum([(my_owner[q] == my_owner[r]).astype(jnp.int32) for q in range(r)], 0) for r in range(8)]

    def find(n, found):
        here = place_of(n // 8, lax.rem(n, 8)) - me * 8
        return tuple(jnp.where(here == s, n, found[s]) for s in range(8))

    found = lax.fori_loop(0, owners * 8, find, (jnp.int32(0),) * 8)
    my_rows[...] = jnp.full_like(my_rows, -1)
    slot_rows[...] = jnp.full_like(slot_rows, -1)
    my_rows[:, 0:per] = rec_ref[me]
    picks = []
    for s in range(8):
        i, r = found[s] // 8, lax.rem(found[s], 8)
        slot_rows[s : s + 1, 0:per] = rec_ref[i, pl.ds(r, 1), :]
        rank = sum([((q < r) & (place_of(i, q) // 8 == me)).astype(jnp.int32) for q in range(8)], 0)
        picks.append(2 * i + jnp.minimum(rank, 1))

    weights.forward()

    def rows_from(d, i, which):
        src = ring(y, SIDE - d)
        place = acts.at[2 * which + i, src]
        return remote(place, place, a_send.at[d, i], a_recv.at[d, i], (x * SIDE + src, head))

    def rows_over(d, i, which):
        place = acts.at[2 * which + i, ring(y, SIDE - d)]
        return remote(place, place, c_send.at[d, i], c_recv.at[d, i], partner)

    for i in (0, 1):
        for d in steps:
            rows_from(d, i, core).wait_recv()
            rows_over(d, i, core).start()

    own_hop.wait()

    @pl.loop(1, owners)
    def _(o):
        hop1_from(o).wait_recv()

    def sort(i):
        for r in range(8):
            hop_out[i, r] = hop_in[place_of(i, r)]

    @pl.loop(1, owners)
    def _(o):
        sort(lax.rem(me + o, owners))
        hop2(o).start()

    sort(me)
    own_out = pltpu.make_async_copy(hop_out.at[me], blocks.at[:, me, core], loc.at[4])
    own_out.start()

    for i in range(SIDE):
        pltpu.make_async_copy(slice_of(i * SIDE + y), acts.at[i, y], loc.at[5 + i]).wait()
    weights.wait_rest()
    weights.wait_opposite()

    def product(i, j):
        return jnp.dot(acts[i, j], w[i], preferred_element_type=F32)

    @pl.loop(0, SIDE)
    def _(j):
        acc[j] = product(2 * core, j)
        acc[j] += product(2 * core + 1, j)

    for i in (0, 1):
        for d in steps:
            rows_over(d, i, 1 - core).wait_recv()

    def sums_to(d):
        to = ring(y, d)
        return remote(part.at[d], sums.at[d], s_send.at[d], s_recv.at[d], (x * SIDE + to, head))

    for d in (OPPOSITE, RIGHT, LEFT):
        j = ring(y, d)
        acc[j] += product(2 - 2 * core, j)
        part[d] = (acc[j] + product(3 - 2 * core, j)).astype(BF16)
        sums_to(d).start()

    def block_from(d, which):
        place = ow.at[which, ring(x, SIDE - d)]
        return remote(place, place, oo_send.at[d], oo_recv.at[d], partner)

    ow_blocks.start()
    ow_blocks.rest()
    own_ow.wait()
    block_from(0, core).start()
    acc[y] += product(2 - 2 * core, y)
    acc[y] += product(3 - 2 * core, y)

    for d in steps:
        remote(part.at[d], sums.at[d], s_send.at[d], s_recv.at[d], (x * SIDE + ring(y, SIDE - d), head)).wait_recv()
        acc[y] += sums[d].astype(F32)

    heads = q_cols // hd
    bias = qb_ref[...].astype(F32).reshape(1, q_cols)
    both = kvb_ref[pl.ds(pl.multiple_of(z * 2 * hd, 2 * hd), 2 * hd)].astype(F32).reshape(1, 2 * hd)
    kv_bias = jnp.where(core == 0, both[:, 0:hd], both[:, hd:])
    for r in range(8):
        lines = slice(per * r, per * (r + 1))
        for j in range(heads):
            at_row = (j // 2 * 16 + r * 2 + j % 2) * per
            qs[at_row : at_row + per, :] = acc[y, lines, j * hd : (j + 1) * hd] + bias[:, j * hd : (j + 1) * hd]
        fpad[r * PAD : r * PAD + per, :] = acc[y, lines, q_cols:width] + kv_bias
        fpad[r * PAD + per : (r + 1) * PAD, :] = jnp.zeros((PAD - per, hd), F32)
    own_fresh[...] = fpad[...].astype(BF16).reshape(own_fresh.shape)
    fresh[core] = own_fresh[...]
    swap = remote(own_fresh, fresh.at[core], x_send.at[1], x_recv.at[1], partner)
    swap.start()
    queries[...] = qs[...].astype(BF16)

    @pl.loop(0, owners)
    def _(o):
        for m in range(2):
            row = sum([jnp.where((my_owner[r] == o) & (my_rank[r] == m), r, 0) for r in range(8)], 0)
            f_out[2 * o + m] = own_fresh[row]

    def give(o):
        to = lax.rem(me + o, owners)
        return remote(
            f_out.at[pl.ds(2 * to, 2)], f_in.at[pl.ds(2 * me, 2)], f_send.at[o], f_recv.at[me], (to, head)
        )

    def take(o):
        src = lax.rem(me + owners - o, owners)
        return remote(
            f_out.at[pl.ds(2 * src, 2)], f_in.at[pl.ds(2 * src, 2)], f_send.at[o], f_recv.at[src], (src, head)
        )

    @pl.loop(1, owners)
    def _(o):
        give(o).start()

    for m in range(2):
        f_in[2 * me + m] = f_out[2 * me + m]

    def core_swap(which):
        return remote(
            blocks.at[:, :, which], blocks.at[:, :, which], x_send.at[0], x_recv.at[0], partner
        )

    own_out.wait()

    @pl.loop(1, owners)
    def _(o):
        hop2_from(o).wait_recv()

    core_swap(core).start()

    ow_blocks.forward()
    core_swap(1 - core).wait_recv()
    remote(fresh.at[1 - core], fresh.at[1 - core], x_send.at[1], x_recv.at[1], partner).wait_recv()

    for r in range(8):
        old_rows = blocks[r].reshape(ks.shape[1], 2 * hd)
        ks[r], vs[r] = blend(old_rows, fresh[0, r], fresh[1, r], my_rows[r : r + 1, 0:PAD])

    def ctx_to(d, pair):
        to = ring(y, d)
        return remote(
            ctx.at[pair], ctxs.at[y // 2, core, pair], t_send.at[d, pair], t_recv.at[d, core, pair],
            (x * SIDE + to, 2 * z + lax.rem(y, 2)),
        )

    def ctx_from(d, which, pair):
        src = ring(y, SIDE - d)
        place = ctxs.at[src // 2, which, pair]
        return remote(
            place, place, t_send.at[d, pair], t_recv.at[d, which, pair], (x * SIDE + src, 2 * z + which)
        )

    mine = lax.rem(y, 2) == core

    for pair in (0, 1):
        lines = pl.ds(pair * queries.shape[0] // 2, queries.shape[0] // 2)
        attend(queries.at[lines], my_rows, ctx.at[pair], ks, vs, sc, top, low, res, flat)
        for d in (RIGHT, LEFT, OPPOSITE):
            ctx_to(d, pair).start()

        @pl.when(mine)
        def _():
            ctxs[y // 2, core, pair] = ctx[pair]

        @pl.when(jnp.logical_not(mine))
        def _():
            ctx_to(0, pair).start()

    ow_blocks.wait_rest()
    block_from(RIGHT, core).start()
    block_from(LEFT, core).start()

    @pl.loop(1, owners)
    def _(o):
        take(o).wait_recv()

    for s in range(8):
        back[core, s] = f_in[picks[s]]
    swap_back = remote(back.at[core], back.at[core], x_send.at[2], x_recv.at[2], partner)
    swap_back.start()

    def renew(s):
        keys, values = blend(old[s].reshape(new.shape[1], 2 * hd), back[0, s], back[1, s], slot_rows[s : s + 1, 0:PAD])
        new[s, :, 0:hd] = keys
        new[s, :, hd : 2 * hd] = values
        pltpu.make_async_copy(new.at[s], new_hbm.at[s], n_sem.at[s]).start()

    old_in.wait()
    remote(back.at[1 - core], back.at[1 - core], x_send.at[2], x_recv.at[2], partner).wait_recv()
    for s in range(8):
        renew(s)

    @pl.when(mine)
    def _():
        for pair in (0, 1):
            ctx_from(0, 1 - core, pair).wait_recv()
            for which in (0, 1):
                ctx_from(OPPOSITE, which, pair).wait_recv()

    @pl.when(jnp.logical_not(mine))
    def _():
        for d in (RIGHT, LEFT):
            for which in (0, 1):
                for pair in (0, 1):
                    ctx_from(d, which, pair).wait_recv()

    ow_blocks.wait_opposite()
    block_from(OPPOSITE, core).start()
    for d in (0,) + steps:
        block_from(d, 1 - core).wait_recv()

    hrow = rows // 2
    order = (4, 3, -3, 2, -2, 1, -1, 0)

    def compute(n):
        target = lax.rem(z + order[n] + levels, levels)
        column, request = target // 2, lax.rem(target, 2)
        total = None
        for which in (0, 1):
            both = jnp.concatenate([ctxs[request, which, 0], ctxs[request, which, 1]], axis=1)
            term = jnp.dot(both, ow[which, column], preferred_element_type=F32)
            total = term if total is None else total + term
        chunk[n] = total

    def lines_of(half):
        return slice(half * hrow, (half + 1) * hrow)

    def ring_copy(step, half, out, into, send_sem, recv_sem, to):
        return remote(
            out.at[step, pl.ds(half * hrow, hrow)],
            into.at[step, pl.ds(half * hrow, hrow)],
            send_sem.at[step, half],
            recv_sem.at[step, half],
            to,
        )

    def rightward(step, half):
        return ring_copy(step, half, r_out, r_in, r_send, r_recv, right)

    def leftward(step, half):
        return ring_copy(step, half, l_out, l_in, l_send, l_recv, left)

    compute(0)
    r_out[0, lines_of(0), :] = chunk[0, lines_of(0), :].astype(BF16)
    rightward(0, 0).start()
    l_out[0, lines_of(1), :] = chunk[0, lines_of(1), :].astype(BF16)
    leftward(0, 1).start()
    compute(1)
    compute(2)
    for step in (1, 2, 3):
        n_right, n_left = 2 * step - 1, 2 * step
        halves = ((1, 0), (0, 1)) if step == 1 else ((0, 1), (1, 0))
        for right_half, left_half in halves:
            value = chunk[n_right, lines_of(right_half), :]
            if step > 1 or right_half == 0:
                rightward(step - 1, right_half).wait_recv()
                value += r_in[step - 1, lines_of(right_half), :].astype(F32)
            r_out[step, lines_of(right_half), :] = value.astype(BF16)
            rightward(step, right_half).start()
            value = chunk[n_left, lines_of(left_half), :]
            if step > 1 or left_half == 1:
                leftward(step - 1, left_half).wait_recv()
                value += l_in[step - 1, lines_of(left_half), :].astype(F32)
            l_out[step, lines_of(left_half), :] = value.astype(BF16)
            leftward(step, left_half).start()
        if step < 3:
            compute(2 * step + 1)
            compute(2 * step + 2)
        else:
            compute(7)

    def flip(half):
        return remote(
            done.at[pl.ds(half * hrow, hrow)], out_ref.at[pl.ds(half * hrow, hrow)],
            x_send.at[3 + half], x_recv.at[3 + half], mirror,
        )

    for half in (0, 1):
        rightward(3, half).wait_recv()
        leftward(3, half).wait_recv()
        value = chunk[7, lines_of(half), :] + r_in[3, lines_of(half), :].astype(F32)
        value += l_in[3, lines_of(half), :].astype(F32)
        done[lines_of(half), :] = value.astype(BF16)

        @pl.when(turn != y)
        def _():
            flip(half).start()

    @pl.when(turn == y)
    def _():
        out_ref[...] = done[...]

    for i in (0, 1):
        for d in steps:
            rows_to(d, i).wait_send()
            rows_over(d, i, core).wait_send()
    for d in steps:
        sums_to(d).wait_send()
        for pair in (0, 1):
            ctx_to(d, pair).wait_send()
    weights.finish()
    ow_blocks.finish()
    for d in (0,) + steps:
        block_from(d, core).wait_send()

    @pl.when(jnp.logical_not(mine))
    def _():
        for pair in (0, 1):
            ctx_to(0, pair).wait_send()

    @pl.loop(1, owners)
    def _(o):
        hop1(o).wait_send()
        hop2(o).wait_send()
        give(o).wait_send()

    core_swap(core).wait_send()
    swap.wait_send()
    swap_back.wait_send()
    rightward(0, 0).wait_send()
    leftward(0, 1).wait_send()
    for step in (1, 2, 3):
        for half in (0, 1):
            rightward(step, half).wait_send()
            leftward(step, half).wait_send()
    for s in range(8):
        pltpu.make_async_copy(new.at[s], new_hbm.at[s], n_sem.at[s]).wait()

    @pl.when(turn != y)
    def _():
        for half in (0, 1):
            flip(half).wait()


def hand_over(out_ref, store_ref, out_copy, store_copy, out_held, held, sem_in, sem_out):
    count = store_ref.shape[0]
    ins = [pltpu.make_async_copy(store_ref.at[s], held.at[s], sem_in.at[s]) for s in range(count)]
    ins.append(pltpu.make_async_copy(out_ref, out_held, sem_in.at[count]))
    outs = [pltpu.make_async_copy(held.at[s], store_copy.at[s, 0], sem_out.at[s]) for s in range(count)]
    outs.append(pltpu.make_async_copy(out_held, out_copy, sem_out.at[count]))
    for copy in ins:
        copy.start()
    for copy_in, copy_out in zip(ins, outs):
        copy_in.wait()
        copy_out.start()
    for copy in outs:
        copy.wait()


def shards(
    hidden, norm_gain, q_weight, q_bias, kv_weight, kv_bias, out_weight, kv_store, stretch_place, req_stretches, rec_rows
):
    owners = lax.axis_size("cache")
    me = lax.axis_index("cache")
    rows, width = hidden.shape
    stretches, _, length, kv_width = kv_store.shape
    hd = kv_width // 2
    per = rec_rows.shape[2]
    depth, q_cols = q_weight.shape
    levels = lax.axis_size("heads") // 2
    heads = q_cols // hd
    vmem = pl.BlockSpec(memory_space=pltpu.VMEM)
    smem = pl.BlockSpec(memory_space=pltpu.SMEM)
    hbm = pl.BlockSpec(memory_space=pl.ANY)
    dma = pltpu.SemaphoreType.DMA

    store = kv_store.reshape(stretches, owners, 2, length // (2 * owners), kv_width)
    piece = length // (2 * owners)

    attn_out, new_store = pl.pallas_call(
        prefill,
        out_shape=(
            jax.ShapeDtypeStruct((rows, q_cols), BF16),
            jax.ShapeDtypeStruct((stretches, length, kv_width), BF16),
        ),
        in_specs=[smem, smem, hbm, vmem, hbm, hbm, vmem, vmem, hbm, hbm, vmem],
        out_specs=(vmem, hbm),
        scratch_shapes=[
            pltpu.VMEM((rows, width), BF16),
            pltpu.VMEM((SIDE, SIDE, rows, depth), BF16),
            pltpu.VMEM((SIDE, depth, q_cols + hd), BF16),
            pltpu.VMEM((SIDE, rows, q_cols + hd), F32),
            pltpu.VMEM((SIDE, rows, q_cols + hd), BF16),
            pltpu.VMEM((SIDE, rows, q_cols + hd), BF16),
            pltpu.VMEM((owners * stretches, piece, kv_width), BF16),
            pltpu.VMEM((owners, stretches, piece, kv_width), BF16),
            pltpu.VMEM((rows * heads, hd), F32),
            pltpu.VMEM((stretches * PAD, hd), F32),
            pltpu.VMEM((stretches, hd), jnp.int32),
            pltpu.VMEM((stretches, hd), jnp.int32),
            pltpu.VMEM((rows * heads, hd), BF16),
            pltpu.VMEM((stretches, PAD, hd), BF16),
            pltpu.VMEM((2, stretches, PAD, hd), BF16),
            pltpu.VMEM((stretches, owners, 2, piece, kv_width), BF16),
            pltpu.VMEM((stretches, length, hd), BF16),
            pltpu.VMEM((stretches, length, hd), BF16),
            pltpu.VMEM((rows * heads * (stretches + 1) // 4, length), F32),
            pltpu.VMEM((rows * heads // 2, hd), F32),
            pltpu.VMEM((rows * heads // 2, hd), F32),
            pltpu.VMEM((rows * heads // 2, hd), F32),
            pltpu.VMEM((rows, q_cols // 2), F32),
            pltpu.VMEM((2, rows, q_cols // 2), BF16),
            pltpu.VMEM((2, SIDE, depth, q_cols), BF16),
            pltpu.VMEM((2, 2, 2, rows, q_cols // 2), BF16),
            pltpu.VMEM((levels, rows, q_cols), F32),
            pltpu.VMEM((4, rows, q_cols), BF16),
            pltpu.VMEM((4, rows, q_cols), BF16),
            pltpu.VMEM((4, rows, q_cols), BF16),
            pltpu.VMEM((4, rows, q_cols), BF16),
            pltpu.VMEM((rows, q_cols), BF16),
            pltpu.VMEM((2 * owners, PAD, hd), BF16),
            pltpu.VMEM((2 * owners, PAD, hd), BF16),
            pltpu.VMEM((2, stretches, PAD, hd), BF16),
            pltpu.VMEM((stretches, owners, 2, piece, kv_width), BF16),
            pltpu.VMEM((stretches, length, kv_width), BF16),
            dma((7 + SIDE,)),
            dma((SIDE, 2)),
            dma((SIDE, 2)),
            dma((SIDE, 2)),
            dma((SIDE, 2)),
            dma((SIDE, 2)),
            dma((SIDE, 2)),
            dma((SIDE,)),
            dma((SIDE,)),
            dma((owners,)),
            dma((owners,)),
            dma((owners,)),
            dma((owners,)),
            dma((5,)),
            dma((5,)),
            dma((SIDE, 2)),
            dma((SIDE, 2)),
            dma((SIDE,)),
            dma((SIDE,)),
            dma((SIDE, 2)),
            dma((SIDE, 2, 2)),
            dma((4, 2)),
            dma((4, 2)),
            dma((4, 2)),
            dma((4, 2)),
            dma((owners,)),
            dma((owners,)),
            dma((8,)),
        ],
        compiler_params=pltpu.CompilerParams(collective_id=0, has_side_effects=True, vmem_limit_bytes=58 << 20),
        name="prefill",
    )(
        stretch_place, req_stretches.T, hidden, norm_gain, q_weight, kv_weight, q_bias, kv_bias, out_weight, store, rec_rows
    )
    return pl.pallas_call(
        hand_over,
        out_shape=(
            jax.ShapeDtypeStruct((rows, q_cols), BF16),
            jax.ShapeDtypeStruct((stretches, 1, length, kv_width), BF16),
        ),
        in_specs=[hbm, hbm],
        out_specs=(hbm, hbm),
        scratch_shapes=[
            pltpu.VMEM((rows, q_cols), BF16),
            pltpu.VMEM((stretches, length, kv_width), BF16),
            dma((stretches + 1,)),
            dma((stretches + 1,)),
        ],
        name="hand_over",
    )(attn_out, new_store)


def solution(mesh):
    placed = (
        P("cache", None),
        P(),
        P("cache", "heads"),
        P("heads"),
        P("cache", None),
        P(),
        P("heads", "cache"),
        P("cache", "heads", None, None),
        P(),
        P(),
        P(),
    )
    return jax.shard_map(
        shards,
        mesh=mesh,
        in_specs=placed,
        out_specs=(P("cache", "heads"), P("cache", "heads", None, None)),
        check_vma=False,
    )
```

```python
import functools
import math

import jax
import jax.numpy as jnp
from jax import lax
from jax.experimental import pallas as pl
from jax.experimental.pallas import tpu as pltpu
from jax.sharding import PartitionSpec as P

MESH = pl.DeviceIdType.MESH
SIDE = 4
BF16 = jnp.bfloat16
F32 = jnp.float32
RIGHT, OPPOSITE, LEFT = 1, 2, 3
PAD = 32


def remote(src, dst, send_sem, recv_sem, device):
    return pltpu.make_async_remote_copy(
        src_ref=src, dst_ref=dst, send_sem=send_sem, recv_sem=recv_sem, device_id=device, device_id_type=MESH
    )


def blend(old, keys, values, rows):
    hd = keys.shape[1]
    hit = lax.broadcasted_iota(jnp.int32, (old.shape[0], PAD), 0) == rows
    table = jnp.concatenate([keys, values, jnp.ones((PAD, hd), BF16)], axis=1)
    new = jnp.dot(hit.astype(F32).astype(BF16), table, preferred_element_type=F32)
    there = new[:, 2 * hd :] > 0.5
    parts = [
        jnp.where(there, new[:, i * hd : (i + 1) * hd], old[:, i * hd : (i + 1) * hd].astype(F32)).astype(BF16)
        for i in (0, 1)
    ]
    return parts[0], parts[1]


def attend(q_ref, row_ref, ctx_ref, ks, vs, sc, top, low, out, flat):
    stretches, length = ks.shape[0], ks.shape[1]
    hd = q_ref.shape[1]
    total = q_ref.shape[0]
    group = total // stretches
    heads = ctx_ref.shape[1] // hd
    per = group // heads
    scale = math.log2(math.e) / math.sqrt(hd)
    top[...] = jnp.full_like(top, -jnp.inf)
    low[...] = jnp.zeros_like(low)
    out[...] = jnp.zeros_like(out)

    def fold(a, op):
        parts = [a[:, i * hd : (i + 1) * hd] for i in range(length // hd)]
        while len(parts) > 1:
            parts = [op(parts[i], parts[i + 1]) for i in range(0, len(parts), 2)]
        return parts[0]

    columns = jnp.transpose(row_ref[...].astype(F32))
    base = [sum(total - t * group for t in range(s)) for s in range(stretches)]
    for s in range(stretches):
        scores = lax.dot_general(
            q_ref[s * group :, :], ks[s], (((1,), (1,)), ((), ())), preferred_element_type=F32
        )
        key = lax.broadcasted_iota(jnp.int32, (group, length), 1).astype(F32)
        last = jnp.concatenate([columns[0:per, s : s + 1]] * heads, axis=0)
        first = jnp.where(key <= last, scores[:group], -jnp.inf)
        sc[base[s] : base[s] + group, :] = first
        top[s * group : (s + 1) * group, :] = jnp.maximum(
            top[s * group : (s + 1) * group, :], fold(first, jnp.maximum)
        )
        if s + 1 < stretches:
            sc[base[s] + group : base[s] + total - s * group, :] = scores[group:]
            top[(s + 1) * group :, :] = jnp.maximum(top[(s + 1) * group :, :], fold(scores[group:], jnp.maximum))
    top[...] = jnp.broadcast_to(jnp.max(top[...], axis=1, keepdims=True), top.shape)
    for s in range(stretches):
        here = slice(s * group, total)
        held = slice(base[s], base[s] + total - s * group)
        peak = top[here, :]
        expon = jnp.concatenate(
            [jnp.exp2((sc[held, i * hd : (i + 1) * hd] - peak) * scale) for i in range(length // hd)], axis=1
        )
        low[here, :] += fold(expon, jnp.add)
        out[here, :] += jnp.dot(expon.astype(BF16), vs[s], preferred_element_type=F32)
    out[...] = out[...] / jnp.sum(low[...], axis=1, keepdims=True)
    for r in range(stretches):
        for j in range(heads):
            at_row = (r * heads + j) * per
            flat[r * per : (r + 1) * per, j * hd : (j + 1) * hd] = out[at_row : at_row + per, :]
    ctx_ref[...] = flat[...].astype(BF16)


def prefill(
    table_ref, req_ref, hid_hbm, gain_ref, qw_hbm, kvw_hbm, qb_ref, kvb_ref, ow_hbm, store_hbm, rec_ref,
    out_ref, new_hbm,
    hid, acts, w, acc, part, sums, hop_in, hop_out, qs, fpad, my_rows, slot_rows,
    queries, own_fresh, fresh, blocks, ks, vs, sc, top, low, res, flat, ctx,
    ow, ctxs, chunk, r_out, l_out, r_in, l_in, done, f_out, f_in, back, old, new,
    loc, w_send, w_recv, a_send, a_recv, c_send, c_recv, s_send, s_recv,
    h1_send, h1_recv, h2_send, h2_recv, x_send, x_recv,
    o_send, o_recv, oo_send, oo_recv, t_send, t_recv,
    r_send, r_recv, l_send, l_recv, f_send, f_recv, n_sem,
):
    me = lax.axis_index("cache")
    head = lax.axis_index("heads")
    core = lax.rem(head, 2)
    partner = (me, head + 1 - 2 * core)
    x, y = me // SIDE, lax.rem(me, SIDE)
    z = head // 2
    owners = SIDE * SIDE
    levels = lax.axis_size("heads") // 2
    right = (me, lax.rem(z + 1, levels) * 2 + core)
    left = (me, lax.rem(z + levels - 1, levels) * 2 + core)
    turn = lax.rem(head, SIDE)
    mirror = (x * SIDE + turn, head - turn + y)
    rows = hid.shape[0]
    depth, width = w.shape[1], w.shape[2]
    q_cols = qw_hbm.shape[1]
    hd = width - q_cols
    per = rows // 8

    def ring(i, d):
        return lax.rem(i + d, SIDE)

    own_hid = pltpu.make_async_copy(hid_hbm, hid, loc.at[2])
    own_q = pltpu.make_async_copy(qw_hbm, w.at[x, :, 0:q_cols], loc.at[0])
    own_kv = pltpu.make_async_copy(
        kvw_hbm.at[:, pl.ds(pl.multiple_of(head * hd, hd), hd)], w.at[x, :, q_cols:width], loc.at[1]
    )
    own_hop = pltpu.make_async_copy(store_hbm.at[:, me, core], hop_in.at[pl.ds(me * 8, 8)], loc.at[3])
    own_hid.start()
    own_q.start()
    own_kv.start()
    own_hop.start()
    own_ow = pltpu.make_async_copy(ow_hbm, ow.at[core, x], loc.at[5 + SIDE])
    own_ow.start()
    old_in = pltpu.make_async_copy(store_hbm, old, loc.at[6 + SIDE])
    old_in.start()

    barrier = pltpu.get_barrier_semaphore()

    @pl.loop(1, owners)
    def _(o):
        pl.semaphore_signal(barrier, inc=1, device_id=(lax.rem(me + o, owners), head), device_id_type=MESH)

    for peer in (partner, left, right):
        pl.semaphore_signal(barrier, inc=1, device_id=peer, device_id_type=MESH)
    for d in (RIGHT, OPPOSITE, LEFT):
        across = (x * SIDE + ring(y, d), head + 1 - 2 * core)
        pl.semaphore_signal(barrier, inc=1, device_id=across, device_id_type=MESH)

    @pl.when(turn != y)
    def _():
        pl.semaphore_signal(barrier, inc=1, device_id=mirror, device_id_type=MESH)

    @pl.when(turn != y)
    def _():
        pl.semaphore_wait(barrier, owners + 6)

    @pl.when(turn == y)
    def _():
        pl.semaphore_wait(barrier, owners + 5)

    def slice_of(c):
        return hid.at[:, pl.ds(pl.multiple_of(c * depth, depth), depth)]

    def rows_to(d, i):
        to = ring(y, d)
        return remote(
            slice_of((2 * core + i) * SIDE + to), acts.at[2 * core + i, y], a_send.at[d, i], a_recv.at[d, i],
            (x * SIDE + to, head),
        )

    def hop1(o):
        to = lax.rem(me + o, owners)
        return remote(
            store_hbm.at[:, to, core], hop_in.at[pl.ds(me * 8, 8)], h1_send.at[o], h1_recv.at[me], (to, head)
        )

    def hop1_from(o):
        src = lax.rem(me + owners - o, owners)
        return remote(
            store_hbm.at[:, src, core], hop_in.at[pl.ds(src * 8, 8)], h1_send.at[o], h1_recv.at[src], (src, head)
        )

    def hop2(o):
        to = lax.rem(me + o, owners)
        return remote(hop_out.at[to], blocks.at[:, me, core], h2_send.at[o], h2_recv.at[me], (to, head))

    def hop2_from(o):
        src = lax.rem(me + owners - o, owners)
        return remote(hop_out.at[src], blocks.at[:, src, core], h2_send.at[o], h2_recv.at[src], (src, head))

    class Ring4:
        def __init__(self, source, place, send_sem, recv_sem):
            self.source, self.place, self.send_sem, self.recv_sem = source, place, send_sem, recv_sem
            self.deep = place(0).shape[0] // 2

        def part(self, ref, half):
            return ref.at[pl.ds(half * self.deep, self.deep)]

        def copy(self, d, half, passed=False):
            to = (ring(x, d) * SIDE + y, head)
            src = self.part(self.place(ring(x, SIDE - d)) if passed else self.source, half)
            dst = self.part(self.place(ring(x, SIDE - d) if passed else x), half)
            k = OPPOSITE if passed else d
            return remote(src, dst, self.send_sem.at[k, half], self.recv_sem.at[k, half], to)

        def wait(self, d, half):
            place = self.part(self.place(ring(x, SIDE - d)), half)
            remote(
                place, place, self.send_sem.at[d, half], self.recv_sem.at[d, half],
                (ring(x, SIDE - d) * SIDE + y, head),
            ).wait_recv()

        def start(self):
            self.copy(RIGHT, 0).start()
            self.copy(LEFT, 1).start()

        def rest(self):
            self.copy(RIGHT, 1).start()
            self.copy(LEFT, 0).start()

        def forward(self):
            self.wait(RIGHT, 0)
            self.copy(RIGHT, 0, True).start()
            self.wait(LEFT, 1)
            self.copy(LEFT, 1, True).start()

        def wait_rest(self):
            self.wait(RIGHT, 1)
            self.wait(LEFT, 0)

        def wait_opposite(self):
            self.wait(OPPOSITE, 0)
            self.wait(OPPOSITE, 1)

        def finish(self):
            for half in (0, 1):
                self.copy(RIGHT, half).wait_send()
                self.copy(LEFT, half).wait_send()
            self.copy(RIGHT, 0, True).wait_send()
            self.copy(LEFT, 1, True).wait_send()

    weights = Ring4(w.at[x], lambda i: w.at[i], w_send, w_recv)
    ow_blocks = Ring4(ow_hbm, lambda i: ow.at[core, i], o_send, o_recv)

    steps = (RIGHT, LEFT, OPPOSITE)
    @pl.loop(1, owners)
    def _(o):
        hop1(o).start()

    own_q.wait()
    own_kv.wait()
    weights.start()

    own_hid.wait()
    tall = 16

    @pl.loop(0, rows // tall)
    def _(i):
        lines = pl.ds(pl.multiple_of(i * tall, tall), tall)
        total = jnp.zeros((tall, 1), F32)
        for c in range(owners):
            v = hid[lines, c * depth : (c + 1) * depth].astype(F32)
            total += jnp.sum(v * v, axis=-1, keepdims=True)
        factor = lax.rsqrt(total / (owners * depth) + 1e-06)
        for c in range(owners):
            v = hid[lines, c * depth : (c + 1) * depth].astype(F32)
            g = gain_ref[c * depth : (c + 1) * depth].astype(F32).reshape(1, depth)
            hid[lines, c * depth : (c + 1) * depth] = (v * factor * g).astype(BF16)

    for i in (0, 1):
        for d in steps:
            rows_to(d, i).start()
    weights.rest()

    for i in range(SIDE):
        pltpu.make_async_copy(slice_of(i * SIDE + y), acts.at[i, y], loc.at[5 + i]).start()

    def place_of(i, r):
        return table_ref[req_ref[r, i]]

    my_owner = [place_of(me, r) // 8 for r in range(8)]
    my_rank = [sum([(my_owner[q] == my_owner[r]).astype(jnp.int32) for q in range(r)], 0) for r in range(8)]

    def find(n, found):
        here = place_of(n // 8, lax.rem(n, 8)) - me * 8
        return tuple(jnp.where(here == s, n, found[s]) for s in range(8))

    found = lax.fori_loop(0, owners * 8, find, (jnp.int32(0),) * 8)
    my_rows[...] = jnp.full_like(my_rows, -1)
    slot_rows[...] = jnp.full_like(slot_rows, -1)
    my_rows[:, 0:per] = rec_ref[me]
    picks = []
    for s in range(8):
        i, r = found[s] // 8, lax.rem(found[s], 8)
        slot_rows[s : s + 1, 0:per] = rec_ref[i, pl.ds(r, 1), :]
        rank = sum([((q < r) & (place_of(i, q) // 8 == me)).astype(jnp.int32) for q in range(8)], 0)
        picks.append(2 * i + jnp.minimum(rank, 1))

    weights.forward()

    def rows_from(d, i, which):
        src = ring(y, SIDE - d)
        place = acts.at[2 * which + i, src]
        return remote(place, place, a_send.at[d, i], a_recv.at[d, i], (x * SIDE + src, head))

    def rows_over(d, i, which):
        place = acts.at[2 * which + i, ring(y, SIDE - d)]
        return remote(place, place, c_send.at[d, i], c_recv.at[d, i], partner)

    for i in (0, 1):
        for d in steps:
            rows_from(d, i, core).wait_recv()
            rows_over(d, i, core).start()

    own_hop.wait()

    @pl.loop(1, owners)
    def _(o):
        hop1_from(o).wait_recv()

    def sort(i):
        for r in range(8):
            hop_out[i, r] = hop_in[place_of(i, r)]

    @pl.loop(1, owners)
    def _(o):
        sort(lax.rem(me + o, owners))
        hop2(o).start()

    sort(me)
    own_out = pltpu.make_async_copy(hop_out.at[me], blocks.at[:, me, core], loc.at[4])
    own_out.start()

    for i in range(SIDE):
        pltpu.make_async_copy(slice_of(i * SIDE + y), acts.at[i, y], loc.at[5 + i]).wait()
    weights.wait_rest()
    weights.wait_opposite()

    def product(i, j):
        return jnp.dot(acts[i, j], w[i], preferred_element_type=F32)

    @pl.loop(0, SIDE)
    def _(j):
        acc[j] = product(2 * core, j)
        acc[j] += product(2 * core + 1, j)

    for i in (0, 1):
        for d in steps:
            rows_over(d, i, 1 - core).wait_recv()

    def sums_to(d):
        to = ring(y, d)
        return remote(part.at[d], sums.at[d], s_send.at[d], s_recv.at[d], (x * SIDE + to, head))

    for d in (OPPOSITE, RIGHT, LEFT):
        j = ring(y, d)
        acc[j] += product(2 - 2 * core, j)
        part[d] = (acc[j] + product(3 - 2 * core, j)).astype(BF16)
        sums_to(d).start()

    def block_from(d, which):
        place = ow.at[which, ring(x, SIDE - d)]
        return remote(place, place, oo_send.at[d], oo_recv.at[d], partner)

    ow_blocks.start()
    ow_blocks.rest()
    own_ow.wait()
    block_from(0, core).start()
    acc[y] += product(2 - 2 * core, y)
    acc[y] += product(3 - 2 * core, y)

    for d in steps:
        remote(part.at[d], sums.at[d], s_send.at[d], s_recv.at[d], (x * SIDE + ring(y, SIDE - d), head)).wait_recv()
        acc[y] += sums[d].astype(F32)

    heads = q_cols // hd
    bias = qb_ref[...].astype(F32).reshape(1, q_cols)
    both = kvb_ref[pl.ds(pl.multiple_of(z * 2 * hd, 2 * hd), 2 * hd)].astype(F32).reshape(1, 2 * hd)
    kv_bias = jnp.where(core == 0, both[:, 0:hd], both[:, hd:])
    for r in range(8):
        lines = slice(per * r, per * (r + 1))
        for j in range(heads):
            at_row = (j // 2 * 16 + r * 2 + j % 2) * per
            qs[at_row : at_row + per, :] = acc[y, lines, j * hd : (j + 1) * hd] + bias[:, j * hd : (j + 1) * hd]
        fpad[r * PAD : r * PAD + per, :] = acc[y, lines, q_cols:width] + kv_bias
        fpad[r * PAD + per : (r + 1) * PAD, :] = jnp.zeros((PAD - per, hd), F32)
    own_fresh[...] = fpad[...].astype(BF16).reshape(own_fresh.shape)
    fresh[core] = own_fresh[...]
    swap = remote(own_fresh, fresh.at[core], x_send.at[1], x_recv.at[1], partner)
    swap.start()
    queries[...] = qs[...].astype(BF16)

    @pl.loop(0, owners)
    def _(o):
        for m in range(2):
            row = sum([jnp.where((my_owner[r] == o) & (my_rank[r] == m), r, 0) for r in range(8)], 0)
            f_out[2 * o + m] = own_fresh[row]

    def give(o):
        to = lax.rem(me + o, owners)
        return remote(
            f_out.at[pl.ds(2 * to, 2)], f_in.at[pl.ds(2 * me, 2)], f_send.at[o], f_recv.at[me], (to, head)
        )

    def take(o):
        src = lax.rem(me + owners - o, owners)
        return remote(
            f_out.at[pl.ds(2 * src, 2)], f_in.at[pl.ds(2 * src, 2)], f_send.at[o], f_recv.at[src], (src, head)
        )

    @pl.loop(1, owners)
    def _(o):
        give(o).start()

    for m in range(2):
        f_in[2 * me + m] = f_out[2 * me + m]

    def core_swap(which):
        return remote(
            blocks.at[:, :, which], blocks.at[:, :, which], x_send.at[0], x_recv.at[0], partner
        )

    own_out.wait()

    @pl.loop(1, owners)
    def _(o):
        hop2_from(o).wait_recv()

    core_swap(core).start()

    ow_blocks.forward()
    core_swap(1 - core).wait_recv()
    remote(fresh.at[1 - core], fresh.at[1 - core], x_send.at[1], x_recv.at[1], partner).wait_recv()

    for r in range(8):
        old_rows = blocks[r].reshape(ks.shape[1], 2 * hd)
        ks[r], vs[r] = blend(old_rows, fresh[0, r], fresh[1, r], my_rows[r : r + 1, 0:PAD])

    def ctx_to(d, pair):
        to = ring(y, d)
        return remote(
            ctx.at[pair], ctxs.at[y // 2, core, pair], t_send.at[d, pair], t_recv.at[d, core, pair],
            (x * SIDE + to, 2 * z + lax.rem(y, 2)),
        )

    def ctx_from(d, which, pair):
        src = ring(y, SIDE - d)
        place = ctxs.at[src // 2, which, pair]
        return remote(
            place, place, t_send.at[d, pair], t_recv.at[d, which, pair], (x * SIDE + src, 2 * z + which)
        )

    mine = lax.rem(y, 2) == core

    for pair in (0, 1):
        lines = pl.ds(pair * queries.shape[0] // 2, queries.shape[0] // 2)
        attend(queries.at[lines], my_rows, ctx.at[pair], ks, vs, sc, top, low, res, flat)
        for d in (RIGHT, LEFT, OPPOSITE):
            ctx_to(d, pair).start()

        @pl.when(mine)
        def _():
            ctxs[y // 2, core, pair] = ctx[pair]

        @pl.when(jnp.logical_not(mine))
        def _():
            ctx_to(0, pair).start()

    ow_blocks.wait_rest()
    block_from(RIGHT, core).start()
    block_from(LEFT, core).start()

    @pl.loop(1, owners)
    def _(o):
        take(o).wait_recv()

    for s in range(8):
        back[core, s] = f_in[picks[s]]
    swap_back = remote(back.at[core], back.at[core], x_send.at[2], x_recv.at[2], partner)
    swap_back.start()

    def renew(s):
        keys, values = blend(old[s].reshape(new.shape[1], 2 * hd), back[0, s], back[1, s], slot_rows[s : s + 1, 0:PAD])
        new[s, :, 0:hd] = keys
        new[s, :, hd : 2 * hd] = values
        pltpu.make_async_copy(new.at[s], new_hbm.at[s], n_sem.at[s]).start()

    old_in.wait()
    remote(back.at[1 - core], back.at[1 - core], x_send.at[2], x_recv.at[2], partner).wait_recv()
    for s in range(8):
        renew(s)

    @pl.when(mine)
    def _():
        for pair in (0, 1):
            ctx_from(0, 1 - core, pair).wait_recv()
            for which in (0, 1):
                ctx_from(OPPOSITE, which, pair).wait_recv()

    @pl.when(jnp.logical_not(mine))
    def _():
        for d in (RIGHT, LEFT):
            for which in (0, 1):
                for pair in (0, 1):
                    ctx_from(d, which, pair).wait_recv()

    ow_blocks.wait_opposite()
    block_from(OPPOSITE, core).start()
    for d in (0,) + steps:
        block_from(d, 1 - core).wait_recv()

    hrow = rows // 2
    order = (4, 3, -3, 2, -2, 1, -1, 0)

    def compute(n):
        target = lax.rem(z + order[n] + levels, levels)
        column, request = target // 2, lax.rem(target, 2)
        total = None
        for which in (0, 1):
            both = jnp.concatenate([ctxs[request, which, 0], ctxs[request, which, 1]], axis=1)
            term = jnp.dot(both, ow[which, column], preferred_element_type=F32)
            total = term if total is None else total + term
        chunk[n] = total

    def lines_of(half):
        return slice(half * hrow, (half + 1) * hrow)

    def ring_copy(step, half, out, into, send_sem, recv_sem, to):
        return remote(
            out.at[step, pl.ds(half * hrow, hrow)],
            into.at[step, pl.ds(half * hrow, hrow)],
            send_sem.at[step, half],
            recv_sem.at[step, half],
            to,
        )

    def rightward(step, half):
        return ring_copy(step, half, r_out, r_in, r_send, r_recv, right)

    def leftward(step, half):
        return ring_copy(step, half, l_out, l_in, l_send, l_recv, left)

    compute(0)
    r_out[0, lines_of(0), :] = chunk[0, lines_of(0), :].astype(BF16)
    rightward(0, 0).start()
    l_out[0, lines_of(1), :] = chunk[0, lines_of(1), :].astype(BF16)
    leftward(0, 1).start()
    compute(1)
    compute(2)
    for step in (1, 2, 3):
        n_right, n_left = 2 * step - 1, 2 * step
        halves = ((1, 0), (0, 1)) if step == 1 else ((0, 1), (1, 0))
        for right_half, left_half in halves:
            value = chunk[n_right, lines_of(right_half), :]
            if step > 1 or right_half == 0:
                rightward(step - 1, right_half).wait_recv()
                value += r_in[step - 1, lines_of(right_half), :].astype(F32)
            r_out[step, lines_of(right_half), :] = value.astype(BF16)
            rightward(step, right_half).start()
            value = chunk[n_left, lines_of(left_half), :]
            if step > 1 or left_half == 1:
                leftward(step - 1, left_half).wait_recv()
                value += l_in[step - 1, lines_of(left_half), :].astype(F32)
            l_out[step, lines_of(left_half), :] = value.astype(BF16)
            leftward(step, left_half).start()
        if step < 3:
            compute(2 * step + 1)
            compute(2 * step + 2)
        else:
            compute(7)

    def flip(half):
        return remote(
            done.at[pl.ds(half * hrow, hrow)], out_ref.at[pl.ds(half * hrow, hrow)],
            x_send.at[3 + half], x_recv.at[3 + half], mirror,
        )

    for half in (0, 1):
        rightward(3, half).wait_recv()
        leftward(3, half).wait_recv()
        value = chunk[7, lines_of(half), :] + r_in[3, lines_of(half), :].astype(F32)
        value += l_in[3, lines_of(half), :].astype(F32)
        done[lines_of(half), :] = value.astype(BF16)

        @pl.when(turn != y)
        def _():
            flip(half).start()

    @pl.when(turn == y)
    def _():
        out_ref[...] = done[...]

    for i in (0, 1):
        for d in steps:
            rows_to(d, i).wait_send()
            rows_over(d, i, core).wait_send()
    for d in steps:
        sums_to(d).wait_send()
        for pair in (0, 1):
            ctx_to(d, pair).wait_send()
    weights.finish()
    ow_blocks.finish()
    for d in (0,) + steps:
        block_from(d, core).wait_send()

    @pl.when(jnp.logical_not(mine))
    def _():
        for pair in (0, 1):
            ctx_to(0, pair).wait_send()

    @pl.loop(1, owners)
    def _(o):
        hop1(o).wait_send()
        hop2(o).wait_send()
        give(o).wait_send()

    core_swap(core).wait_send()
    swap.wait_send()
    swap_back.wait_send()
    rightward(0, 0).wait_send()
    leftward(0, 1).wait_send()
    for step in (1, 2, 3):
        for half in (0, 1):
            rightward(step, half).wait_send()
            leftward(step, half).wait_send()
    for s in range(8):
        pltpu.make_async_copy(new.at[s], new_hbm.at[s], n_sem.at[s]).wait()

    @pl.when(turn != y)
    def _():
        for half in (0, 1):
            flip(half).wait()


def hand_over(out_ref, store_ref, out_copy, store_copy, out_held, held, sem_in, sem_out):
    count = store_ref.shape[0]
    ins = [pltpu.make_async_copy(store_ref.at[s], held.at[s], sem_in.at[s]) for s in range(count)]
    ins.append(pltpu.make_async_copy(out_ref, out_held, sem_in.at[count]))
    outs = [pltpu.make_async_copy(held.at[s], store_copy.at[s, 0], sem_out.at[s]) for s in range(count)]
    outs.append(pltpu.make_async_copy(out_held, out_copy, sem_out.at[count]))
    for copy in ins:
        copy.start()
    for copy_in, copy_out in zip(ins, outs):
        copy_in.wait()
        copy_out.start()
    for copy in outs:
        copy.wait()


def shards(
    hidden, norm_gain, q_weight, q_bias, kv_weight, kv_bias, out_weight, kv_store, stretch_place, req_stretches, rec_rows
):
    owners = lax.axis_size("cache")
    me = lax.axis_index("cache")
    rows, width = hidden.shape
    stretches, _, length, kv_width = kv_store.shape
    hd = kv_width // 2
    per = rec_rows.shape[2]
    depth, q_cols = q_weight.shape
    levels = lax.axis_size("heads") // 2
    heads = q_cols // hd
    vmem = pl.BlockSpec(memory_space=pltpu.VMEM)
    smem = pl.BlockSpec(memory_space=pltpu.SMEM)
    hbm = pl.BlockSpec(memory_space=pl.ANY)
    dma = pltpu.SemaphoreType.DMA

    store = kv_store.reshape(stretches, owners, 2, length // (2 * owners), kv_width)
    piece = length // (2 * owners)

    attn_out, new_store = pl.pallas_call(
        prefill,
        out_shape=(
            jax.ShapeDtypeStruct((rows, q_cols), BF16),
            jax.ShapeDtypeStruct((stretches, length, kv_width), BF16),
        ),
        in_specs=[smem, smem, hbm, vmem, hbm, hbm, vmem, vmem, hbm, hbm, vmem],
        out_specs=(vmem, hbm),
        scratch_shapes=[
            pltpu.VMEM((rows, width), BF16),
            pltpu.VMEM((SIDE, SIDE, rows, depth), BF16),
            pltpu.VMEM((SIDE, depth, q_cols + hd), BF16),
            pltpu.VMEM((SIDE, rows, q_cols + hd), F32),
            pltpu.VMEM((SIDE, rows, q_cols + hd), BF16),
            pltpu.VMEM((SIDE, rows, q_cols + hd), BF16),
            pltpu.VMEM((owners * stretches, piece, kv_width), BF16),
            pltpu.VMEM((owners, stretches, piece, kv_width), BF16),
            pltpu.VMEM((rows * heads, hd), F32),
            pltpu.VMEM((stretches * PAD, hd), F32),
            pltpu.VMEM((stretches, hd), jnp.int32),
            pltpu.VMEM((stretches, hd), jnp.int32),
            pltpu.VMEM((rows * heads, hd), BF16),
            pltpu.VMEM((stretches, PAD, hd), BF16),
            pltpu.VMEM((2, stretches, PAD, hd), BF16),
            pltpu.VMEM((stretches, owners, 2, piece, kv_width), BF16),
            pltpu.VMEM((stretches, length, hd), BF16),
            pltpu.VMEM((stretches, length, hd), BF16),
            pltpu.VMEM((rows * heads * (stretches + 1) // 4, length), F32),
            pltpu.VMEM((rows * heads // 2, hd), F32),
            pltpu.VMEM((rows * heads // 2, hd), F32),
            pltpu.VMEM((rows * heads // 2, hd), F32),
            pltpu.VMEM((rows, q_cols // 2), F32),
            pltpu.VMEM((2, rows, q_cols // 2), BF16),
            pltpu.VMEM((2, SIDE, depth, q_cols), BF16),
            pltpu.VMEM((2, 2, 2, rows, q_cols // 2), BF16),
            pltpu.VMEM((levels, rows, q_cols), F32),
            pltpu.VMEM((4, rows, q_cols), BF16),
            pltpu.VMEM((4, rows, q_cols), BF16),
            pltpu.VMEM((4, rows, q_cols), BF16),
            pltpu.VMEM((4, rows, q_cols), BF16),
            pltpu.VMEM((rows, q_cols), BF16),
            pltpu.VMEM((2 * owners, PAD, hd), BF16),
            pltpu.VMEM((2 * owners, PAD, hd), BF16),
            pltpu.VMEM((2, stretches, PAD, hd), BF16),
            pltpu.VMEM((stretches, owners, 2, piece, kv_width), BF16),
            pltpu.VMEM((stretches, length, kv_width), BF16),
            dma((7 + SIDE,)),
            dma((SIDE, 2)),
            dma((SIDE, 2)),
            dma((SIDE, 2)),
            dma((SIDE, 2)),
            dma((SIDE, 2)),
            dma((SIDE, 2)),
            dma((SIDE,)),
            dma((SIDE,)),
            dma((owners,)),
            dma((owners,)),
            dma((owners,)),
            dma((owners,)),
            dma((5,)),
            dma((5,)),
            dma((SIDE, 2)),
            dma((SIDE, 2)),
            dma((SIDE,)),
            dma((SIDE,)),
            dma((SIDE, 2)),
            dma((SIDE, 2, 2)),
            dma((4, 2)),
            dma((4, 2)),
            dma((4, 2)),
            dma((4, 2)),
            dma((owners,)),
            dma((owners,)),
            dma((8,)),
        ],
        compiler_params=pltpu.CompilerParams(collective_id=0, has_side_effects=True, vmem_limit_bytes=58 << 20),
        name="prefill",
    )(
        stretch_place, req_stretches.T, hidden, norm_gain, q_weight, kv_weight, q_bias, kv_bias, out_weight, store, rec_rows
    )
    return pl.pallas_call(
        hand_over,
        out_shape=(
            jax.ShapeDtypeStruct((rows, q_cols), BF16),
            jax.ShapeDtypeStruct((stretches, 1, length, kv_width), BF16),
        ),
        in_specs=[hbm, hbm],
        out_specs=(hbm, hbm),
        scratch_shapes=[
            pltpu.VMEM((rows, q_cols), BF16),
            pltpu.VMEM((stretches, length, kv_width), BF16),
            dma((stretches + 1,)),
            dma((stretches + 1,)),
        ],
        name="hand_over",
    )(attn_out, new_store)


def solution(mesh):
    placed = (
        P("cache", None),
        P(),
        P("cache", "heads"),
        P("heads"),
        P("cache", None),
        P(),
        P("heads", "cache"),
        P("cache", "heads", None, None),
        P(),
        P(),
        P(),
    )
    return jax.shard_map(
        shards,
        mesh=mesh,
        in_specs=placed,
        out_specs=(P("cache", "heads"), P("cache", "heads", None, None)),
        check_vma=False,
    )
```
